128 devices in a mesh: dp: 16 (over z, y), tensor: 8 (over x, core).
Axes of the slice: x: 4, y: 4, z: 4, core: 2. Of those that a mesh axis runs over, the one named last changes fastest.
Arguments:
- tile_tokens: bfloat16 [256, 256, 1536], P('dp'), may hold values from -6 to 6
- vit_qkv: bfloat16 [1536, 24, 3, 64], P(None, 'tensor'), as said below
- vit_out: bfloat16 [1536, 1536], P('tensor'), may hold values from -0.15625 to 0.15625
- tile_norm_gain: bfloat16 [1536], replicated, may hold values from 0.099609375 to 1.8984375
- fresh_proj: bfloat16 [1536, 768], replicated, may hold values from -0.15625 to 0.15625
- tile_target: int32 [256], replicated, may hold values from 0 to 16383
- cached_rows: bfloat16 [16384, 768], P(('dp', 'tensor')), may hold values from -6 to 6
- slide_tiles: int32 [4], replicated, may hold values from 1 to 8192, 16384 in all
- head_shift: int32 [16], replicated, may hold values from 0 to 15
- long_gain: bfloat16 [768], replicated, may hold values from 0.099609375 to 1.8984375
- long_qkv: bfloat16 [768, 16, 3, 48], replicated, as said below
- long_out: bfloat16 [768, 768], replicated, may hold values from -0.21875 to 0.21875
Outputs:
- slide_output: bfloat16 [16384, 768], P(('dp', 'tensor'))
The draws below stay inside these ranges and needn't reach their ends.
Inputs may be any that keep to these rules, and one draw needn't show every extreme that they name: `slide_tiles`: the counts sum to 16384; the largest is exactly 8192. `tile_target`: rows may repeat. `vit_qkv`: dense projection entries. `long_qkv`: dense projection entries.
All inputs are finite; a program needn't handle non-finite values.
Results may differ from the reference program's by a relative error of at most 0.006.
Values may be sent and summed in bfloat16 or wider, within the bound.
A program may use at most 192 MiB of HBM per device.

```python
import math
import jax
import jax.numpy as jnp
import numpy as np
from jax import lax

VH = 24
VS = 64
LH = 16
LS = 48
TILE_TOK = 256
SLIDES = 4
D = 1536
LD = 768
TILES = 256
SEQ = 16384
SEG0 = 1024
PAIRS = 5


def projection_base(key, fan_in, heads, head_size):
    gains = jnp.array([1.6, 1.6, 1.0], jnp.float32)[None, None, :, None]
    return jax.random.normal(key, (fan_in, heads, 3, head_size), jnp.float32) * gains / math.sqrt(fan_in)


def draw_vit_qkv(key, part):
    key = jax.random.fold_in(key, 11)
    main_key = jax.random.fold_in(key, 0)
    weights = projection_base(main_key, D, VH, VS)
    return weights.astype(jnp.bfloat16)


def draw_long_qkv(key, part):
    key = jax.random.fold_in(key, 23)
    main_key = jax.random.fold_in(key, 0)
    weights = projection_base(main_key, LD, LH, LS)
    return weights.astype(jnp.bfloat16)


def with_ends(values, key, least, top_value):
    longest = values.shape.index(max(values.shape))
    spots = []
    for shift in (0, 1):
        where = [jax.random.randint(jax.random.fold_in(key, axis), (), 0, length) for axis, length in enumerate(values.shape)]
        where[longest] = (where[longest] + shift) % values.shape[longest]
        spots.append(tuple(where))
    return values.at[spots[0]].set(least).at[spots[1]].set(top_value)


def block_levels(stream_key, dims, cuts, least, high):
    level, own = 1.0, jax.random.fold_in(stream_key, 6)
    for dim, parts in cuts:
        draws = jnp.exp(jax.random.uniform(jax.random.fold_in(own, dim), (parts,), jnp.float32, least / len(cuts), high / len(cuts)))
        level = level * jnp.repeat(draws, dims[dim] // parts).reshape([-1 if axis == dim else 1 for axis in range(len(dims))])
    return level


def split_up(amount, total, reach, skew):
    portions = [(1 << 20) // math.isqrt(standing ** skew) + 1 for standing in range(2, amount + 1)]
    surplus, holding = total - reach - (amount - 1), [1] * (amount - 1)
    while surplus > 0:
        free = [i for i in range(amount - 1) if holding[i] < reach]
        pool, remaining = sum([portions[i] for i in free]), surplus
        for i in free:
            extra = min(reach - holding[i], max(1, remaining * portions[i] // pool), surplus)
            holding[i] = holding[i] + extra
            surplus = surplus - extra
    return np.array([reach] + holding)


def uneven_parts(stream_key, amount, total, limit, skew):
    if amount == 2:
        one = jax.random.randint(stream_key, (), max(1, total - limit), min(limit, total - 1) + 1)
        return jnp.stack([one, total - one])
    lengths = jnp.asarray(split_up(amount, total, limit, skew), jnp.int32)
    twos = (amount - 1) // 2
    source_of, taker = lengths[1:1 + 2 * twos:2], lengths[2:2 + 2 * twos:2]
    margin = jnp.minimum(source_of - 1, limit - taker)
    shifted = jax.random.randint(jax.random.fold_in(stream_key, 1), (twos,), 0, 1 << 20) % (margin + 1)
    lengths = lengths.at[1:1 + 2 * twos:2].set(source_of - shifted).at[2:2 + 2 * twos:2].set(taker + shifted)
    return lengths[jax.random.permutation(jax.random.fold_in(stream_key, 2), amount)]


def normal_values(own_key, dims, deviation, bound, cuts=(), kind=jnp.bfloat16):
    entries = jax.random.normal(own_key, dims, jnp.float32) * deviation
    if len(cuts) > 0:
        entries = block_levels(own_key, dims, cuts, -0.22, 0.18) * entries
    return jnp.clip(entries, min=-bound, max=bound).astype(kind)


def setup_inputs(seed: int = 0) -> dict:
    arg_keys = jax.random.split(jax.random.key(seed), 13)
    tile_tokens = normal_values(arg_keys[0], (TILES, TILE_TOK, D), 1.0, 6.0, ((0, 16),))
    vit_qkv = draw_vit_qkv(jax.random.fold_in(arg_keys[12], 71), 0)
    vit_out = normal_values(arg_keys[2], (D, D), D ** -0.5, 0.15625, ((0, 8),))
    tile_norm_gain = jnp.clip(1.0 + 0.18 * jax.random.normal(arg_keys[3], (D,), jnp.float32), 0.099609375, 1.8984375).astype(jnp.bfloat16)
    fresh_proj = normal_values(arg_keys[4], (D, LD), D ** -0.5, 0.15625)
    tile_target = with_ends(jax.random.randint(arg_keys[5], (TILES,), 0, SEQ), jax.random.fold_in(arg_keys[5], 1), 0, SEQ - 1).astype(jnp.int32)
    cached_rows = normal_values(arg_keys[6], (SEQ, LD), 1.0, 6.0, ((0, 128),))
    slide_tiles = uneven_parts(arg_keys[7], SLIDES, SEQ, SEQ // 2, 2).astype(jnp.int32)
    head_shift = with_ends(jax.random.randint(arg_keys[8], (LH,), 0, SEQ // SEG0), jax.random.fold_in(arg_keys[8], 1), 0, (SEQ // SEG0) - 1).astype(jnp.int32)
    long_gain = jnp.clip(1.0 + 0.18 * jax.random.normal(arg_keys[9], (LD,), jnp.float32), 0.099609375, 1.8984375).astype(jnp.bfloat16)
    long_qkv = draw_long_qkv(jax.random.fold_in(arg_keys[12], 71), 0)
    long_out = normal_values(arg_keys[11], (LD, LD), LD ** -0.5, 0.21875)
    return dict(tile_tokens=tile_tokens, vit_qkv=vit_qkv, vit_out=vit_out, tile_norm_gain=tile_norm_gain, fresh_proj=fresh_proj, tile_target=tile_target, cached_rows=cached_rows, slide_tiles=slide_tiles, head_shift=head_shift, long_gain=long_gain, long_qkv=long_qkv, long_out=long_out)


EPSILON = 1e-06
NEGATIVE = -1e+30
HIGHEST = lax.Precision.HIGHEST

def normalize(values):
    center = values - lax.optimization_barrier(jnp.mean(values, axis=-1, keepdims=True))
    return center * lax.rsqrt(lax.optimization_barrier(jnp.mean(center * center, axis=-1, keepdims=True)) + EPSILON)

def rounded(values):
    return lax.optimization_barrier(values.astype(jnp.bfloat16)).astype(jnp.float32)

def encode_tile(single, vit_qkv):
    normed = normalize(single.astype(jnp.float32)).astype(jnp.bfloat16)
    projected = jnp.dot(normed, vit_qkv.reshape(D, VH * 3 * VS), preferred_element_type=jnp.float32)
    projected = rounded(projected).reshape(TILE_TOK, VH, 3, VS)
    scores = jnp.einsum('qhd,khd->hqk', projected[:, :, 0], projected[:, :, 1], precision=HIGHEST) / math.sqrt(VS)
    highest = lax.optimization_barrier(jnp.max(scores, axis=-1, keepdims=True))
    weights = jnp.exp(scores - highest)
    totals = lax.optimization_barrier(jnp.sum(weights, axis=-1))
    mixture = jnp.einsum('hqk,khd->qhd', rounded(weights), projected[:, :, 2], precision=HIGHEST)
    mixture = mixture / jnp.transpose(totals)[:, :, None]
    attended = rounded(mixture).reshape(TILE_TOK, D)
    return (lax.optimization_barrier(jnp.mean(attended, axis=0)), lax.optimization_barrier(jnp.mean(single.astype(jnp.float32), axis=0)))

def pair_head(packed, shift, slide_ids, stride):
    offset = (shift % stride).astype(jnp.int32)
    picked = lax.dynamic_index_in_dim(packed.reshape(SEQ // stride, stride, 3 * LS), offset, axis=1, keepdims=False)
    picked_ids = lax.dynamic_index_in_dim(slide_ids.reshape(SEQ // stride, stride), offset, axis=1, keepdims=False)
    groups = picked.reshape(-1, SEG0, 3 * LS).astype(jnp.float32)
    group_ids = picked_ids.reshape(-1, SEG0)
    scores = jnp.einsum('sqd,skd->sqk', groups[:, :, :LS], groups[:, :, LS:2 * LS], precision=HIGHEST) / math.sqrt(LS)
    scores = jnp.where(group_ids[:, :, None] == group_ids[:, None, :], scores, NEGATIVE)
    highest = lax.optimization_barrier(jnp.max(scores, axis=-1))
    weights = jnp.exp(scores - highest[:, :, None])
    totals = lax.optimization_barrier(jnp.sum(weights, axis=-1))
    mixture = jnp.einsum('sqk,skd->sqd', rounded(weights), groups[:, :, 2 * LS:], precision=HIGHEST) / totals[:, :, None]
    spread = lax.dynamic_update_index_in_dim(jnp.zeros((SEQ // stride, stride, LS), jnp.float32), mixture.reshape(SEQ // stride, LS), offset, 1)
    level_rows = lax.dynamic_update_index_in_dim(jnp.full((SEQ // stride, stride), NEGATIVE, jnp.float32), (highest + jnp.log(totals)).reshape(SEQ // stride), offset, 1)
    return (spread.reshape(SEQ, LS), level_rows.reshape(SEQ))

def reference(tile_tokens, vit_qkv, vit_out, tile_norm_gain, fresh_proj, tile_target, cached_rows, slide_tiles, head_shift, long_gain, long_qkv, long_out):
    pooled_attention, tile_means = lax.map(lambda single: encode_tile(single, vit_qkv), tile_tokens)
    pooled = tile_means + jnp.dot(pooled_attention, vit_out.astype(jnp.float32), precision=HIGHEST)
    normed = (normalize(pooled) * tile_norm_gain.astype(jnp.float32)).astype(jnp.bfloat16)
    fresh_rows = jnp.dot(normed, fresh_proj, preferred_element_type=jnp.float32).astype(jnp.bfloat16)
    seq_rows = cached_rows.astype(jnp.float32).at[tile_target].add(fresh_rows.astype(jnp.float32))
    hidden = (normalize(seq_rows) * long_gain.astype(jnp.float32)).astype(jnp.bfloat16)
    packed = jnp.dot(hidden, long_qkv.reshape(LD, LH * 3 * LS), preferred_element_type=jnp.float32).astype(jnp.bfloat16)
    packed = jnp.transpose(packed.reshape(SEQ, LH, 3 * LS), (1, 0, 2))
    slide_ends = jnp.cumsum(slide_tiles).astype(jnp.int32)
    positions = jnp.arange(SEQ, dtype=jnp.int32)
    slide_ids = lax.optimization_barrier(jnp.sum((slide_ends[None, :] <= positions[:, None]).astype(jnp.int32), axis=1))
    outputs = []
    levels = []
    for pair_index in range(PAIRS):
        stride = 2 ** pair_index
        spread, level_rows = lax.map(lambda head_item: pair_head(head_item[0], head_item[1], slide_ids, stride), (packed, head_shift))
        outputs.append(spread)
        levels.append(level_rows)
    stacked_level = jnp.stack(levels)
    largest = lax.optimization_barrier(jnp.max(stacked_level, axis=0))
    shares = jnp.exp(stacked_level - largest)
    combined = lax.optimization_barrier(jnp.sum(shares[..., None] * jnp.stack(outputs), axis=0)) / lax.optimization_barrier(jnp.sum(shares, axis=0))[..., None]
    mixture = jnp.transpose(combined, (1, 0, 2)).reshape(SEQ, LD).astype(jnp.bfloat16)
    return (seq_rows + jnp.dot(mixture, long_out, preferred_element_type=jnp.float32)).astype(jnp.bfloat16)
```

```python
import functools
import math

import jax
import jax.numpy as jnp
from jax import lax
from jax.experimental import pallas as pl
from jax.experimental.pallas import tpu as pltpu
from jax.sharding import PartitionSpec as P

MESH = pl.DeviceIdType.MESH
EPSILON = 1e-06
OUTSIDE = -1e30
LOG2E = 1.4426950408889634
NN = (((1,), (0,)), ((), ()))
NT = (((1,), (1,)), ((), ()))
TN = (((0,), (0,)), ((), ()))
F32 = jnp.float32
BF16 = jnp.bfloat16

TILES_HERE = 16
TOK = 256
D = 1536
VH_HERE = 3
VS = 64
VW = VH_HERE * 3 * VS
LD = 768
LH = 16
LS = 48
LW = 3 * LS
ROWS = 128
SEG = 1024
CHUNK = 2048
KX = 64
VIT_SCALE = LOG2E / math.sqrt(VS)
LONG_SCALE = LOG2E / math.sqrt(LS)


def dot(a, b, dims=NN):
    return lax.dot_general(a, b, dims, preferred_element_type=F32)


def iota(shape, dim):
    return lax.broadcasted_iota(jnp.int32, shape, dim)


def split3(value):
    high = value.astype(BF16)
    rest = value - high.astype(F32)
    middle = rest.astype(BF16)
    low = (rest - middle.astype(F32)).astype(BF16)
    return high, middle, low


def tile_kernel(x_ref, w_ref, pooled_ref, mean_ref, wext, csum):
    step = pl.program_id(0)
    tensor = lax.axis_index("tensor")

    @pl.when(step == 0)
    def _():
        wext[0:VW, :] = w_ref[...]
        row = iota((16, D), 0)
        col = iota((16, D), 1)
        extra = jnp.where(row == 0, 1.0, jnp.where((row == 1) & (col == 0), 1.0, 0.0))
        wext[VW : VW + 16, :] = extra.astype(BF16)
        csum[...] = dot(w_ref[...], jnp.ones((D, TOK), BF16))

    x = x_ref[0]
    raw = dot(wext[...], x, NT)
    mean = raw[VW : VW + 1] * (1.0 / D)
    first_row = raw[VW + 1 : VW + 2]
    first = x[:, 0:1].astype(F32)
    squares = jnp.zeros((TOK, 128), F32)
    for k in range(D // 128):
        delta = x[:, 128 * k : 128 * (k + 1)].astype(F32) - first
        squares = squares + delta * delta
    high, middle, low = split3(squares)
    ones = jnp.ones((16, 128), BF16)
    total = dot(ones, high, NT) + dot(ones, middle, NT) + dot(ones, low, NT)
    shift = mean - first_row
    variance = jnp.maximum(total[0:1] * (1.0 / D) - shift * shift, 0.0)
    scale = lax.rsqrt(variance + EPSILON)
    projected = ((raw[0:VW] - csum[...] * mean) * scale).astype(BF16)
    attended = []
    for head in range(VH_HERE):
        base = head * 3 * VS
        query = projected[base : base + VS]
        key = projected[base + VS : base + 2 * VS]
        value = projected[base + 2 * VS : base + 3 * VS]
        scores = dot(key, query, TN)
        highest = jnp.max(scores, axis=0, keepdims=True)
        weights = jnp.exp2((scores - highest) * VIT_SCALE)
        sums = jnp.sum(weights, axis=0, keepdims=True)
        mixture = dot(value, weights.astype(BF16))
        attended.append((mixture / sums).astype(BF16))
    attended = jnp.concatenate(attended, axis=0)
    pooled = dot(jnp.ones((16, TOK), BF16), attended, NT) * (1.0 / TOK)
    pooled_ref[pl.ds(step, 1), :] = pooled[0:1]

    @pl.when(step // 2 == tensor)
    def _():
        sums = dot(jnp.ones((16, TOK), BF16), x) * (1.0 / TOK)
        mean_ref[pl.ds(step % 2, 1), :] = sums[0:1]


def encode_tiles(tokens, weights):
    return pl.pallas_call(
        tile_kernel,
        grid=(TILES_HERE,),
        in_specs=[
            pl.BlockSpec((1, TOK, D), lambda i: (i, 0, 0)),
            pl.BlockSpec((VW, D), lambda i: (0, 0)),
        ],
        out_specs=[
            pl.BlockSpec((TILES_HERE, VH_HERE * VS), lambda i: (0, 0)),
            pl.BlockSpec((8, D), lambda i: (0, 0)),
        ],
        out_shape=[
            jax.ShapeDtypeStruct((TILES_HERE, VH_HERE * VS), F32),
            jax.ShapeDtypeStruct((8, D), F32),
        ],
        scratch_shapes=[pltpu.VMEM((VW + 16, D), BF16), pltpu.VMEM((VW, TOK), F32)],
        compiler_params=pltpu.CompilerParams(vmem_limit_bytes=32 * 1024 * 1024),
    )(tokens, weights)


def normalize_rows(values):
    center = values - jnp.mean(values, axis=-1, keepdims=True)
    return center * lax.rsqrt(jnp.mean(center * center, axis=-1, keepdims=True) + EPSILON)


def bit_reversed(rank):
    return (rank % 2) * 8 + (rank // 2 % 2) * 4 + (rank // 4 % 2) * 2 + rank // 8


def slide_kernel(
    pooled_ref,
    tile_mean_ref,
    vit_out_hbm,
    tile_gain_ref,
    fresh_proj_hbm,
    target_ref,
    cached_hbm,
    slide_tiles_ref,
    head_shift_ref,
    long_gain_ref,
    long_qkv_hbm,
    long_out_hbm,
    out_ref,
    vit_out,
    fresh_proj,
    cached,
    long_qkv,
    long_out,
    part,
    part_in,
    fresh_in,
    fresh_all,
    seq,
    hidden,
    packed,
    qkv,
    perm,
    qx,
    kx,
    vx,
    send2,
    send3,
    send4,
    got2,
    got3,
    got4,
    num,
    top,
    mix_out,
    mix_in,
    load_sem,
    sems,
):
    d = lax.axis_index("dp")
    t = lax.axis_index("tensor")
    chunk = d // 2
    half = d % 2
    mine = half * 8 + t

    used = [0]

    def remote(src, dst, device):
        i = used[0]
        used[0] += 1
        return pltpu.make_async_remote_copy(
            src_ref=src,
            dst_ref=dst,
            send_sem=sems.at[0, i],
            recv_sem=sems.at[1, i],
            device_id=device,
            device_id_type=MESH,
        )

    barrier = pltpu.get_barrier_semaphore()
    for k in range(1, 8):
        pl.semaphore_signal(barrier, 1, device_id=(d, (t + k) % 8), device_id_type=MESH)
        pl.semaphore_signal(
            barrier, 1, device_id=(2 * chunk + 1 - half, (t + k) % 8), device_id_type=MESH
        )
    for k in range(1, 16):
        pl.semaphore_signal(barrier, 1, device_id=((d + k) % 16, t), device_id_type=MESH)

    loads = [
        pltpu.make_async_copy(src, dst, load_sem.at[i])
        for i, (src, dst) in enumerate(
            [
                (vit_out_hbm, vit_out),
                (fresh_proj_hbm, fresh_proj),
                (cached_hbm, cached),
                (long_qkv_hbm, long_qkv),
                (long_out_hbm, long_out),
            ]
        )
    ]
    for load in loads:
        load.start()

    loads[0].wait()
    high, middle, low = split3(pooled_ref[...])
    weight = vit_out[...]
    partial = dot(high, weight) + dot(middle, weight) + dot(low, weight)
    for k in range(8):
        part[k] = partial[2 * k : 2 * k + 2]
    pl.semaphore_wait(barrier, 29)
    reduce_copies = []
    for k in range(1, 8):
        peer = (t + k) % 8
        copy = remote(part.at[peer], part_in.at[t], (d, peer))
        copy.start()
        reduce_copies.append(copy)
    part_in[pl.ds(t, 1)] = part[pl.ds(t, 1)]

    shift = head_shift_ref[mine] % 16
    place = iota((SEG, 1), 0)
    goal = bit_reversed((place + 16 - shift) % 16) * 64 + place // 16
    perm[...] = jnp.where(goal == iota((SEG, SEG), 1), 1.0, 0.0).astype(BF16)
    end0 = slide_tiles_ref[0]
    end1 = end0 + slide_tiles_ref[1]
    end2 = end1 + slide_tiles_ref[2]

    def slides(count, width, which):
        lane = iota((16, count), 1)
        spot = lane % width
        row = (
            SEG * (2 * which + lane // width)
            + 16 * (spot % 64)
            + (bit_reversed(spot // 64) + shift) % 16
        )
        return (
            (row >= end0).astype(jnp.int32)
            + (row >= end1).astype(jnp.int32)
            + (row >= end2).astype(jnp.int32)
        )

    def query_marks(count, width, which):
        ids = slides(count, width, which)
        return jnp.where(ids == iota(ids.shape, 0), 1.0, 0.0).astype(BF16)

    def key_marks(count, width, which):
        ids = slides(count, width, which)
        feature = iota(ids.shape, 0)
        return jnp.where((feature < 4) & (ids != feature), OUTSIDE, 0.0).astype(BF16)

    def value_marks(count):
        return jnp.where(iota((16, count), 0) == 0, 1.0, 0.0).astype(BF16)

    for copy in reduce_copies:
        copy.wait_recv()
    pooled = tile_mean_ref[0:2, :]
    for k in range(8):
        pooled = pooled + part_in[k]
    normed = (normalize_rows(pooled) * tile_gain_ref[...].astype(F32)).astype(BF16)
    loads[1].wait()
    fresh = dot(normed, fresh_proj[...])
    fresh_in[pl.ds(t, 1)] = fresh[None]
    gather_copies = []
    for k in range(1, 8):
        copy = remote(fresh_in.at[t], fresh_in.at[t], (d, (t + k) % 8))
        copy.start()
        gather_copies.append(copy)
    for copy in gather_copies:
        copy.wait_recv()
    group = jnp.concatenate([fresh_in[k] for k in range(8)], axis=0).astype(BF16)
    here = pl.ds(pl.multiple_of(d * 16, 16), 16)
    fresh_all[here, :] = group
    spread_copies = []
    for k in range(1, 16):
        copy = remote(fresh_all.at[here], fresh_all.at[here], ((d + k) % 16, t))
        copy.start()
        spread_copies.append(copy)
    first_row = (d * 8 + t) * ROWS
    match = (target_ref[...] - first_row == iota((ROWS, 256), 0))
    match = jnp.where(match, 1.0, 0.0).astype(BF16)
    loads[2].wait()
    for copy in spread_copies:
        copy.wait_recv()
    rows = cached[...].astype(F32) + dot(match, fresh_all[...])
    seq[...] = rows
    hidden[...] = (normalize_rows(rows) * long_gain_ref[...].astype(F32)).astype(BF16)

    loads[3].wait()
    head_copies = []
    for k in range(1, 17):
        head = (mine + k) % 16
        weight = long_qkv[pl.ds(pl.multiple_of(head * LW, LW), LW), :]
        block = dot(weight, hidden[...], NT).astype(BF16)
        lanes = pl.ds(pl.multiple_of(mine * ROWS, ROWS), ROWS)
        if k == 16:
            qkv[:, lanes] = block
        else:
            packed[k - 1] = block
            copy = remote(
                packed.at[k - 1], qkv.at[:, lanes], (2 * chunk + head // 8, head % 8)
            )
            copy.start()
            head_copies.append(copy)
    for copy in head_copies:
        copy.wait_recv()

    low_half = iota((LW, 128), 1) < 64
    sides = []
    for side in range(2):
        lanes = slice(side * SEG, (side + 1) * SEG)
        ordered = dot(qkv[:, lanes], perm[...])
        sides.append(ordered[:, 0:128])
        ordered = ordered.astype(BF16)
        qx[0:LS, lanes] = ordered[0:LS]
        kx[0:LS, lanes] = ordered[LS : 2 * LS]
        vx[0:LS, lanes] = ordered[2 * LS : LW]
        send2[:, side * 256 : (side + 1) * 256] = ordered[LS:LW, 0:256]
        send3[:, side * 128 : (side + 1) * 128] = ordered[LS:LW, 0:128]
    both = jnp.where(low_half, sides[0], pltpu.roll(sides[1], 64, 1)).astype(BF16)
    send4[...] = both[LS:LW]
    quad = chunk // 4
    inner = chunk % 4
    far_copies = [
        remote(send2, got2, (2 * (chunk + 1 - 2 * (chunk % 2)) + half, t))
    ]
    for k in range(2):
        other = quad * 4 + (1 - inner // 2) * 2 + (inner % 2 + k) % 2
        far_copies.append(remote(send3, got3.at[k], (2 * other + half, t)))
    for k in range(4):
        other = (1 - quad) * 4 + (inner + k) % 4
        far_copies.append(remote(send4, got4.at[k], (2 * other + half, t)))
    for copy in far_copies:
        copy.start()

    qx[LS:KX, :] = query_marks(CHUNK, SEG, chunk)
    kx[LS:KX, :] = key_marks(CHUNK, SEG, chunk)
    vx[LS:KX, :] = value_marks(CHUNK)

    def attend(keys, values, queries):
        scores = dot(keys, queries, TN)
        highest = jnp.max(scores, axis=0, keepdims=True)
        weights = jnp.exp2((scores - highest) * LONG_SCALE).astype(BF16)
        return dot(values, weights), highest

    def merge(lanes, other_num, other_top):
        old_top = top[0:1, lanes]
        new_top = jnp.maximum(old_top, other_top)
        num[:, lanes] = num[:, lanes] * jnp.exp2(
            (old_top - new_top) * LONG_SCALE
        ) + other_num * jnp.exp2((other_top - new_top) * LONG_SCALE)
        top[0:1, lanes] = new_top

    def first_pair(i, carry):
        for side in range(2):
            lanes = slice(side * SEG, (side + 1) * SEG)
            spot = pl.ds(pl.multiple_of(side * SEG + i * 256, 256), 256)
            result, highest = attend(kx[:, lanes], vx[:, lanes], qx[:, spot])
            num[:, spot] = result
            top[0:1, spot] = highest
        return carry

    lax.fori_loop(0, 4, first_pair, 0)

    def joined(ref, width):
        return jnp.concatenate([ref[:, 0:width], ref[:, SEG : SEG + width]], axis=1)

    keys = joined(kx, 512)
    values = joined(vx, 512)
    for side in range(2):
        for i in range(2):
            lanes = slice(side * SEG + i * 256, side * SEG + (i + 1) * 256)
            merge(lanes, *attend(keys, values, qx[:, lanes]))

    def arrived(block, count, width, which):
        key = jnp.concatenate([block[0:LS], key_marks(count, width, which)], axis=0)
        value = jnp.concatenate([block[LS : 2 * LS], value_marks(count)], axis=0)
        return key, value

    for copy in far_copies:
        copy.wait_recv()
    beside = chunk + 1 - 2 * (chunk % 2)
    key2, value2 = arrived(got2[...], 512, 256, beside)
    keys = jnp.concatenate([joined(kx, 256), key2], axis=1)
    values = jnp.concatenate([joined(vx, 256), value2], axis=1)
    for side in range(2):
        lanes = slice(side * SEG, side * SEG + 256)
        merge(lanes, *attend(keys, values, qx[:, lanes]))

    keys3 = [joined(kx, 128), key2[:, 0:128], key2[:, 256:384]]
    values3 = [joined(vx, 128), value2[:, 0:128], value2[:, 256:384]]
    for k in range(2):
        other = quad * 4 + (1 - inner // 2) * 2 + (inner % 2 + k) % 2
        key, value = arrived(got3[k], 256, 128, other)
        keys3.append(key)
        values3.append(value)
    keys = jnp.concatenate(keys3, axis=1)
    values = jnp.concatenate(values3, axis=1)
    result, highest = attend(keys, values, joined(qx, 128))
    merge(slice(0, 128), result[:, 0:128], highest[:, 0:128])
    merge(slice(SEG, SEG + 128), result[:, 128:256], highest[:, 128:256])

    lower = iota((KX, 128), 1) < 64

    def packed_pair(a, b):
        moved = pltpu.roll(b.astype(F32), 64, 1)
        return jnp.where(lower, a.astype(F32), moved).astype(BF16)

    keys4 = []
    values4 = []
    for blocks, gather in ((keys3, keys4), (values3, values4)):
        own = blocks[0]
        gather.append(packed_pair(own[:, 0:128], own[:, 128:256]))
        gather.append(packed_pair(blocks[1], blocks[2]))
        for k in range(2):
            far = blocks[3 + k]
            gather.append(packed_pair(far[:, 0:128], far[:, 128:256]))
    for k in range(4):
        other = (1 - quad) * 4 + (inner + 4 - k) % 4
        key, value = arrived(got4[k], 128, 64, other)
        keys4.append(key)
        values4.append(value)
    keys = jnp.concatenate(keys4, axis=1)
    values = jnp.concatenate(values4, axis=1)
    query = packed_pair(qx[:, 0:128], qx[:, SEG : SEG + 128])
    result, highest = attend(keys, values, query)
    highest = jnp.broadcast_to(highest, (8, 128))
    for side in range(2):
        if side == 1:
            result = pltpu.roll(result, 64, 1)
            highest = pltpu.roll(highest, 64, 1)
        lanes = slice(side * SEG, side * SEG + 128)
        merge(
            lanes,
            jnp.where(lower, result, 0.0),
            jnp.where(lower[0:1], highest[0:1], OUTSIDE),
        )

    mix_copies = []
    for side in range(2):
        lanes = slice(side * SEG, (side + 1) * SEG)
        blended = (num[0:LS, lanes] / num[LS : LS + 1, lanes]).astype(BF16)
        natural = dot(blended, perm[...], NT).astype(BF16)
        for i in range(8):
            mix_out[side * 8 + i] = natural[:, i * ROWS : (i + 1) * ROWS]
    for k in range(1, 16):
        device = (mine + k) % 16
        copy = remote(
            mix_out.at[device],
            mix_in.at[mine],
            (2 * chunk + device // 8, device % 8),
        )
        copy.start()
        mix_copies.append(copy)
    mix_in[pl.ds(mine, 1)] = mix_out[pl.ds(mine, 1)]
    loads[4].wait()
    for copy in mix_copies:
        copy.wait_recv()
    mixture = mix_in[...].reshape(LD, ROWS)
    out_ref[...] = (seq[...] + dot(mixture, long_out[...], TN)).astype(BF16)

    for copies in (
        reduce_copies, gather_copies, spread_copies, head_copies, far_copies, mix_copies
    ):
        for copy in copies:
            copy.wait_send()


def slide_layer(*arguments):
    vmem = pl.BlockSpec(memory_space=pltpu.VMEM)
    smem = pl.BlockSpec(memory_space=pltpu.SMEM)
    hbm = pl.BlockSpec(memory_space=pl.ANY)
    return pl.pallas_call(
        slide_kernel,
        out_shape=jax.ShapeDtypeStruct((ROWS, LD), BF16),
        in_specs=[vmem, vmem, hbm, vmem, hbm, vmem, hbm, smem, smem, vmem, hbm, hbm],
        out_specs=vmem,
        scratch_shapes=[
            pltpu.VMEM((VH_HERE * VS, D), BF16),
            pltpu.VMEM((D, LD), BF16),
            pltpu.VMEM((ROWS, LD), BF16),
            pltpu.VMEM((LH * LW, LD), BF16),
            pltpu.VMEM((LD, LD), BF16),
            pltpu.VMEM((8, 2, D), F32),
            pltpu.VMEM((8, 2, D), F32),
            pltpu.VMEM((8, 2, LD), F32),
            pltpu.VMEM((256, LD), BF16),
            pltpu.VMEM((ROWS, LD), F32),
            pltpu.VMEM((ROWS, LD), BF16),
            pltpu.VMEM((15, LW, ROWS), BF16),
            pltpu.VMEM((LW, CHUNK), BF16),
            pltpu.VMEM((SEG, SEG), BF16),
            pltpu.VMEM((KX, CHUNK), BF16),
            pltpu.VMEM((KX, CHUNK), BF16),
            pltpu.VMEM((KX, CHUNK), BF16),
            pltpu.VMEM((2 * LS, 512), BF16),
            pltpu.VMEM((2 * LS, 256), BF16),
            pltpu.VMEM((2 * LS, 128), BF16),
            pltpu.VMEM((2 * LS, 512), BF16),
            pltpu.VMEM((2, 2 * LS, 256), BF16),
            pltpu.VMEM((4, 2 * LS, 128), BF16),
            pltpu.VMEM((KX, CHUNK), F32),
            pltpu.VMEM((8, CHUNK), F32),
            pltpu.VMEM((16, LS, ROWS), BF16),
            pltpu.VMEM((16, LS, ROWS), BF16),
            pltpu.SemaphoreType.DMA((5,)),
            pltpu.SemaphoreType.DMA((2, 66)),
        ],
        compiler_params=pltpu.CompilerParams(
            collective_id=0,
            has_side_effects=True,
            vmem_limit_bytes=48 * 1024 * 1024,
        ),
    )(*arguments)


def body(
    tile_tokens,
    vit_qkv,
    vit_out,
    tile_norm_gain,
    fresh_proj,
    tile_target,
    cached_rows,
    slide_tiles,
    head_shift,
    long_gain,
    long_qkv,
    long_out,
):
    vit_rows = jnp.transpose(vit_qkv, (1, 2, 3, 0)).reshape(VW, D)
    long_rows = jnp.transpose(long_qkv, (1, 2, 3, 0)).reshape(LH * LW, LD)
    pooled, tile_means = encode_tiles(tile_tokens, vit_rows)
    return slide_layer(
        pooled,
        tile_means,
        vit_out,
        tile_norm_gain.reshape(1, D),
        fresh_proj,
        tile_target.reshape(1, 256),
        cached_rows,
        slide_tiles,
        head_shift,
        long_gain.reshape(1, LD),
        long_rows,
        long_out,
    )


def solution(mesh):
    placed = (
        P("dp", None, None),
        P(None, "tensor", None, None),
        P("tensor", None),
        P(),
        P(),
        P(),
        P(("dp", "tensor"), None),
        P(),
        P(),
        P(),
        P(),
        P(),
    )
    return jax.shard_map(
        body, mesh=mesh, in_specs=placed, out_specs=P(("dp", "tensor"), None), check_vma=False
    )
```

```python
import functools
import math

import jax
import jax.numpy as jnp
from jax import lax
from jax.experimental import pallas as pl
from jax.experimental.pallas import tpu as pltpu
from jax.sharding import PartitionSpec as P

MESH = pl.DeviceIdType.MESH
EPSILON = 1e-06
OUTSIDE = -1e30
LOG2E = 1.4426950408889634
NN = (((1,), (0,)), ((), ()))
NT = (((1,), (1,)), ((), ()))
TN = (((0,), (0,)), ((), ()))
F32 = jnp.float32
BF16 = jnp.bfloat16

TILES_HERE = 16
TOK = 256
D = 1536
VH_HERE = 3
VS = 64
VW = VH_HERE * 3 * VS
LD = 768
LH = 16
LS = 48
LW = 3 * LS
ROWS = 128
SEG = 1024
CHUNK = 2048
KX = 64
GROUP = 2
WIDE = GROUP * TOK
AHEAD = 4
VIT_SCALE = LOG2E / math.sqrt(VS)
LONG_SCALE = LOG2E / math.sqrt(LS)


def dot(a, b, dims=NN):
    return lax.dot_general(a, b, dims, preferred_element_type=F32)


def iota(shape, dim):
    return lax.broadcasted_iota(jnp.int32, shape, dim)


def split3(value):
    high = value.astype(BF16)
    rest = value - high.astype(F32)
    middle = rest.astype(BF16)
    low = (rest - middle.astype(F32)).astype(BF16)
    return high, middle, low


def normalize_rows(values):
    center = values - jnp.mean(values, axis=-1, keepdims=True)
    return center * lax.rsqrt(jnp.mean(center * center, axis=-1, keepdims=True) + EPSILON)


def whole_row(ref):
    rows = ref[...].astype(F32)
    return jnp.concatenate([rows[k : k + 1] for k in range(rows.shape[0])], axis=1)


def bit_reversed(rank):
    return (rank % 2) * 8 + (rank // 2 % 2) * 4 + (rank // 4 % 2) * 2 + rank // 8


def whole_kernel(
    tokens_hbm,
    vit_qkv_hbm,
    vit_out_hbm,
    tile_gain_ref,
    fresh_proj_hbm,
    target_ref,
    cached_hbm,
    slide_tiles_ref,
    head_shift_ref,
    long_gain_ref,
    long_qkv_hbm,
    long_out_hbm,
    out_ref,
    tokens,
    vit_qkv,
    csum,
    projected,
    attended,
    token_mean,
    vit_out,
    fresh_proj,
    cached,
    long_qkv,
    long_out,
    part,
    part_in,
    fresh_in,
    fresh_all,
    seq,
    hidden,
    packed,
    qkv,
    perm,
    qx,
    kx,
    vx,
    send2,
    send3,
    send4,
    got2,
    got3,
    got4,
    num,
    top,
    mix_out,
    mix_in,
    token_sem,
    load_sem,
    sems,
):
    d = lax.axis_index("dp")
    t = lax.axis_index("tensor")
    chunk = d // 2
    half = d % 2
    mine = half * 8 + t

    used = [0]

    def remote(src, dst, device):
        i = used[0]
        used[0] += 1
        return pltpu.make_async_remote_copy(
            src_ref=src,
            dst_ref=dst,
            send_sem=sems.at[0, i],
            recv_sem=sems.at[1, i],
            device_id=device,
            device_id_type=MESH,
        )

    barrier = pltpu.get_barrier_semaphore()
    for k in range(1, 8):
        pl.semaphore_signal(barrier, 1, device_id=(d, (t + k) % 8), device_id_type=MESH)
        pl.semaphore_signal(
            barrier, 1, device_id=(2 * chunk + 1 - half, (t + k) % 8), device_id_type=MESH
        )
    for k in range(1, 16):
        pl.semaphore_signal(barrier, 1, device_id=((d + k) % 16, t), device_id_type=MESH)

    vit_load = pltpu.make_async_copy(vit_qkv_hbm, vit_qkv.at[0:VW], load_sem.at[5])
    vit_load.start()
    token_loads = [
        pltpu.make_async_copy(tokens_hbm.at[i], tokens.at[i], token_sem.at[i])
        for i in range(TILES_HERE)
    ]
    for load in token_loads[:AHEAD]:
        load.start()
    loads = [
        pltpu.make_async_copy(src, dst, load_sem.at[i])
        for i, (src, dst) in enumerate(
            [
                (vit_out_hbm, vit_out),
                (fresh_proj_hbm, fresh_proj),
                (cached_hbm, cached),
                (long_qkv_hbm, long_qkv),
                (long_out_hbm, long_out),
            ]
        )
    ]

    row = iota((16, D), 0)
    col = iota((16, D), 1)
    extra = jnp.where(row == 0, 1.0, jnp.where((row == 1) & (col == 0), 1.0, 0.0))
    vit_qkv[VW : VW + 16, :] = extra.astype(BF16)
    shift = head_shift_ref[mine] % 16
    place = iota((SEG, 1), 0)
    goal = bit_reversed((place + 16 - shift) % 16) * 64 + place // 16
    perm[...] = jnp.where(goal == iota((SEG, SEG), 1), 1.0, 0.0).astype(BF16)
    end0 = slide_tiles_ref[0]
    end1 = end0 + slide_tiles_ref[1]
    end2 = end1 + slide_tiles_ref[2]

    def slides(count, width, which):
        lane = iota((16, count), 1)
        spot = lane % width
        row = (
            SEG * (2 * which + lane // width)
            + 16 * (spot % 64)
            + (bit_reversed(spot // 64) + shift) % 16
        )
        return (
            (row >= end0).astype(jnp.int32)
            + (row >= end1).astype(jnp.int32)
            + (row >= end2).astype(jnp.int32)
        )

    def query_marks(count, width, which):
        ids = slides(count, width, which)
        return jnp.where(ids == iota(ids.shape, 0), 1.0, 0.0).astype(BF16)

    def key_marks(count, width, which):
        ids = slides(count, width, which)
        feature = iota(ids.shape, 0)
        return jnp.where((feature < 4) & (ids != feature), OUTSIDE, 0.0).astype(BF16)

    def value_marks(count):
        return jnp.where(iota((16, count), 0) == 0, 1.0, 0.0).astype(BF16)

    qx[LS:KX, :] = query_marks(CHUNK, SEG, chunk)
    kx[LS:KX, :] = key_marks(CHUNK, SEG, chunk)
    vx[LS:KX, :] = value_marks(CHUNK)


    vit_load.wait()
    csum[...] = dot(vit_qkv[0:VW], jnp.ones((D, 128), BF16))

    def project(group):
        for i in range(GROUP):
            token_loads[group * GROUP + i].wait()
        for i in range(GROUP):
            after = group * GROUP + i + AHEAD
            if after < TILES_HERE:
                token_loads[after].start()
        x = tokens[group * GROUP : (group + 1) * GROUP].reshape(WIDE, D)
        raw = dot(vit_qkv[...], x, NT)
        mean = raw[VW : VW + 1] * (1.0 / D)
        shift_row = mean - raw[VW + 1 : VW + 2]
        first = x[:, 0:1].astype(F32)
        squares = jnp.zeros((WIDE, 128), F32)
        for k in range(D // 128):
            delta = x[:, 128 * k : 128 * (k + 1)].astype(F32) - first
            squares = squares + delta * delta
        ones = jnp.ones((16, 128), BF16)
        total = sum(dot(ones, piece, NT) for piece in split3(squares))
        variance = jnp.maximum(total[0:1] * (1.0 / D) - shift_row * shift_row, 0.0)
        scale = lax.rsqrt(variance + EPSILON)
        spread = jnp.concatenate([csum[...]] * (WIDE // 128), axis=1)
        projected[group % 2] = ((raw[0:VW] - spread * mean) * scale).astype(BF16)

    def attention(group):
        for i in range(GROUP):
            lanes = slice(i * TOK, (i + 1) * TOK)

            def piece(head, which):
                first = (head * 3 + which) * VS
                return projected[group % 2, first : first + VS, lanes]

            heads = range(VH_HERE)
            scores = [dot(piece(head, 1), piece(head, 0), TN) for head in heads]
            highest = [jnp.max(score, axis=0, keepdims=True) for score in scores]
            weights = [
                jnp.exp2((score - high) * VIT_SCALE) for score, high in zip(scores, highest)
            ]
            sums = [jnp.sum(weight, axis=0, keepdims=True) for weight in weights]
            mixed = [
                dot(piece(head, 2), weights[head].astype(BF16)) for head in heads
            ]
            place = (group * GROUP + i) * TOK
            for head in heads:
                attended[head * VS : (head + 1) * VS, place : place + TOK] = (
                    mixed[head] / sums[head]
                ).astype(BF16)

    groups = TILES_HERE // GROUP
    project(0)
    for group in range(groups):
        if group + 1 < groups:
            project(group + 1)
        else:
            for load in loads:
                load.start()
        attention(group)
    for i in range(2):
        sums = dot(jnp.ones((16, TOK), BF16), tokens[2 * t + i])
        token_mean[i : i + 1, :] = sums[0:1] * (1.0 / TOK)
    tile_of = iota((TILES_HERE, TILES_HERE * TOK), 1) // TOK
    picks = jnp.where(iota(tile_of.shape, 0) == tile_of, 1.0 / TOK, 0.0).astype(BF16)
    pooled_term = dot(picks, attended[...], NT)

    loads[0].wait()
    high, middle, low = split3(pooled_term)
    weight = vit_out[...]
    partial = dot(high, weight) + dot(middle, weight) + dot(low, weight)
    for k in range(8):
        part[k] = partial[2 * k : 2 * k + 2]
    pl.semaphore_wait(barrier, 29)
    reduce_copies = []
    for k in range(1, 8):
        peer = (t + k) % 8
        copy = remote(part.at[peer], part_in.at[t], (d, peer))
        copy.start()
        reduce_copies.append(copy)
    part_in[pl.ds(t, 1)] = part[pl.ds(t, 1)]

    for copy in reduce_copies:
        copy.wait_recv()
    pooled = token_mean[0:2, :]
    for k in range(8):
        pooled = pooled + part_in[k]
    normed = (normalize_rows(pooled) * whole_row(tile_gain_ref)).astype(BF16)
    loads[1].wait()
    fresh = dot(normed, fresh_proj[...])
    fresh_in[pl.ds(t, 1)] = fresh[None]
    gather_copies = []
    for k in range(1, 8):
        copy = remote(fresh_in.at[t], fresh_in.at[t], (d, (t + k) % 8))
        copy.start()
        gather_copies.append(copy)
    for copy in gather_copies:
        copy.wait_recv()
    group = jnp.concatenate([fresh_in[k] for k in range(8)], axis=0).astype(BF16)
    here = pl.ds(pl.multiple_of(d * 16, 16), 16)
    fresh_all[here, :] = group
    spread_copies = []
    for k in range(1, 16):
        copy = remote(fresh_all.at[here], fresh_all.at[here], ((d + k) % 16, t))
        copy.start()
        spread_copies.append(copy)
    first_row = (d * 8 + t) * ROWS
    match = (target_ref[...] - first_row == iota((ROWS, 256), 0))
    match = jnp.where(match, 1.0, 0.0).astype(BF16)
    loads[2].wait()
    for copy in spread_copies:
        copy.wait_recv()
    rows = cached[...].astype(F32) + dot(match, fresh_all[...])
    seq[...] = rows
    hidden[...] = (normalize_rows(rows) * whole_row(long_gain_ref)).astype(BF16)

    loads[3].wait()
    head_copies = []
    for k in range(1, 17):
        head = (mine + k) % 16
        weight = long_qkv[pl.ds(pl.multiple_of(head * LW, LW), LW), :]
        block = dot(weight, hidden[...], NT).astype(BF16)
        lanes = pl.ds(pl.multiple_of(mine * ROWS, ROWS), ROWS)
        if k == 16:
            qkv[:, lanes] = block
        else:
            packed[k - 1] = block
            copy = remote(
                packed.at[k - 1], qkv.at[:, lanes], (2 * chunk + head // 8, head % 8)
            )
            copy.start()
            head_copies.append(copy)
    for copy in head_copies:
        copy.wait_recv()

    low_half = iota((LW, 128), 1) < 64
    sides = []
    for side in range(2):
        lanes = slice(side * SEG, (side + 1) * SEG)
        ordered = dot(qkv[:, lanes], perm[...])
        sides.append(ordered[:, 0:128])
        ordered = ordered.astype(BF16)
        qx[0:LS, lanes] = ordered[0:LS]
        kx[0:LS, lanes] = ordered[LS : 2 * LS]
        vx[0:LS, lanes] = ordered[2 * LS : LW]
        send2[:, side * 256 : (side + 1) * 256] = ordered[LS:LW, 0:256]
        send3[:, side * 128 : (side + 1) * 128] = ordered[LS:LW, 0:128]
    both = jnp.where(low_half, sides[0], pltpu.roll(sides[1], 64, 1)).astype(BF16)
    send4[...] = both[LS:LW]
    quad = chunk // 4
    inner = chunk % 4
    far_copies = [
        remote(send2, got2, (2 * (chunk + 1 - 2 * (chunk % 2)) + half, t))
    ]
    for k in range(2):
        other = quad * 4 + (1 - inner // 2) * 2 + (inner % 2 + k) % 2
        far_copies.append(remote(send3, got3.at[k], (2 * other + half, t)))
    for k in range(4):
        other = (1 - quad) * 4 + (inner + k) % 4
        far_copies.append(remote(send4, got4.at[k], (2 * other + half, t)))
    for copy in far_copies:
        copy.start()

    def attend(keys, values, queries):
        scores = dot(keys, queries, TN)
        highest = jnp.max(scores, axis=0, keepdims=True)
        weights = jnp.exp2((scores - highest) * LONG_SCALE).astype(BF16)
        return dot(values, weights), highest

    def merge(lanes, other_num, other_top):
        old_top = top[0:1, lanes]
        new_top = jnp.maximum(old_top, other_top)
        num[:, lanes] = num[:, lanes] * jnp.exp2(
            (old_top - new_top) * LONG_SCALE
        ) + other_num * jnp.exp2((other_top - new_top) * LONG_SCALE)
        top[0:1, lanes] = new_top

    def first_pair(i, carry):
        for side in range(2):
            lanes = slice(side * SEG, (side + 1) * SEG)
            spot = pl.ds(pl.multiple_of(side * SEG + i * 256, 256), 256)
            result, highest = attend(kx[:, lanes], vx[:, lanes], qx[:, spot])
            num[:, spot] = result
            top[0:1, spot] = highest
        return carry

    lax.fori_loop(0, 4, first_pair, 0)

    def joined(ref, width):
        return jnp.concatenate([ref[:, 0:width], ref[:, SEG : SEG + width]], axis=1)

    keys = joined(kx, 512)
    values = joined(vx, 512)
    for side in range(2):
        for i in range(2):
            lanes = slice(side * SEG + i * 256, side * SEG + (i + 1) * 256)
            merge(lanes, *attend(keys, values, qx[:, lanes]))

    def arrived(block, count, width, which):
        key = jnp.concatenate([block[0:LS], key_marks(count, width, which)], axis=0)
        value = jnp.concatenate([block[LS : 2 * LS], value_marks(count)], axis=0)
        return key, value

    for copy in far_copies:
        copy.wait_recv()
    beside = chunk + 1 - 2 * (chunk % 2)
    key2, value2 = arrived(got2[...], 512, 256, beside)
    keys = jnp.concatenate([joined(kx, 256), key2], axis=1)
    values = jnp.concatenate([joined(vx, 256), value2], axis=1)
    for side in range(2):
        lanes = slice(side * SEG, side * SEG + 256)
        merge(lanes, *attend(keys, values, qx[:, lanes]))

    keys3 = [joined(kx, 128), key2[:, 0:128], key2[:, 256:384]]
    values3 = [joined(vx, 128), value2[:, 0:128], value2[:, 256:384]]
    for k in range(2):
        other = quad * 4 + (1 - inner // 2) * 2 + (inner % 2 + k) % 2
        key, value = arrived(got3[k], 256, 128, other)
        keys3.append(key)
        values3.append(value)
    keys = jnp.concatenate(keys3, axis=1)
    values = jnp.concatenate(values3, axis=1)
    result, highest = attend(keys, values, joined(qx, 128))
    merge(slice(0, 128), result[:, 0:128], highest[:, 0:128])
    merge(slice(SEG, SEG + 128), result[:, 128:256], highest[:, 128:256])

    lower = iota((KX, 128), 1) < 64

    def packed_pair(a, b):
        moved = pltpu.roll(b.astype(F32), 64, 1)
        return jnp.where(lower, a.astype(F32), moved).astype(BF16)

    keys4 = []
    values4 = []
    for blocks, gather in ((keys3, keys4), (values3, values4)):
        own = blocks[0]
        gather.append(packed_pair(own[:, 0:128], own[:, 128:256]))
        gather.append(packed_pair(blocks[1], blocks[2]))
        for k in range(2):
            far = blocks[3 + k]
            gather.append(packed_pair(far[:, 0:128], far[:, 128:256]))
    for k in range(4):
        other = (1 - quad) * 4 + (inner + 4 - k) % 4
        key, value = arrived(got4[k], 128, 64, other)
        keys4.append(key)
        values4.append(value)
    keys = jnp.concatenate(keys4, axis=1)
    values = jnp.concatenate(values4, axis=1)
    query = packed_pair(qx[:, 0:128], qx[:, SEG : SEG + 128])
    result, highest = attend(keys, values, query)
    highest = jnp.broadcast_to(highest, (8, 128))
    for side in range(2):
        if side == 1:
            result = pltpu.roll(result, 64, 1)
            highest = pltpu.roll(highest, 64, 1)
        lanes = slice(side * SEG, side * SEG + 128)
        merge(
            lanes,
            jnp.where(lower, result, 0.0),
            jnp.where(lower[0:1], highest[0:1], OUTSIDE),
        )

    mix_copies = []
    for side in range(2):
        lanes = slice(side * SEG, (side + 1) * SEG)
        blended = (num[0:LS, lanes] / num[LS : LS + 1, lanes]).astype(BF16)
        natural = dot(blended, perm[...], NT).astype(BF16)
        for i in range(8):
            mix_out[side * 8 + i] = natural[:, i * ROWS : (i + 1) * ROWS]
    for k in range(1, 16):
        device = (mine + k) % 16
        copy = remote(
            mix_out.at[device],
            mix_in.at[mine],
            (2 * chunk + device // 8, device % 8),
        )
        copy.start()
        mix_copies.append(copy)
    mix_in[pl.ds(mine, 1)] = mix_out[pl.ds(mine, 1)]
    loads[4].wait()
    for copy in mix_copies:
        copy.wait_recv()
    mixture = mix_in[...].reshape(LD, ROWS)
    out_ref[...] = (seq[...] + dot(mixture, long_out[...], TN)).astype(BF16)

    for copies in (
        reduce_copies, gather_copies, spread_copies, head_copies, far_copies, mix_copies
    ):
        for copy in copies:
            copy.wait_send()


def whole_layer(*arguments):
    vmem = pl.BlockSpec(memory_space=pltpu.VMEM)
    smem = pl.BlockSpec(memory_space=pltpu.SMEM)
    hbm = pl.BlockSpec(memory_space=pl.ANY)
    return pl.pallas_call(
        whole_kernel,
        out_shape=jax.ShapeDtypeStruct((ROWS, LD), BF16),
        in_specs=[hbm, hbm, hbm, vmem, hbm, vmem, hbm, smem, smem, vmem, hbm, hbm],
        out_specs=vmem,
        scratch_shapes=[
            pltpu.VMEM((TILES_HERE, TOK, D), BF16),
            pltpu.VMEM((VW + 16, D), BF16),
            pltpu.VMEM((VW, 128), F32),
            pltpu.VMEM((2, VW, WIDE), BF16),
            pltpu.VMEM((VH_HERE * VS, TILES_HERE * TOK), BF16),
            pltpu.VMEM((8, D), F32),
            pltpu.VMEM((VH_HERE * VS, D), BF16),
            pltpu.VMEM((D, LD), BF16),
            pltpu.VMEM((ROWS, LD), BF16),
            pltpu.VMEM((LH * LW, LD), BF16),
            pltpu.VMEM((LD, LD), BF16),
            pltpu.VMEM((8, 2, D), F32),
            pltpu.VMEM((8, 2, D), F32),
            pltpu.VMEM((8, 2, LD), F32),
            pltpu.VMEM((256, LD), BF16),
            pltpu.VMEM((ROWS, LD), F32),
            pltpu.VMEM((ROWS, LD), BF16),
            pltpu.VMEM((15, LW, ROWS), BF16),
            pltpu.VMEM((LW, CHUNK), BF16),
            pltpu.VMEM((SEG, SEG), BF16),
            pltpu.VMEM((KX, CHUNK), BF16),
            pltpu.VMEM((KX, CHUNK), BF16),
            pltpu.VMEM((KX, CHUNK), BF16),
            pltpu.VMEM((2 * LS, 512), BF16),
            pltpu.VMEM((2 * LS, 256), BF16),
            pltpu.VMEM((2 * LS, 128), BF16),
            pltpu.VMEM((2 * LS, 512), BF16),
            pltpu.VMEM((2, 2 * LS, 256), BF16),
            pltpu.VMEM((4, 2 * LS, 128), BF16),
            pltpu.VMEM((KX, CHUNK), F32),
            pltpu.VMEM((8, CHUNK), F32),
            pltpu.VMEM((16, LS, ROWS), BF16),
            pltpu.VMEM((16, LS, ROWS), BF16),
            pltpu.SemaphoreType.DMA((TILES_HERE,)),
            pltpu.SemaphoreType.DMA((6,)),
            pltpu.SemaphoreType.DMA((2, 66)),
        ],
        compiler_params=pltpu.CompilerParams(
            collective_id=0,
            has_side_effects=True,
            vmem_limit_bytes=60 * 1024 * 1024,
        ),
    )(*arguments)


def body(
    tile_tokens,
    vit_qkv,
    vit_out,
    tile_norm_gain,
    fresh_proj,
    tile_target,
    cached_rows,
    slide_tiles,
    head_shift,
    long_gain,
    long_qkv,
    long_out,
):
    vit_rows = jnp.transpose(vit_qkv, (1, 2, 3, 0)).reshape(VW, D)
    long_rows = jnp.transpose(long_qkv, (1, 2, 3, 0)).reshape(LH * LW, LD)
    return whole_layer(
        tile_tokens,
        vit_rows,
        vit_out,
        tile_norm_gain.reshape(D // 128, 128),
        fresh_proj,
        tile_target.reshape(1, 256),
        cached_rows,
        slide_tiles,
        head_shift,
        long_gain.reshape(LD // 128, 128),
        long_rows,
        long_out,
    )


def solution(mesh):
    placed = (
        P("dp", None, None),
        P(None, "tensor", None, None),
        P("tensor", None),
        P(),
        P(),
        P(),
        P(("dp", "tensor"), None),
        P(),
        P(),
        P(),
        P(),
        P(),
    )
    return jax.shard_map(
        body, mesh=mesh, in_specs=placed, out_specs=P(("dp", "tensor"), None), check_vma=False
    )
```

```python
import functools
import math

import jax
import jax.numpy as jnp
from jax import lax
from jax.experimental import pallas as pl
from jax.experimental.pallas import tpu as pltpu
from jax.sharding import PartitionSpec as P

MESH = pl.DeviceIdType.MESH
EPSILON = 1e-06
OUTSIDE = -1e30
LOG2E = 1.4426950408889634
NN = (((1,), (0,)), ((), ()))
NT = (((1,), (1,)), ((), ()))
TN = (((0,), (0,)), ((), ()))
F32 = jnp.float32
BF16 = jnp.bfloat16

TILES_HERE = 16
TOK = 256
D = 1536
VH_HERE = 3
VS = 64
VW = VH_HERE * 3 * VS
LD = 768
LH = 16
LS = 48
LW = 3 * LS
ROWS = 128
SEG = 1024
CHUNK = 2048
KX = 64
GROUP = 2
WIDE = GROUP * TOK
AHEAD = 4
VIT_SCALE = LOG2E / math.sqrt(VS)
LONG_SCALE = LOG2E / math.sqrt(LS)


def dot(a, b, dims=NN):
    return lax.dot_general(a, b, dims, preferred_element_type=F32)


def iota(shape, dim):
    return lax.broadcasted_iota(jnp.int32, shape, dim)


def split3(value):
    high = value.astype(BF16)
    rest = value - high.astype(F32)
    middle = rest.astype(BF16)
    low = (rest - middle.astype(F32)).astype(BF16)
    return high, middle, low


def normalize_rows(values):
    center = values - jnp.mean(values, axis=-1, keepdims=True)
    return center * lax.rsqrt(jnp.mean(center * center, axis=-1, keepdims=True) + EPSILON)


def whole_row(ref):
    rows = ref[...].astype(F32)
    return jnp.concatenate([rows[k : k + 1] for k in range(rows.shape[0])], axis=1)


def bit_reversed(rank):
    return (rank % 2) * 8 + (rank // 2 % 2) * 4 + (rank // 4 % 2) * 2 + rank // 8


def whole_kernel(
    tokens_hbm,
    vit_qkv_hbm,
    vit_out_hbm,
    tile_gain_ref,
    fresh_proj_hbm,
    target_ref,
    cached_hbm,
    slide_tiles_ref,
    head_shift_ref,
    long_gain_ref,
    long_qkv_hbm,
    long_out_hbm,
    out_ref,
    tokens,
    vit_qkv,
    csum,
    projected,
    attended,
    token_mean,
    vit_out,
    fresh_proj,
    cached,
    long_qkv,
    long_out,
    part,
    part_in,
    fresh_in,
    fresh_all,
    hidden,
    named_out,
    named_in,
    named_mid,
    named_all,
    same,
    lands,
    keep,
    packed,
    qkv,
    perm,
    qx,
    kx,
    vx,
    send2,
    send3,
    send4,
    got2,
    got3,
    got4,
    num,
    top,
    mix_out,
    mix_in,
    token_sem,
    load_sem,
    sems,
):
    d = lax.axis_index("dp")
    t = lax.axis_index("tensor")
    chunk = d // 2
    half = d % 2
    mine = half * 8 + t

    used = [0]

    def remote(src, dst, device):
        i = used[0]
        used[0] += 1
        return pltpu.make_async_remote_copy(
            src_ref=src,
            dst_ref=dst,
            send_sem=sems.at[0, i],
            recv_sem=sems.at[1, i],
            device_id=device,
            device_id_type=MESH,
        )

    barrier = pltpu.get_barrier_semaphore()
    for k in range(1, 8):
        pl.semaphore_signal(barrier, 1, device_id=(d, (t + k) % 8), device_id_type=MESH)
        pl.semaphore_signal(
            barrier, 1, device_id=(2 * chunk + 1 - half, (t + k) % 8), device_id_type=MESH
        )
    for k in range(1, 16):
        pl.semaphore_signal(barrier, 1, device_id=((d + k) % 16, t), device_id_type=MESH)

    vit_load = pltpu.make_async_copy(vit_qkv_hbm, vit_qkv.at[0:VW], load_sem.at[5])
    vit_load.start()
    loads = [
        pltpu.make_async_copy(src, dst, load_sem.at[i])
        for i, (src, dst) in enumerate(
            [
                (vit_out_hbm, vit_out),
                (fresh_proj_hbm, fresh_proj),
                (cached_hbm, cached),
                (long_qkv_hbm, long_qkv),
                (long_out_hbm, long_out),
            ]
        )
    ]
    loads[2].start()
    token_loads = [
        pltpu.make_async_copy(tokens_hbm.at[i], tokens.at[i], token_sem.at[i])
        for i in range(TILES_HERE)
    ]
    for load in token_loads[:AHEAD]:
        load.start()
    loads[3].start()

    row = iota((16, D), 0)
    col = iota((16, D), 1)
    extra = jnp.where(row == 0, 1.0, jnp.where((row == 1) & (col == 0), 1.0, 0.0))
    vit_qkv[VW : VW + 16, :] = extra.astype(BF16)
    shift = head_shift_ref[mine] % 16
    place = iota((SEG, 1), 0)
    goal = bit_reversed((place + 16 - shift) % 16) * 64 + place // 16
    perm[...] = jnp.where(goal == iota((SEG, SEG), 1), 1.0, 0.0).astype(BF16)
    end0 = slide_tiles_ref[0]
    end1 = end0 + slide_tiles_ref[1]
    end2 = end1 + slide_tiles_ref[2]

    def slides(count, width, which):
        lane = iota((16, count), 1)
        spot = lane % width
        row = (
            SEG * (2 * which + lane // width)
            + 16 * (spot % 64)
            + (bit_reversed(spot // 64) + shift) % 16
        )
        return (
            (row >= end0).astype(jnp.int32)
            + (row >= end1).astype(jnp.int32)
            + (row >= end2).astype(jnp.int32)
        )

    def query_marks(count, width, which):
        ids = slides(count, width, which)
        return jnp.where(ids == iota(ids.shape, 0), 1.0, 0.0).astype(BF16)

    def key_marks(count, width, which):
        ids = slides(count, width, which)
        feature = iota(ids.shape, 0)
        return jnp.where((feature < 4) & (ids != feature), OUTSIDE, 0.0).astype(BF16)

    def value_marks(count):
        return jnp.where(iota((16, count), 0) == 0, 1.0, 0.0).astype(BF16)

    qx[LS:KX, :] = query_marks(CHUNK, SEG, chunk)
    kx[LS:KX, :] = key_marks(CHUNK, SEG, chunk)
    vx[LS:KX, :] = value_marks(CHUNK)


    lane_target = target_ref[...]
    diagonal = iota((256, 256), 0) == iota((256, 256), 1)
    target = jnp.sum(
        jnp.where(diagonal, lane_target.astype(F32), 0.0), axis=1, keepdims=True
    ).astype(jnp.int32)
    equal = target == lane_target
    same[...] = jnp.where(equal, 1.0, 0.0).astype(BF16)
    earlier = jnp.where(equal & (iota((256, 256), 1) < iota((256, 256), 0)), 1.0, 0.0)
    leads = jnp.sum(earlier, axis=1, keepdims=True) < 0.5

    def landing(which, width):
        away = target - which * CHUNK
        spot = away % SEG
        lane = bit_reversed((spot + 16 - shift) % 16) * 64 + spot // 16
        good = leads & (away >= 0) & (away < CHUNK) & (lane < width)
        goal = jnp.where(good, away // SEG * width + lane, -1)
        return jnp.where(goal == iota((256, 2 * width), 1), 1.0, 0.0).astype(BF16)

    quad = chunk // 4
    inner = chunk % 4
    beside = chunk + 1 - 2 * (chunk % 2)
    across = [quad * 4 + (1 - inner // 2) * 2 + (inner % 2 + k) % 2 for k in range(2)]
    beyond = [(1 - quad) * 4 + (inner + 4 - k) % 4 for k in range(4)]
    lands[:, 0:CHUNK] = landing(chunk, SEG)
    lands[:, CHUNK : CHUNK + 512] = landing(beside, 256)
    for k in range(2):
        begin = CHUNK + 512 + 256 * k
        lands[:, begin : begin + 256] = landing(across[k], 128)
    for k in range(4):
        begin = CHUNK + 1024 + 128 * k
        lands[:, begin : begin + 128] = landing(beyond[k], 64)
    keep[...] = 1.0 - dot(jnp.ones((16, 256), BF16), lands[:, 0:CHUNK])[0:8]

    loads[2].wait()
    first_row = (d * 8 + t) * ROWS
    stored = cached[...]
    hidden[...] = (normalize_rows(stored.astype(F32)) * whole_row(long_gain_ref)).astype(BF16)
    mine_only = jnp.where(target - first_row == iota((256, ROWS), 1), 1.0, 0.0).astype(BF16)
    named_out[...] = dot(mine_only, stored).astype(BF16)
    here = pl.ds(pl.multiple_of(d * 16, 16), 16)
    pl.semaphore_wait(barrier, 29)
    named_copies = []
    middle_copies = []
    last_copies = []
    head_copies = []
    far_copies = []
    for k in range(1, 16):
        peer = (d + k) % 16
        there = pl.ds(pl.multiple_of(peer * 16, 16), 16)
        copy = remote(named_out.at[there], named_in.at[here], (peer, t))
        copy.start()
        named_copies.append(copy)
    named_in[here] = named_out[here]

    def sum_over_dp():
        for copy in named_copies:
            copy.wait_recv()
        total = sum(named_in[16 * k : 16 * k + 16].astype(F32) for k in range(16))
        slot = pl.ds(pl.multiple_of(t * 16, 16), 16)
        named_mid[slot] = total.astype(BF16)
        for k in range(1, 8):
            copy = remote(named_mid.at[slot], named_mid.at[slot], (d, (t + k) % 8))
            copy.start()
            middle_copies.append(copy)

    def sum_over_tensor():
        for copy in middle_copies:
            copy.wait_recv()
        total = sum(named_mid[16 * k : 16 * k + 16].astype(F32) for k in range(8))
        named_all[here] = total.astype(BF16)
        for k in range(1, 16):
            copy = remote(named_all.at[here], named_all.at[here], ((d + k) % 16, t))
            copy.start()
            last_copies.append(copy)

    def send_heads():
        loads[3].wait()
        for k in range(1, 17):
            head = (mine + k) % 16
            weight = long_qkv[pl.ds(pl.multiple_of(head * LW, LW), LW), :]
            block = dot(weight, hidden[...], NT).astype(BF16)
            lanes = pl.ds(pl.multiple_of(mine * ROWS, ROWS), ROWS)
            if k == 16:
                qkv[:, lanes] = block
            else:
                packed[k - 1] = block
                copy = remote(
                    packed.at[k - 1], qkv.at[:, lanes], (2 * chunk + head // 8, head % 8)
                )
                copy.start()
                head_copies.append(copy)

    def sort_rows():
        for copy in head_copies:
            copy.wait_recv()
        low_half = iota((LW, 128), 1) < 64
        sides = []
        for side in range(2):
            lanes = slice(side * SEG, (side + 1) * SEG)
            ordered = dot(qkv[:, lanes], perm[...]) * keep[0:1, lanes]
            sides.append(ordered[:, 0:128])
            ordered = ordered.astype(BF16)
            qx[0:LS, lanes] = ordered[0:LS]
            kx[0:LS, lanes] = ordered[LS : 2 * LS]
            vx[0:LS, lanes] = ordered[2 * LS : LW]
            send2[:, side * 256 : (side + 1) * 256] = ordered[LS:LW, 0:256]
            send3[:, side * 128 : (side + 1) * 128] = ordered[LS:LW, 0:128]
        both = jnp.where(low_half, sides[0], pltpu.roll(sides[1], 64, 1)).astype(BF16)
        send4[...] = both[LS:LW]
        far_copies.append(
            remote(send2, got2, (2 * (chunk + 1 - 2 * (chunk % 2)) + half, t))
        )
        for k in range(2):
            other = quad * 4 + (1 - inner // 2) * 2 + (inner % 2 + k) % 2
            far_copies.append(remote(send3, got3.at[k], (2 * other + half, t)))
        for k in range(4):
            other = (1 - quad) * 4 + (inner + k) % 4
            far_copies.append(remote(send4, got4.at[k], (2 * other + half, t)))
        for copy in far_copies:
            copy.start()

    vit_load.wait()
    csum[...] = dot(vit_qkv[0:VW], jnp.ones((D, 128), BF16))

    def project(group):
        for i in range(GROUP):
            token_loads[group * GROUP + i].wait()
        for i in range(GROUP):
            after = group * GROUP + i + AHEAD
            if after < TILES_HERE:
                token_loads[after].start()
        x = tokens[group * GROUP : (group + 1) * GROUP].reshape(WIDE, D)
        raw = dot(vit_qkv[...], x, NT)
        mean = raw[VW : VW + 1] * (1.0 / D)
        shift_row = mean - raw[VW + 1 : VW + 2]
        first = x[:, 0:1].astype(F32)
        squares = jnp.zeros((WIDE, 128), F32)
        for k in range(D // 128):
            delta = x[:, 128 * k : 128 * (k + 1)].astype(F32) - first
            squares = squares + delta * delta
        ones = jnp.ones((16, 128), BF16)
        total = sum(dot(ones, piece, NT) for piece in split3(squares))
        variance = jnp.maximum(total[0:1] * (1.0 / D) - shift_row * shift_row, 0.0)
        scale = lax.rsqrt(variance + EPSILON)
        spread = jnp.concatenate([csum[...]] * (WIDE // 128), axis=1)
        projected[group % 2] = ((raw[0:VW] - spread * mean) * scale).astype(BF16)

    def attention(group):
        for i in range(GROUP):
            lanes = slice(i * TOK, (i + 1) * TOK)

            def piece(head, which):
                first = (head * 3 + which) * VS
                return projected[group % 2, first : first + VS, lanes]

            heads = range(VH_HERE)
            scores = [dot(piece(head, 1), piece(head, 0), TN) for head in heads]
            highest = [jnp.max(score, axis=0, keepdims=True) for score in scores]
            weights = [
                jnp.exp2((score - high) * VIT_SCALE) for score, high in zip(scores, highest)
            ]
            sums = [jnp.sum(weight, axis=0, keepdims=True) for weight in weights]
            mixed = [
                dot(piece(head, 2), weights[head].astype(BF16)) for head in heads
            ]
            place = (group * GROUP + i) * TOK
            for head in heads:
                attended[head * VS : (head + 1) * VS, place : place + TOK] = (
                    mixed[head] / sums[head]
                ).astype(BF16)

    groups = TILES_HERE // GROUP
    project(0)
    send_heads()
    for group in range(groups):
        if group + 1 < groups:
            project(group + 1)
        if group == groups - 3:
            for i in (0, 1, 4):
                loads[i].start()
        attention(group)
        if group == 1:
            sum_over_dp()
        if group == 2:
            sort_rows()
        if group == 3:
            sum_over_tensor()
    for i in range(2):
        sums = dot(jnp.ones((16, TOK), BF16), tokens[2 * t + i])
        token_mean[i : i + 1, :] = sums[0:1] * (1.0 / TOK)
    tile_of = iota((TILES_HERE, TILES_HERE * TOK), 1) // TOK
    picks = jnp.where(iota(tile_of.shape, 0) == tile_of, 1.0 / TOK, 0.0).astype(BF16)
    pooled_term = dot(picks, attended[...], NT)

    loads[0].wait()
    high, middle, low = split3(pooled_term)
    weight = vit_out[...]
    partial = dot(high, weight) + dot(middle, weight) + dot(low, weight)
    for k in range(8):
        part[k] = partial[2 * k : 2 * k + 2]
    reduce_copies = []
    for k in range(1, 8):
        peer = (t + k) % 8
        copy = remote(part.at[peer], part_in.at[t], (d, peer))
        copy.start()
        reduce_copies.append(copy)
    part_in[pl.ds(t, 1)] = part[pl.ds(t, 1)]

    for copy in reduce_copies:
        copy.wait_recv()
    pooled = token_mean[0:2, :]
    for k in range(8):
        pooled = pooled + part_in[k]
    normed = (normalize_rows(pooled) * whole_row(tile_gain_ref)).astype(BF16)
    loads[1].wait()
    fresh = dot(normed, fresh_proj[...])
    fresh_in[pl.ds(t, 1)] = fresh[None]
    gather_copies = []
    for k in range(1, 8):
        copy = remote(fresh_in.at[t], fresh_in.at[t], (d, (t + k) % 8))
        copy.start()
        gather_copies.append(copy)
    for copy in gather_copies:
        copy.wait_recv()
    group = jnp.concatenate([fresh_in[k] for k in range(8)], axis=0).astype(BF16)
    fresh_all[here, :] = group
    spread_copies = []
    for k in range(1, 16):
        copy = remote(fresh_all.at[here], fresh_all.at[here], ((d + k) % 16, t))
        copy.start()
        spread_copies.append(copy)
    for copy in last_copies:
        copy.wait_recv()
    for copy in far_copies:
        copy.wait_recv()
    for copy in spread_copies:
        copy.wait_recv()

    changed = named_all[...].astype(F32) + dot(same[...], fresh_all[...])
    changed = (normalize_rows(changed) * whole_row(long_gain_ref)).astype(BF16)
    weight = long_qkv[pl.ds(pl.multiple_of(mine * LW, LW), LW), :]
    renewed = dot(weight, changed, NT).astype(BF16)

    def add(ref, rows, lanes, change):
        ref[rows, lanes] = (ref[rows, lanes].astype(F32) + change).astype(BF16)

    change = dot(renewed, lands[:, 0:CHUNK])
    everything = slice(0, CHUNK)
    add(qx, slice(0, LS), everything, change[0:LS])
    add(kx, slice(0, LS), everything, change[LS : 2 * LS])
    add(vx, slice(0, LS), everything, change[2 * LS : LW])
    far_change = dot(renewed[LS:LW], lands[:, CHUNK : CHUNK + 1536])

    def attend(keys, values, queries):
        scores = dot(keys, queries, TN)
        highest = jnp.max(scores, axis=0, keepdims=True)
        weights = jnp.exp2((scores - highest) * LONG_SCALE).astype(BF16)
        return dot(values, weights), highest

    def merge(lanes, other_num, other_top):
        old_top = top[0:1, lanes]
        new_top = jnp.maximum(old_top, other_top)
        num[:, lanes] = num[:, lanes] * jnp.exp2(
            (old_top - new_top) * LONG_SCALE
        ) + other_num * jnp.exp2((other_top - new_top) * LONG_SCALE)
        top[0:1, lanes] = new_top

    def first_pair(i, carry):
        for side in range(2):
            lanes = slice(side * SEG, (side + 1) * SEG)
            spot = pl.ds(pl.multiple_of(side * SEG + i * 256, 256), 256)
            result, highest = attend(kx[:, lanes], vx[:, lanes], qx[:, spot])
            num[:, spot] = result
            top[0:1, spot] = highest
        return carry

    lax.fori_loop(0, 4, first_pair, 0)

    def joined(ref, width):
        return jnp.concatenate([ref[:, 0:width], ref[:, SEG : SEG + width]], axis=1)

    keys = joined(kx, 512)
    values = joined(vx, 512)
    for side in range(2):
        for i in range(2):
            lanes = slice(side * SEG + i * 256, side * SEG + (i + 1) * 256)
            merge(lanes, *attend(keys, values, qx[:, lanes]))

    def arrived(block, begin, count, width, which):
        block = (block.astype(F32) + far_change[:, begin : begin + count]).astype(BF16)
        key = jnp.concatenate([block[0:LS], key_marks(count, width, which)], axis=0)
        value = jnp.concatenate([block[LS : 2 * LS], value_marks(count)], axis=0)
        return key, value

    key2, value2 = arrived(got2[...], 0, 512, 256, beside)
    keys = jnp.concatenate([joined(kx, 256), key2], axis=1)
    values = jnp.concatenate([joined(vx, 256), value2], axis=1)
    for side in range(2):
        lanes = slice(side * SEG, side * SEG + 256)
        merge(lanes, *attend(keys, values, qx[:, lanes]))

    keys3 = [joined(kx, 128), key2[:, 0:128], key2[:, 256:384]]
    values3 = [joined(vx, 128), value2[:, 0:128], value2[:, 256:384]]
    for k in range(2):
        key, value = arrived(got3[k], 512 + 256 * k, 256, 128, across[k])
        keys3.append(key)
        values3.append(value)
    keys = jnp.concatenate(keys3, axis=1)
    values = jnp.concatenate(values3, axis=1)
    result, highest = attend(keys, values, joined(qx, 128))
    merge(slice(0, 128), result[:, 0:128], highest[:, 0:128])
    merge(slice(SEG, SEG + 128), result[:, 128:256], highest[:, 128:256])

    lower = iota((KX, 128), 1) < 64

    def packed_pair(a, b):
        moved = pltpu.roll(b.astype(F32), 64, 1)
        return jnp.where(lower, a.astype(F32), moved).astype(BF16)

    keys4 = []
    values4 = []
    for blocks, gather in ((keys3, keys4), (values3, values4)):
        own = blocks[0]
        gather.append(packed_pair(own[:, 0:128], own[:, 128:256]))
        gather.append(packed_pair(blocks[1], blocks[2]))
        for k in range(2):
            far = blocks[3 + k]
            gather.append(packed_pair(far[:, 0:128], far[:, 128:256]))
    for k in range(4):
        key, value = arrived(got4[k], 1024 + 128 * k, 128, 64, beyond[k])
        keys4.append(key)
        values4.append(value)
    keys = jnp.concatenate(keys4, axis=1)
    values = jnp.concatenate(values4, axis=1)
    query = packed_pair(qx[:, 0:128], qx[:, SEG : SEG + 128])
    result, highest = attend(keys, values, query)
    highest = jnp.broadcast_to(highest, (8, 128))
    for side in range(2):
        if side == 1:
            result = pltpu.roll(result, 64, 1)
            highest = pltpu.roll(highest, 64, 1)
        lanes = slice(side * SEG, side * SEG + 128)
        merge(
            lanes,
            jnp.where(lower, result, 0.0),
            jnp.where(lower[0:1], highest[0:1], OUTSIDE),
        )

    mix_copies = []
    for side in range(2):
        lanes = slice(side * SEG, (side + 1) * SEG)
        blended = (num[0:LS, lanes] / num[LS : LS + 1, lanes]).astype(BF16)
        natural = dot(blended, perm[...], NT).astype(BF16)
        for i in range(8):
            mix_out[side * 8 + i] = natural[:, i * ROWS : (i + 1) * ROWS]
    for k in range(1, 16):
        device = (mine + k) % 16
        copy = remote(
            mix_out.at[device],
            mix_in.at[mine],
            (2 * chunk + device // 8, device % 8),
        )
        copy.start()
        mix_copies.append(copy)
    mix_in[pl.ds(mine, 1)] = mix_out[pl.ds(mine, 1)]
    match = (lane_target - first_row == iota((ROWS, 256), 0))
    match = jnp.where(match, 1.0, 0.0).astype(BF16)
    rows = cached[...].astype(F32) + dot(match, fresh_all[...])
    loads[4].wait()
    for copy in mix_copies:
        copy.wait_recv()
    mixture = mix_in[...].reshape(LD, ROWS)
    out_ref[...] = (rows + dot(mixture, long_out[...], TN)).astype(BF16)

    for copies in (
        named_copies, middle_copies, last_copies,
        reduce_copies, gather_copies, spread_copies, head_copies, far_copies, mix_copies
    ):
        for copy in copies:
            copy.wait_send()


def whole_layer(*arguments):
    vmem = pl.BlockSpec(memory_space=pltpu.VMEM)
    smem = pl.BlockSpec(memory_space=pltpu.SMEM)
    hbm = pl.BlockSpec(memory_space=pl.ANY)
    return pl.pallas_call(
        whole_kernel,
        out_shape=jax.ShapeDtypeStruct((ROWS, LD), BF16),
        in_specs=[hbm, hbm, hbm, vmem, hbm, vmem, hbm, smem, smem, vmem, hbm, hbm],
        out_specs=vmem,
        scratch_shapes=[
            pltpu.VMEM((TILES_HERE, TOK, D), BF16),
            pltpu.VMEM((VW + 16, D), BF16),
            pltpu.VMEM((VW, 128), F32),
            pltpu.VMEM((2, VW, WIDE), BF16),
            pltpu.VMEM((VH_HERE * VS, TILES_HERE * TOK), BF16),
            pltpu.VMEM((8, D), F32),
            pltpu.VMEM((VH_HERE * VS, D), BF16),
            pltpu.VMEM((D, LD), BF16),
            pltpu.VMEM((ROWS, LD), BF16),
            pltpu.VMEM((LH * LW, LD), BF16),
            pltpu.VMEM((LD, LD), BF16),
            pltpu.VMEM((8, 2, D), F32),
            pltpu.VMEM((8, 2, D), F32),
            pltpu.VMEM((8, 2, LD), F32),
            pltpu.VMEM((256, LD), BF16),
            pltpu.VMEM((ROWS, LD), BF16),
            pltpu.VMEM((256, LD), BF16),
            pltpu.VMEM((256, LD), BF16),
            pltpu.VMEM((128, LD), BF16),
            pltpu.VMEM((256, LD), BF16),
            pltpu.VMEM((256, 256), BF16),
            pltpu.VMEM((256, CHUNK + 1536), BF16),
            pltpu.VMEM((8, CHUNK), F32),
            pltpu.VMEM((15, LW, ROWS), BF16),
            pltpu.VMEM((LW, CHUNK), BF16),
            pltpu.VMEM((SEG, SEG), BF16),
            pltpu.VMEM((KX, CHUNK), BF16),
            pltpu.VMEM((KX, CHUNK), BF16),
            pltpu.VMEM((KX, CHUNK), BF16),
            pltpu.VMEM((2 * LS, 512), BF16),
            pltpu.VMEM((2 * LS, 256), BF16),
            pltpu.VMEM((2 * LS, 128), BF16),
            pltpu.VMEM((2 * LS, 512), BF16),
            pltpu.VMEM((2, 2 * LS, 256), BF16),
            pltpu.VMEM((4, 2 * LS, 128), BF16),
            pltpu.VMEM((KX, CHUNK), F32),
            pltpu.VMEM((8, CHUNK), F32),
            pltpu.VMEM((16, LS, ROWS), BF16),
            pltpu.VMEM((16, LS, ROWS), BF16),
            pltpu.SemaphoreType.DMA((TILES_HERE,)),
            pltpu.SemaphoreType.DMA((6,)),
            pltpu.SemaphoreType.DMA((2, 103)),
        ],
        compiler_params=pltpu.CompilerParams(
            collective_id=0,
            has_side_effects=True,
            vmem_limit_bytes=60 * 1024 * 1024,
        ),
    )(*arguments)


def body(
    tile_tokens,
    vit_qkv,
    vit_out,
    tile_norm_gain,
    fresh_proj,
    tile_target,
    cached_rows,
    slide_tiles,
    head_shift,
    long_gain,
    long_qkv,
    long_out,
):
    vit_rows = jnp.transpose(vit_qkv, (1, 2, 3, 0)).reshape(VW, D)
    long_rows = jnp.transpose(long_qkv, (1, 2, 3, 0)).reshape(LH * LW, LD)
    return whole_layer(
        tile_tokens,
        vit_rows,
        vit_out,
        tile_norm_gain.reshape(D // 128, 128),
        fresh_proj,
        tile_target.reshape(1, 256),
        cached_rows,
        slide_tiles,
        head_shift,
        long_gain.reshape(LD // 128, 128),
        long_rows,
        long_out,
    )


def solution(mesh):
    placed = (
        P("dp", None, None),
        P(None, "tensor", None, None),
        P("tensor", None),
        P(),
        P(),
        P(),
        P(("dp", "tensor"), None),
        P(),
        P(),
        P(),
        P(),
        P(),
    )
    return jax.shard_map(
        body, mesh=mesh, in_specs=placed, out_specs=P(("dp", "tensor"), None), check_vma=False
    )
```

```python
import functools
import math

import jax
import jax.numpy as jnp
from jax import lax
from jax.experimental import pallas as pl
from jax.experimental.pallas import tpu as pltpu
from jax.sharding import PartitionSpec as P

MESH = pl.DeviceIdType.MESH
EPSILON = 1e-06
OUTSIDE = -1e30
LOG2E = 1.4426950408889634
NN = (((1,), (0,)), ((), ()))
NT = (((1,), (1,)), ((), ()))
TN = (((0,), (0,)), ((), ()))
F32 = jnp.float32
BF16 = jnp.bfloat16

TILES_HERE = 16
TOK = 256
D = 1536
VH_HERE = 3
VS = 64
VW = VH_HERE * 3 * VS
LD = 768
LH = 16
LS = 48
LW = 3 * LS
ROWS = 128
SEG = 1024
CHUNK = 2048
KX = 64
GROUP = 2
WIDE = GROUP * TOK
AHEAD = 4
VIT_SCALE = LOG2E / math.sqrt(VS)
LONG_SCALE = LOG2E / math.sqrt(LS)


def dot(a, b, dims=NN):
    return lax.dot_general(a, b, dims, preferred_element_type=F32)


def iota(shape, dim):
    return lax.broadcasted_iota(jnp.int32, shape, dim)


def split3(value):
    high = value.astype(BF16)
    rest = value - high.astype(F32)
    middle = rest.astype(BF16)
    low = (rest - middle.astype(F32)).astype(BF16)
    return high, middle, low


def normalize_rows(values):
    center = values - jnp.mean(values, axis=-1, keepdims=True)
    return center * lax.rsqrt(jnp.mean(center * center, axis=-1, keepdims=True) + EPSILON)


def whole_row(ref):
    rows = ref[...].astype(F32)
    return jnp.concatenate([rows[k : k + 1] for k in range(rows.shape[0])], axis=1)


def bit_reversed(rank):
    return (rank % 2) * 8 + (rank // 2 % 2) * 4 + (rank // 4 % 2) * 2 + rank // 8


def whole_kernel(
    tokens_hbm,
    vit_qkv_hbm,
    vit_out_hbm,
    tile_gain_ref,
    fresh_proj_hbm,
    target_ref,
    cached_hbm,
    slide_tiles_ref,
    head_shift_ref,
    long_gain_ref,
    long_qkv_hbm,
    long_out_hbm,
    out_ref,
    tokens,
    vit_qkv,
    csum,
    projected,
    attended,
    token_mean,
    vit_out,
    fresh_proj,
    cached,
    long_qkv,
    long_out,
    part,
    part_in,
    fresh_in,
    fresh_all,
    hidden,
    named_out,
    named_in,
    named_mid,
    named_all,
    same,
    lands,
    keep,
    packed,
    qkv,
    perm,
    qx,
    kx,
    vx,
    keys_by_row,
    send2,
    send3,
    send4,
    got2,
    got3,
    got4,
    num,
    top,
    mix_out,
    mix_in,
    token_sem,
    load_sem,
    sems,
):
    d = lax.axis_index("dp")
    t = lax.axis_index("tensor")
    chunk = d // 2
    half = d % 2
    mine = half * 8 + t

    def remote(i, src, dst, device):
        return pltpu.make_async_remote_copy(
            src_ref=src,
            dst_ref=dst,
            send_sem=sems.at[0, i],
            recv_sem=sems.at[1, i],
            device_id=device,
            device_id_type=MESH,
        )

    def tile_rows(index):
        return pl.ds(pl.multiple_of(index * 16, 16), 16)

    def chunk_device(index):
        return 2 * chunk + index // 8, index % 8

    def named_copy(k):
        peer = (d + k) % 16
        return remote(
            k - 1, named_out.at[tile_rows(peer)], named_in.at[tile_rows(d)], (peer, t)
        )

    def middle_copy(k):
        slot = named_mid.at[tile_rows(t)]
        return remote(14 + k, slot, slot, (d, (t + k) % 8))

    def last_copy(k):
        slot = named_all.at[tile_rows(d)]
        return remote(21 + k, slot, slot, ((d + k) % 16, t))

    def head_copy(k):
        lanes = pl.ds(pl.multiple_of(mine * ROWS, ROWS), ROWS)
        return remote(
            36 + k, packed.at[k - 1], qkv.at[:, lanes], chunk_device((mine + k) % 16)
        )

    def far_copy(k):
        quad, inner = chunk // 4, chunk % 4
        if k == 0:
            return remote(52, send2, got2, (2 * (chunk + 1 - 2 * (chunk % 2)) + half, t))
        if k < 3:
            other = quad * 4 + (1 - inner // 2) * 2 + (inner % 2 + k - 1) % 2
            return remote(52 + k, send3, got3.at[k - 1], (2 * other + half, t))
        other = (1 - quad) * 4 + (inner + k - 3) % 4
        return remote(52 + k, send4, got4.at[k - 3], (2 * other + half, t))

    def reduce_copy(k):
        peer = (t + k) % 8
        return remote(58 + k, part.at[peer], part_in.at[t], (d, peer))

    def gather_copy(k):
        return remote(65 + k, fresh_in.at[t], fresh_in.at[t], (d, (t + k) % 8))

    def spread_copy(k):
        slot = fresh_all.at[tile_rows(d)]
        return remote(72 + k, slot, slot, ((d + k) % 16, t))

    def mix_copy(k):
        device = (mine + k) % 16
        return remote(87 + k, mix_out.at[device], mix_in.at[mine], chunk_device(device))

    def every(copy, count, what):
        first = 0 if copy is far_copy else 1
        for k in range(first, first + count):
            getattr(copy(k), what)()

    barrier = pltpu.get_barrier_semaphore()
    for k in range(1, 8):
        pl.semaphore_signal(barrier, 1, device_id=(d, (t + k) % 8), device_id_type=MESH)
        pl.semaphore_signal(
            barrier, 1, device_id=(2 * chunk + 1 - half, (t + k) % 8), device_id_type=MESH
        )
    for k in range(1, 16):
        pl.semaphore_signal(barrier, 1, device_id=((d + k) % 16, t), device_id_type=MESH)

    vit_load = pltpu.make_async_copy(vit_qkv_hbm, vit_qkv.at[0:VW], load_sem.at[5])
    vit_load.start()
    loads = [
        pltpu.make_async_copy(src, dst, load_sem.at[i])
        for i, (src, dst) in enumerate(
            [
                (vit_out_hbm, vit_out),
                (fresh_proj_hbm, fresh_proj),
                (cached_hbm, cached),
                (long_qkv_hbm, long_qkv),
                (long_out_hbm, long_out),
            ]
        )
    ]
    loads[2].start()
    def token_load(i):
        return pltpu.make_async_copy(tokens_hbm.at[i], tokens.at[i], token_sem.at[i])

    for i in range(AHEAD):
        token_load(i).start()
    loads[3].start()

    row = iota((16, D), 0)
    col = iota((16, D), 1)
    extra = jnp.where(row == 0, 1.0, jnp.where((row == 1) & (col == 0), 1.0, 0.0))
    vit_qkv[VW : VW + 16, :] = extra.astype(BF16)
    shift = head_shift_ref[mine] % 16
    place = iota((SEG, 1), 0)
    goal = bit_reversed((place + 16 - shift) % 16) * 64 + place // 16
    perm[...] = jnp.where(goal == iota((SEG, SEG), 1), 1.0, 0.0).astype(BF16)
    end0 = slide_tiles_ref[0]
    end1 = end0 + slide_tiles_ref[1]
    end2 = end1 + slide_tiles_ref[2]

    def slides(count, width, which):
        lane = iota((16, count), 1)
        spot = lane % width
        row = (
            SEG * (2 * which + lane // width)
            + 16 * (spot % 64)
            + (bit_reversed(spot // 64) + shift) % 16
        )
        return (
            (row >= end0).astype(jnp.int32)
            + (row >= end1).astype(jnp.int32)
            + (row >= end2).astype(jnp.int32)
        )

    def query_marks(count, width, which):
        ids = slides(count, width, which)
        return jnp.where(ids == iota(ids.shape, 0), 1.0, 0.0).astype(BF16)

    def key_marks(count, width, which):
        ids = slides(count, width, which)
        feature = iota(ids.shape, 0)
        return jnp.where((feature < 4) & (ids != feature), OUTSIDE, 0.0).astype(BF16)

    def value_marks(count):
        return jnp.where(iota((16, count), 0) == 0, 1.0, 0.0).astype(BF16)

    qx[LS:KX, :] = query_marks(CHUNK, SEG, chunk)
    kx[LS:KX, :] = key_marks(CHUNK, SEG, chunk)
    vx[LS:KX, :] = value_marks(CHUNK)


    lane_target = target_ref[...]
    diagonal = iota((256, 256), 0) == iota((256, 256), 1)
    target = jnp.sum(
        jnp.where(diagonal, lane_target.astype(F32), 0.0), axis=1, keepdims=True
    ).astype(jnp.int32)
    equal = target == lane_target
    same[...] = jnp.where(equal, 1.0, 0.0).astype(BF16)
    earlier = jnp.where(equal & (iota((256, 256), 1) < iota((256, 256), 0)), 1.0, 0.0)
    leads = jnp.sum(earlier, axis=1, keepdims=True) < 0.5

    def landing(which, width):
        away = target - which * CHUNK
        spot = away % SEG
        lane = bit_reversed((spot + 16 - shift) % 16) * 64 + spot // 16
        good = leads & (away >= 0) & (away < CHUNK) & (lane < width)
        goal = jnp.where(good, away // SEG * width + lane, -1)
        return jnp.where(goal == iota((256, 2 * width), 1), 1.0, 0.0).astype(BF16)

    quad = chunk // 4
    inner = chunk % 4
    beside = chunk + 1 - 2 * (chunk % 2)
    across = [quad * 4 + (1 - inner // 2) * 2 + (inner % 2 + k) % 2 for k in range(2)]
    beyond = [(1 - quad) * 4 + (inner + 4 - k) % 4 for k in range(4)]
    lands[:, 0:CHUNK] = landing(chunk, SEG)
    lands[:, CHUNK : CHUNK + 512] = landing(beside, 256)
    for k in range(2):
        begin = CHUNK + 512 + 256 * k
        lands[:, begin : begin + 256] = landing(across[k], 128)
    for k in range(4):
        begin = CHUNK + 1024 + 128 * k
        lands[:, begin : begin + 128] = landing(beyond[k], 64)
    keep[...] = 1.0 - dot(jnp.ones((16, 256), BF16), lands[:, 0:CHUNK])[0:8]

    loads[2].wait()
    first_row = (d * 8 + t) * ROWS
    stored = cached[...]
    hidden[...] = (normalize_rows(stored.astype(F32)) * whole_row(long_gain_ref)).astype(BF16)
    mine_only = jnp.where(target - first_row == iota((256, ROWS), 1), 1.0, 0.0).astype(BF16)
    named_out[...] = dot(mine_only, stored).astype(BF16)
    pl.semaphore_wait(barrier, 29)
    every(named_copy, 15, "start")
    named_in[tile_rows(d)] = named_out[tile_rows(d)]

    def sum_over_dp():
        every(named_copy, 15, "wait_recv")
        total = sum(named_in[16 * k : 16 * k + 16].astype(F32) for k in range(16))
        named_mid[tile_rows(t)] = total.astype(BF16)
        every(middle_copy, 7, "start")

    def sum_over_tensor():
        every(middle_copy, 7, "wait_recv")
        total = sum(named_mid[16 * k : 16 * k + 16].astype(F32) for k in range(8))
        named_all[tile_rows(d)] = total.astype(BF16)
        every(last_copy, 15, "start")

    def head_block(head):
        weight = long_qkv[pl.ds(pl.multiple_of(head * LW, LW), LW), :]
        return dot(weight, hidden[...], NT).astype(BF16)

    def send_heads():
        loads[3].wait()

        def send_head(k, carry):
            packed[k - 1] = head_block((mine + k) % 16)
            head_copy(k).start()
            return carry

        lax.fori_loop(1, 16, send_head, 0)
        qkv[:, pl.ds(pl.multiple_of(mine * ROWS, ROWS), ROWS)] = head_block(mine)

    def sort_rows():
        every(head_copy, 15, "wait_recv")
        low_half = iota((LW, 128), 1) < 64
        sides = []
        for side in range(2):
            lanes = slice(side * SEG, (side + 1) * SEG)
            ordered = dot(qkv[:, lanes], perm[...]) * keep[0:1, lanes]
            sides.append(ordered[:, 0:128])
            ordered = ordered.astype(BF16)
            qx[0:LS, lanes] = ordered[0:LS]
            kx[0:LS, lanes] = ordered[LS : 2 * LS]
            vx[0:LS, lanes] = ordered[2 * LS : LW]
            send2[:, side * 256 : (side + 1) * 256] = ordered[LS:LW, 0:256]
            send3[:, side * 128 : (side + 1) * 128] = ordered[LS:LW, 0:128]
        both = jnp.where(low_half, sides[0], pltpu.roll(sides[1], 64, 1)).astype(BF16)
        send4[...] = both[LS:LW]
        every(far_copy, 7, "start")

    vit_load.wait()
    csum[...] = dot(vit_qkv[0:VW], jnp.ones((D, 128), BF16))

    def project(group):
        for i in range(GROUP):
            token_load(group * GROUP + i).wait()
        for i in range(GROUP):
            after = group * GROUP + i + AHEAD

            @pl.when(after < TILES_HERE)
            def _():
                token_load(after).start()

        x = tokens[pl.ds(group * GROUP, GROUP)].reshape(WIDE, D)
        raw = dot(vit_qkv[...], x, NT)
        mean = raw[VW : VW + 1] * (1.0 / D)
        shift_row = mean - raw[VW + 1 : VW + 2]
        first = x[:, 0:1].astype(F32)
        squares = jnp.zeros((WIDE, 128), F32)
        for k in range(D // 128):
            delta = x[:, 128 * k : 128 * (k + 1)].astype(F32) - first
            squares = squares + delta * delta
        ones = jnp.ones((16, 128), BF16)
        total = sum(dot(ones, piece, NT) for piece in split3(squares))
        variance = jnp.maximum(total[0:1] * (1.0 / D) - shift_row * shift_row, 0.0)
        scale = lax.rsqrt(variance + EPSILON)
        spread = jnp.concatenate([csum[...]] * (WIDE // 128), axis=1)
        projected[...] = ((raw[0:VW] - spread * mean) * scale).astype(BF16)

    def attention(group):
        def piece(job, which):
            i, head = job
            first = (head * 3 + which) * VS
            return projected[first : first + VS, i * TOK : (i + 1) * TOK]

        jobs = [(i, head) for i in range(GROUP) for head in range(VH_HERE)]
        scores = [dot(piece(job, 1), piece(job, 0), TN) for job in jobs]
        highest = [jnp.max(score, axis=0, keepdims=True) for score in scores]
        weights = [
            jnp.exp2((score - high) * VIT_SCALE) for score, high in zip(scores, highest)
        ]
        sums = [jnp.sum(weight, axis=0, keepdims=True) for weight in weights]
        mixed = [dot(piece(job, 2), weight.astype(BF16)) for job, weight in zip(jobs, weights)]
        for (i, head), mixture, total in zip(jobs, mixed, sums):
            place = pl.ds(pl.multiple_of((group * GROUP + i) * TOK, TOK), TOK)
            attended[head * VS : (head + 1) * VS, place] = (mixture / total).astype(BF16)

    groups = TILES_HERE // GROUP

    def one_group(group, carry):
        project(group)
        attention(group)

        @pl.when(group == 0)
        def _():
            send_heads()

        @pl.when(group == 1)
        def _():
            sum_over_dp()

        @pl.when(group == 2)
        def _():
            sort_rows()

        @pl.when(group == 3)
        def _():
            sum_over_tensor()
            for i in (0, 1, 4):
                loads[i].start()

        return carry

    lax.fori_loop(0, groups, one_group, 0)
    for i in range(2):
        sums = dot(jnp.ones((16, TOK), BF16), tokens[2 * t + i])
        token_mean[i : i + 1, :] = sums[0:1] * (1.0 / TOK)
    tile_of = iota((TILES_HERE, TILES_HERE * TOK), 1) // TOK
    picks = jnp.where(iota(tile_of.shape, 0) == tile_of, 1.0 / TOK, 0.0).astype(BF16)
    pooled_term = dot(picks, attended[...], NT)

    loads[0].wait()
    high, middle, low = split3(pooled_term)
    weight = vit_out[...]
    partial = dot(high, weight) + dot(middle, weight) + dot(low, weight)
    for k in range(8):
        part[k] = partial[2 * k : 2 * k + 2]
    every(reduce_copy, 7, "start")
    part_in[pl.ds(t, 1)] = part[pl.ds(t, 1)]

    every(reduce_copy, 7, "wait_recv")
    pooled = token_mean[0:2, :]
    for k in range(8):
        pooled = pooled + part_in[k]
    normed = (normalize_rows(pooled) * whole_row(tile_gain_ref)).astype(BF16)
    loads[1].wait()
    fresh = dot(normed, fresh_proj[...])
    fresh_in[pl.ds(t, 1)] = fresh[None]
    every(gather_copy, 7, "start")
    every(gather_copy, 7, "wait_recv")
    group = jnp.concatenate([fresh_in[k] for k in range(8)], axis=0).astype(BF16)
    fresh_all[tile_rows(d)] = group
    every(spread_copy, 15, "start")
    every(last_copy, 15, "wait_recv")
    every(far_copy, 7, "wait_recv")
    every(spread_copy, 15, "wait_recv")

    changed = named_all[...].astype(F32) + dot(same[...], fresh_all[...])
    changed = (normalize_rows(changed) * whole_row(long_gain_ref)).astype(BF16)
    weight = long_qkv[pl.ds(pl.multiple_of(mine * LW, LW), LW), :]
    renewed = dot(weight, changed, NT).astype(BF16)

    def add(ref, rows, lanes, change):
        ref[rows, lanes] = (ref[rows, lanes].astype(F32) + change).astype(BF16)

    change = dot(renewed, lands[:, 0:CHUNK])
    everything = slice(0, CHUNK)
    add(qx, slice(0, LS), everything, change[0:LS])
    add(kx, slice(0, LS), everything, change[LS : 2 * LS])
    add(vx, slice(0, LS), everything, change[2 * LS : LW])
    far_change = dot(renewed[LS:LW], lands[:, CHUNK : CHUNK + 1536])
    for side in range(2):
        lanes = slice(side * SEG, (side + 1) * SEG)
        keys_by_row[lanes, :] = jnp.transpose(kx[:, lanes])

    def attend(keys, values, queries):
        scores = dot(keys, queries)
        highest = jnp.max(scores, axis=0, keepdims=True)
        weights = jnp.exp2((scores - highest) * LONG_SCALE).astype(BF16)
        return dot(values, weights), highest

    def merge(lanes, other_num, other_top):
        old_top = top[0:1, lanes]
        new_top = jnp.maximum(old_top, other_top)
        num[:, lanes] = num[:, lanes] * jnp.exp2(
            (old_top - new_top) * LONG_SCALE
        ) + other_num * jnp.exp2((other_top - new_top) * LONG_SCALE)
        top[0:1, lanes] = new_top

    def first_pair(i, carry):
        for side in range(2):
            lanes = slice(side * SEG, (side + 1) * SEG)
            spot = pl.ds(pl.multiple_of(side * SEG + i * 256, 256), 256)
            result, highest = attend(keys_by_row[lanes, :], vx[:, lanes], qx[:, spot])
            num[:, spot] = result
            top[0:1, spot] = highest
        return carry

    lax.fori_loop(0, 4, first_pair, 0)

    def joined(ref, width):
        return jnp.concatenate([ref[:, 0:width], ref[:, SEG : SEG + width]], axis=1)

    def joined_rows(width):
        return [keys_by_row[0:width, :], keys_by_row[SEG : SEG + width, :]]

    def second_pair(i, carry):
        keys = jnp.concatenate(joined_rows(512), axis=0)
        values = joined(vx, 512)
        for side in range(2):
            spot = pl.ds(pl.multiple_of(side * SEG + i * 256, 256), 256)
            merge(spot, *attend(keys, values, qx[:, spot]))
        return carry

    lax.fori_loop(0, 2, second_pair, 0)

    def arrived(block, begin, count, width, which):
        block = (block.astype(F32) + far_change[:, begin : begin + count]).astype(BF16)
        key = jnp.concatenate([block[0:LS], key_marks(count, width, which)], axis=0)
        value = jnp.concatenate([block[LS : 2 * LS], value_marks(count)], axis=0)
        return jnp.transpose(key), value

    key2, value2 = arrived(got2[...], 0, 512, 256, beside)
    keys = jnp.concatenate(joined_rows(256) + [key2], axis=0)
    values = jnp.concatenate([joined(vx, 256), value2], axis=1)
    for side in range(2):
        lanes = slice(side * SEG, side * SEG + 256)
        merge(lanes, *attend(keys, values, qx[:, lanes]))

    keys3 = joined_rows(128) + [key2[0:128], key2[256:384]]
    values3 = [joined(vx, 128), value2[:, 0:128], value2[:, 256:384]]
    for k in range(2):
        key, value = arrived(got3[k], 512 + 256 * k, 256, 128, across[k])
        keys3 += [key[0:128], key[128:256]]
        values3.append(value)
    keys = jnp.concatenate(keys3, axis=0)
    values = jnp.concatenate(values3, axis=1)
    result, highest = attend(keys, values, joined(qx, 128))
    merge(slice(0, 128), result[:, 0:128], highest[:, 0:128])
    merge(slice(SEG, SEG + 128), result[:, 128:256], highest[:, 128:256])

    lower = iota((KX, 128), 1) < 64

    def packed_pair(a, b):
        moved = pltpu.roll(b.astype(F32), 64, 1)
        return jnp.where(lower, a.astype(F32), moved).astype(BF16)

    keys4 = [key[0:64] for key in keys3]
    own = values3[0]
    values4 = [
        packed_pair(own[:, 0:128], own[:, 128:256]),
        packed_pair(values3[1], values3[2]),
    ]
    for far in values3[3:]:
        values4.append(packed_pair(far[:, 0:128], far[:, 128:256]))
    for k in range(4):
        key, value = arrived(got4[k], 1024 + 128 * k, 128, 64, beyond[k])
        keys4.append(key)
        values4.append(value)
    keys = jnp.concatenate(keys4, axis=0)
    values = jnp.concatenate(values4, axis=1)
    query = packed_pair(qx[:, 0:128], qx[:, SEG : SEG + 128])
    result, highest = attend(keys, values, query)
    highest = jnp.broadcast_to(highest, (8, 128))
    for side in range(2):
        if side == 1:
            result = pltpu.roll(result, 64, 1)
            highest = pltpu.roll(highest, 64, 1)
        lanes = slice(side * SEG, side * SEG + 128)
        merge(
            lanes,
            jnp.where(lower, result, 0.0),
            jnp.where(lower[0:1], highest[0:1], OUTSIDE),
        )

    for side in range(2):
        lanes = slice(side * SEG, (side + 1) * SEG)
        blended = (num[0:LS, lanes] / num[LS : LS + 1, lanes]).astype(BF16)
        natural = dot(blended, perm[...], NT).astype(BF16)
        for i in range(8):
            mix_out[side * 8 + i] = natural[:, i * ROWS : (i + 1) * ROWS]
    every(mix_copy, 15, "start")
    mix_in[pl.ds(mine, 1)] = mix_out[pl.ds(mine, 1)]
    match = (lane_target - first_row == iota((ROWS, 256), 0))
    match = jnp.where(match, 1.0, 0.0).astype(BF16)
    rows = cached[...].astype(F32) + dot(match, fresh_all[...])
    loads[4].wait()
    every(mix_copy, 15, "wait_recv")
    mixture = mix_in[...].reshape(LD, ROWS)
    out_ref[...] = (rows + dot(mixture, long_out[...], TN)).astype(BF16)

    for copy, count in (
        (named_copy, 15),
        (middle_copy, 7),
        (last_copy, 15),
        (head_copy, 15),
        (far_copy, 7),
        (reduce_copy, 7),
        (gather_copy, 7),
        (spread_copy, 15),
        (mix_copy, 15),
    ):
        every(copy, count, "wait_send")


def whole_layer(*arguments):
    vmem = pl.BlockSpec(memory_space=pltpu.VMEM)
    smem = pl.BlockSpec(memory_space=pltpu.SMEM)
    hbm = pl.BlockSpec(memory_space=pl.ANY)
    return pl.pallas_call(
        whole_kernel,
        out_shape=jax.ShapeDtypeStruct((ROWS, LD), BF16),
        in_specs=[hbm, hbm, hbm, vmem, hbm, vmem, hbm, smem, smem, vmem, hbm, hbm],
        out_specs=vmem,
        scratch_shapes=[
            pltpu.VMEM((TILES_HERE, TOK, D), BF16),
            pltpu.VMEM((VW + 16, D), BF16),
            pltpu.VMEM((VW, 128), F32),
            pltpu.VMEM((VW, WIDE), BF16),
            pltpu.VMEM((VH_HERE * VS, TILES_HERE * TOK), BF16),
            pltpu.VMEM((8, D), F32),
            pltpu.VMEM((VH_HERE * VS, D), BF16),
            pltpu.VMEM((D, LD), BF16),
            pltpu.VMEM((ROWS, LD), BF16),
            pltpu.VMEM((LH * LW, LD), BF16),
            pltpu.VMEM((LD, LD), BF16),
            pltpu.VMEM((8, 2, D), F32),
            pltpu.VMEM((8, 2, D), F32),
            pltpu.VMEM((8, 2, LD), F32),
            pltpu.VMEM((256, LD), BF16),
            pltpu.VMEM((ROWS, LD), BF16),
            pltpu.VMEM((256, LD), BF16),
            pltpu.VMEM((256, LD), BF16),
            pltpu.VMEM((128, LD), BF16),
            pltpu.VMEM((256, LD), BF16),
            pltpu.VMEM((256, 256), BF16),
            pltpu.VMEM((256, CHUNK + 1536), BF16),
            pltpu.VMEM((8, CHUNK), F32),
            pltpu.VMEM((15, LW, ROWS), BF16),
            pltpu.VMEM((LW, CHUNK), BF16),
            pltpu.VMEM((SEG, SEG), BF16),
            pltpu.VMEM((KX, CHUNK), BF16),
            pltpu.VMEM((KX, CHUNK), BF16),
            pltpu.VMEM((KX, CHUNK), BF16),
            pltpu.VMEM((CHUNK, KX), BF16),
            pltpu.VMEM((2 * LS, 512), BF16),
            pltpu.VMEM((2 * LS, 256), BF16),
            pltpu.VMEM((2 * LS, 128), BF16),
            pltpu.VMEM((2 * LS, 512), BF16),
            pltpu.VMEM((2, 2 * LS, 256), BF16),
            pltpu.VMEM((4, 2 * LS, 128), BF16),
            pltpu.VMEM((KX, CHUNK), F32),
            pltpu.VMEM((8, CHUNK), F32),
            pltpu.VMEM((16, LS, ROWS), BF16),
            pltpu.VMEM((16, LS, ROWS), BF16),
            pltpu.SemaphoreType.DMA((TILES_HERE,)),
            pltpu.SemaphoreType.DMA((6,)),
            pltpu.SemaphoreType.DMA((2, 103)),
        ],
        compiler_params=pltpu.CompilerParams(
            collective_id=0,
            has_side_effects=True,
            vmem_limit_bytes=60 * 1024 * 1024,
        ),
    )(*arguments)


def body(
    tile_tokens,
    vit_qkv,
    vit_out,
    tile_norm_gain,
    fresh_proj,
    tile_target,
    cached_rows,
    slide_tiles,
    head_shift,
    long_gain,
    long_qkv,
    long_out,
):
    vit_rows = jnp.transpose(vit_qkv, (1, 2, 3, 0)).reshape(VW, D)
    long_rows = jnp.transpose(long_qkv, (1, 2, 3, 0)).reshape(LH * LW, LD)
    return whole_layer(
        tile_tokens,
        vit_rows,
        vit_out,
        tile_norm_gain.reshape(D // 128, 128),
        fresh_proj,
        tile_target.reshape(1, 256),
        cached_rows,
        slide_tiles,
        head_shift,
        long_gain.reshape(LD // 128, 128),
        long_rows,
        long_out,
    )


def solution(mesh):
    placed = (
        P("dp", None, None),
        P(None, "tensor", None, None),
        P("tensor", None),
        P(),
        P(),
        P(),
        P(("dp", "tensor"), None),
        P(),
        P(),
        P(),
        P(),
        P(),
    )
    return jax.shard_map(
        body, mesh=mesh, in_specs=placed, out_specs=P(("dp", "tensor"), None), check_vma=False
    )
```

```python
import functools
import math

import jax
import jax.numpy as jnp
from jax import lax
from jax.experimental import pallas as pl
from jax.experimental.pallas import tpu as pltpu
from jax.sharding import PartitionSpec as P

MESH = pl.DeviceIdType.MESH
EPSILON = 1e-06
OUTSIDE = -1e30
LOG2E = 1.4426950408889634
NN = (((1,), (0,)), ((), ()))
NT = (((1,), (1,)), ((), ()))
TN = (((0,), (0,)), ((), ()))
F32 = jnp.float32
BF16 = jnp.bfloat16

TILES_HERE = 16
TOK = 256
D = 1536
VH_HERE = 3
VS = 64
VW = VH_HERE * 3 * VS
LD = 768
LH = 16
LS = 48
LW = 3 * LS
ROWS = 128
SEG = 1024
CHUNK = 2048
KX = 64
FAR = 1536
GROUP = 4
WIDE = GROUP * TOK
AHEAD = 4
VIT_SCALE = LOG2E / math.sqrt(VS)
LONG_SCALE = LOG2E / math.sqrt(LS)


def dot(a, b, dims=NN):
    return lax.dot_general(a, b, dims, preferred_element_type=F32)


def iota(shape, dim):
    return lax.broadcasted_iota(jnp.int32, shape, dim)


def split3(value):
    high = value.astype(BF16)
    rest = value - high.astype(F32)
    middle = rest.astype(BF16)
    low = (rest - middle.astype(F32)).astype(BF16)
    return high, middle, low


def normalize_rows(values):
    center = values - jnp.mean(values, axis=-1, keepdims=True)
    return center * lax.rsqrt(jnp.mean(center * center, axis=-1, keepdims=True) + EPSILON)


def whole_row(ref):
    rows = ref[...].astype(F32)
    return jnp.concatenate([rows[k : k + 1] for k in range(rows.shape[0])], axis=1)


def whole_kernel(
    tokens_hbm,
    vit_qkv_hbm,
    vit_out_hbm,
    tile_gain_ref,
    fresh_proj_hbm,
    target_ref,
    cached_hbm,
    slide_tiles_ref,
    head_shift_ref,
    long_gain_ref,
    long_qkv_hbm,
    long_out_hbm,
    out_ref,
    tokens,
    vit_qkv,
    csum,
    projected,
    attended,
    token_mean,
    vit_out,
    fresh_proj,
    cached,
    long_qkv,
    long_out,
    part,
    part_in,
    fresh_in,
    fresh_all,
    hidden,
    named_out,
    named_in,
    named_mid,
    named_all,
    same,
    lands,
    keep,
    far_marks,
    packed,
    qkv,
    perm,
    qx,
    kx,
    vx,
    keys_by_row,
    send2,
    send3,
    send4,
    got2,
    got3,
    got4,
    num,
    top,
    mix_out,
    mix_in,
    token_sem,
    load_sem,
    sems,
):
    d = lax.axis_index("dp")
    t = lax.axis_index("tensor")
    chunk = d // 2
    half = d % 2
    mine = half * 8 + t

    def remote(i, src, dst, device):
        return pltpu.make_async_remote_copy(
            src_ref=src,
            dst_ref=dst,
            send_sem=sems.at[0, i],
            recv_sem=sems.at[1, i],
            device_id=device,
            device_id_type=MESH,
        )

    half_lanes = pl.ds(pl.multiple_of(t % 2 * (LD // 2), LD // 2), LD // 2)

    def tile_rows(index):
        return pl.ds(pl.multiple_of(index * 16, 16), 16)

    def chunk_device(index):
        return 2 * chunk + index // 8, index % 8

    def named_copy(k):
        peer = (d + k) % 16
        return remote(
            k - 1, named_out.at[tile_rows(peer)], named_in.at[tile_rows(d)], (peer, t)
        )

    def middle_copy(k):
        slot = named_mid.at[tile_rows(t)]
        return remote(14 + k, slot, slot, (d, (t + k) % 8))

    def last_copy(k):
        slot = named_all.at[tile_rows(d)]
        return remote(21 + k, slot, slot, ((d + k) % 16, t))

    def head_copy(k):
        lanes = pl.ds(pl.multiple_of(mine * ROWS, ROWS), ROWS)
        return remote(
            36 + k, packed.at[k - 1], qkv.at[:, lanes], chunk_device((mine + k) % 16)
        )

    def far_copy(k):
        quad, inner = chunk // 4, chunk % 4
        if k == 0:
            return remote(52, send2, got2, (2 * (chunk + 1 - 2 * (chunk % 2)) + half, t))
        if k < 3:
            other = quad * 4 + (1 - inner // 2) * 2 + (inner % 2 + k - 1) % 2
            return remote(52 + k, send3, got3.at[k - 1], (2 * other + half, t))
        other = (1 - quad) * 4 + (inner + k - 3) % 4
        return remote(52 + k, send4, got4.at[k - 3], (2 * other + half, t))

    def reduce_copy(k):
        peer = (t + k) % 8
        return remote(58 + k, part.at[peer], part_in.at[t], (d, peer))

    def gather_copy(k):
        return remote(65 + k, fresh_in.at[t], fresh_in.at[t], (d, (t + k) % 8))

    def spread_copy(k):
        slot = fresh_all.at[tile_rows(d), half_lanes]
        return remote(72 + k, slot, slot, ((d + k) % 16, t))

    def sibling_copy(k):
        slot = fresh_all.at[:, half_lanes]
        return remote(102 + k, slot, slot, (d, t + 1 - 2 * (t % 2)))

    def mix_copy(k):
        device = (mine + k) % 16
        return remote(87 + k, mix_out.at[device], mix_in.at[mine], chunk_device(device))

    def every(copy, count, what):
        first = 0 if copy is far_copy else 1
        for k in range(first, first + count):
            getattr(copy(k), what)()

    barrier = pltpu.get_barrier_semaphore()
    for k in range(1, 8):
        pl.semaphore_signal(barrier, 1, device_id=(d, (t + k) % 8), device_id_type=MESH)
        pl.semaphore_signal(
            barrier, 1, device_id=(2 * chunk + 1 - half, (t + k) % 8), device_id_type=MESH
        )
    for k in range(1, 16):
        pl.semaphore_signal(barrier, 1, device_id=((d + k) % 16, t), device_id_type=MESH)

    vit_load = pltpu.make_async_copy(vit_qkv_hbm, vit_qkv.at[0:VW], load_sem.at[5])
    vit_load.start()
    loads = [
        pltpu.make_async_copy(src, dst, load_sem.at[i])
        for i, (src, dst) in enumerate(
            [
                (vit_out_hbm, vit_out),
                (fresh_proj_hbm, fresh_proj),
                (cached_hbm, cached),
                (long_qkv_hbm, long_qkv),
                (long_out_hbm, long_out),
            ]
        )
    ]
    loads[2].start()
    def token_load(i):
        return pltpu.make_async_copy(tokens_hbm.at[i], tokens.at[i], token_sem.at[i])

    for i in range(AHEAD):
        token_load(i).start()
    loads[3].start()

    row = iota((16, D), 0)
    col = iota((16, D), 1)
    extra = jnp.where(row == 0, 1.0, jnp.where((row == 1) & (col == 0), 1.0, 0.0))
    vit_qkv[VW : VW + 16, :] = extra.astype(BF16)
    shift = head_shift_ref[mine] & 15
    end0 = slide_tiles_ref[0]
    end1 = end0 + slide_tiles_ref[1]
    end2 = end1 + slide_tiles_ref[2]

    def picked_rows(count, bits, which):
        lane = iota((1, count), 1)
        spot = lane & ((1 << bits) - 1)
        rank = spot >> 6
        turned = ((rank & 1) << 3) | ((rank & 2) << 1) | ((rank & 4) >> 1) | ((rank & 8) >> 3)
        inside = ((spot & 63) << 4) + ((turned + shift) & 15)
        return SEG * (2 * which + (lane >> bits)) + inside

    quad = chunk // 4
    inner = chunk % 4
    beside = chunk + 1 - 2 * (chunk % 2)
    across = [quad * 4 + (1 - inner // 2) * 2 + (inner % 2 + k) % 2 for k in range(2)]
    beyond = [(1 - quad) * 4 + (inner + 4 - k) % 4 for k in range(4)]
    every_row = jnp.concatenate(
        [picked_rows(CHUNK, 10, chunk), picked_rows(512, 8, beside)]
        + [picked_rows(256, 7, which) for which in across]
        + [picked_rows(128, 6, which) for which in beyond],
        axis=1,
    )
    perm[...] = jnp.where(
        iota((SEG, SEG), 0) == picked_rows(SEG, 10, 0), 1.0, 0.0
    ).astype(BF16)
    ids = (
        (every_row >= end0).astype(jnp.int32)
        + (every_row >= end1).astype(jnp.int32)
        + (every_row >= end2).astype(jnp.int32)
    )
    feature = iota((16, CHUNK + FAR), 0)
    own = ids[:, 0:CHUNK]
    qx[LS:KX, :] = jnp.where(own == feature[:, 0:CHUNK], 1.0, 0.0).astype(BF16)
    marks = jnp.where((feature < 4) & (ids != feature), OUTSIDE, 0.0).astype(BF16)
    kx[LS:KX, :] = marks[:, 0:CHUNK]
    far_marks[...] = marks[:, CHUNK:]

    def value_marks(count):
        return jnp.where(iota((16, count), 0) == 0, 1.0, 0.0).astype(BF16)

    vx[LS:KX, :] = value_marks(CHUNK)

    lane_target = target_ref[...]
    diagonal = iota((256, 256), 0) == iota((256, 256), 1)
    target = jnp.sum(
        jnp.where(diagonal, lane_target.astype(F32), 0.0), axis=1, keepdims=True
    ).astype(jnp.int32)
    equal = target == lane_target
    same[...] = jnp.where(equal, 1.0, 0.0).astype(BF16)
    earlier = jnp.where(equal & (iota((256, 256), 1) < iota((256, 256), 0)), 1.0, 0.0)
    leads = jnp.sum(earlier, axis=1, keepdims=True) < 0.5
    lands[...] = jnp.where(jnp.where(leads, target, -1) == every_row, 1.0, 0.0).astype(BF16)
    keep[...] = 1.0 - dot(jnp.ones((16, 256), BF16), lands[:, 0:CHUNK])[0:8]

    loads[2].wait()
    first_row = (d * 8 + t) * ROWS
    stored = cached[...]
    hidden[...] = (normalize_rows(stored.astype(F32)) * whole_row(long_gain_ref)).astype(BF16)
    mine_only = jnp.where(target - first_row == iota((256, ROWS), 1), 1.0, 0.0).astype(BF16)
    named_out[...] = dot(mine_only, stored).astype(BF16)
    pl.semaphore_wait(barrier, 29)
    every(named_copy, 15, "start")
    named_in[tile_rows(d)] = named_out[tile_rows(d)]

    def sum_over_dp():
        every(named_copy, 15, "wait_recv")
        total = sum(named_in[16 * k : 16 * k + 16].astype(F32) for k in range(16))
        named_mid[tile_rows(t)] = total.astype(BF16)
        every(middle_copy, 7, "start")

    def sum_over_tensor():
        every(middle_copy, 7, "wait_recv")
        total = sum(named_mid[16 * k : 16 * k + 16].astype(F32) for k in range(8))
        named_all[tile_rows(d)] = total.astype(BF16)
        every(last_copy, 15, "start")

    def head_block(head):
        weight = long_qkv[pl.ds(pl.multiple_of(head * LW, LW), LW), :]
        return dot(weight, hidden[...], NT).astype(BF16)

    def send_heads():
        loads[3].wait()

        def send_head(k, carry):
            packed[k - 1] = head_block((mine + k) % 16)
            head_copy(k).start()
            return carry

        lax.fori_loop(1, 16, send_head, 0)
        qkv[:, pl.ds(pl.multiple_of(mine * ROWS, ROWS), ROWS)] = head_block(mine)

    def sort_rows():
        every(head_copy, 15, "wait_recv")
        low_half = iota((LW, 128), 1) < 64
        sides = []
        for side in range(2):
            lanes = slice(side * SEG, (side + 1) * SEG)
            ordered = dot(qkv[:, lanes], perm[...]) * keep[0:1, lanes]
            sides.append(ordered[:, 0:128])
            ordered = ordered.astype(BF16)
            qx[0:LS, lanes] = ordered[0:LS]
            kx[0:LS, lanes] = ordered[LS : 2 * LS]
            vx[0:LS, lanes] = ordered[2 * LS : LW]
            send2[:, side * 256 : (side + 1) * 256] = ordered[LS:LW, 0:256]
            send3[:, side * 128 : (side + 1) * 128] = ordered[LS:LW, 0:128]
        both = jnp.where(low_half, sides[0], pltpu.roll(sides[1], 64, 1)).astype(BF16)
        send4[...] = both[LS:LW]
        every(far_copy, 7, "start")

    vit_load.wait()
    csum[...] = dot(vit_qkv[0:VW], jnp.ones((D, 128), BF16))

    def project(group):
        for i in range(GROUP):
            token_load(group * GROUP + i).wait()
        for i in range(GROUP):
            after = group * GROUP + i + AHEAD

            @pl.when(after < TILES_HERE)
            def _():
                token_load(after).start()

        x = tokens[pl.ds(group * GROUP, GROUP)].reshape(WIDE, D)
        raw = dot(vit_qkv[...], x, NT)
        mean = raw[VW : VW + 1] * (1.0 / D)
        shift_row = mean - raw[VW + 1 : VW + 2]
        first = x[:, 0:1].astype(F32)
        squares = jnp.zeros((WIDE, 128), F32)
        for k in range(D // 128):
            delta = x[:, 128 * k : 128 * (k + 1)].astype(F32) - first
            squares = squares + delta * delta
        ones = jnp.ones((16, 128), BF16)
        total = sum(dot(ones, piece, NT) for piece in split3(squares))
        variance = jnp.maximum(total[0:1] * (1.0 / D) - shift_row * shift_row, 0.0)
        scale = lax.rsqrt(variance + EPSILON)
        spread = jnp.concatenate([csum[...]] * (WIDE // 128), axis=1)
        projected[...] = ((raw[0:VW] - spread * mean) * scale).astype(BF16)

    def attention(group):
        def piece(job, which):
            i, head = job
            first = (head * 3 + which) * VS
            return projected[first : first + VS, i * TOK : (i + 1) * TOK]

        jobs = [(i, head) for i in range(GROUP) for head in range(VH_HERE)]
        scores = [dot(piece(job, 1), piece(job, 0), TN) for job in jobs]
        highest = [jnp.max(score, axis=0, keepdims=True) for score in scores]
        weights = [
            jnp.exp2((score - high) * VIT_SCALE) for score, high in zip(scores, highest)
        ]
        sums = [jnp.sum(weight, axis=0, keepdims=True) for weight in weights]
        mixed = [dot(piece(job, 2), weight.astype(BF16)) for job, weight in zip(jobs, weights)]
        for (i, head), mixture, total in zip(jobs, mixed, sums):
            place = pl.ds(pl.multiple_of((group * GROUP + i) * TOK, TOK), TOK)
            attended[head * VS : (head + 1) * VS, place] = (mixture / total).astype(BF16)

    groups = TILES_HERE // GROUP

    def one_group(group, carry):
        project(group)
        attention(group)

        @pl.when(group == 0)
        def _():
            send_heads()
            sum_over_dp()

        @pl.when(group == 1)
        def _():
            sort_rows()
            sum_over_tensor()

        @pl.when(group == 2)
        def _():
            for i in (0, 1, 4):
                loads[i].start()

        return carry

    lax.fori_loop(0, groups, one_group, 0)
    for i in range(2):
        sums = dot(jnp.ones((16, TOK), BF16), tokens[2 * t + i])
        token_mean[i : i + 1, :] = sums[0:1] * (1.0 / TOK)
    tile_of = iota((TILES_HERE, TILES_HERE * TOK), 1) // TOK
    picks = jnp.where(iota(tile_of.shape, 0) == tile_of, 1.0 / TOK, 0.0).astype(BF16)
    pooled_term = dot(picks, attended[...], NT)

    loads[0].wait()
    partial = dot(jnp.concatenate(split3(pooled_term), axis=0), vit_out[...])
    partial = partial[0:16] + partial[16:32] + partial[32:48]
    for k in range(8):
        part[k] = partial[2 * k : 2 * k + 2]
    every(reduce_copy, 7, "start")
    part_in[pl.ds(t, 1)] = part[pl.ds(t, 1)]

    every(reduce_copy, 7, "wait_recv")
    pooled = token_mean[0:2, :]
    for k in range(8):
        pooled = pooled + part_in[k]
    normed = (normalize_rows(pooled) * whole_row(tile_gain_ref)).astype(BF16)
    loads[1].wait()
    fresh = dot(normed, fresh_proj[...])
    fresh_in[pl.ds(t, 1)] = fresh[None]
    every(gather_copy, 7, "start")
    every(gather_copy, 7, "wait_recv")
    group = jnp.concatenate([fresh_in[k] for k in range(8)], axis=0).astype(BF16)
    fresh_all[tile_rows(d), half_lanes] = jnp.where(
        t % 2 == 0, group[:, 0 : LD // 2], group[:, LD // 2 : LD]
    )
    every(spread_copy, 15, "start")
    every(last_copy, 15, "wait_recv")
    every(far_copy, 7, "wait_recv")
    every(spread_copy, 15, "wait_recv")
    every(sibling_copy, 1, "start")
    every(sibling_copy, 1, "wait_recv")

    changed = named_all[...].astype(F32) + dot(same[...], fresh_all[...])
    changed = (normalize_rows(changed) * whole_row(long_gain_ref)).astype(BF16)
    weight = long_qkv[pl.ds(pl.multiple_of(mine * LW, LW), LW), :]
    renewed = dot(weight, changed, NT).astype(BF16)

    def add(ref, rows, lanes, change):
        ref[rows, lanes] = (ref[rows, lanes].astype(F32) + change).astype(BF16)

    change = dot(renewed, lands[:, 0:CHUNK])
    everything = slice(0, CHUNK)
    add(qx, slice(0, LS), everything, change[0:LS])
    add(kx, slice(0, LS), everything, change[LS : 2 * LS])
    add(vx, slice(0, LS), everything, change[2 * LS : LW])
    far_change = dot(renewed[LS:LW], lands[:, CHUNK : CHUNK + FAR])
    for side in range(2):
        lanes = slice(side * SEG, (side + 1) * SEG)
        keys_by_row[lanes, :] = jnp.transpose(kx[:, lanes])

    def attend(jobs):
        scores = [dot(keys, queries) for keys, _, queries in jobs]
        highest = [jnp.max(score, axis=0, keepdims=True) for score in scores]
        weights = [
            jnp.exp2((score - high) * LONG_SCALE).astype(BF16)
            for score, high in zip(scores, highest)
        ]
        results = [dot(values, weight) for (_, values, _), weight in zip(jobs, weights)]
        return list(zip(results, highest))

    def merge(lanes, other_num, other_top):
        old_top = top[0:1, lanes]
        new_top = jnp.maximum(old_top, other_top)
        num[:, lanes] = num[:, lanes] * jnp.exp2(
            (old_top - new_top) * LONG_SCALE
        ) + other_num * jnp.exp2((other_top - new_top) * LONG_SCALE)
        top[0:1, lanes] = new_top

    def first_pair(i, carry):
        jobs = []
        spots = []
        for side in range(2):
            lanes = slice(side * SEG, (side + 1) * SEG)
            spot = pl.ds(pl.multiple_of(side * SEG + i * 512, 512), 512)
            jobs.append((keys_by_row[lanes, :], vx[:, lanes], qx[:, spot]))
            spots.append(spot)
        for spot, (result, highest) in zip(spots, attend(jobs)):
            num[:, spot] = result
            top[0:1, spot] = highest
        return carry

    lax.fori_loop(0, 2, first_pair, 0)

    def joined(ref, width):
        return jnp.concatenate([ref[:, 0:width], ref[:, SEG : SEG + width]], axis=1)

    def joined_rows(width):
        return [keys_by_row[0:width, :], keys_by_row[SEG : SEG + width, :]]

    keys = jnp.concatenate(joined_rows(512), axis=0)
    values = joined(vx, 512)
    jobs = [(keys, values, qx[:, side * SEG : side * SEG + 512]) for side in range(2)]

    def arrived(block, begin, count):
        place = slice(begin, begin + count)
        block = (block.astype(F32) + far_change[:, place]).astype(BF16)
        key = jnp.concatenate([block[0:LS], far_marks[:, place]], axis=0)
        value = jnp.concatenate([block[LS : 2 * LS], value_marks(count)], axis=0)
        return jnp.transpose(key), value

    key2, value2 = arrived(got2[...], 0, 512)
    keys = jnp.concatenate(joined_rows(256) + [key2], axis=0)
    values = jnp.concatenate([joined(vx, 256), value2], axis=1)
    jobs.append((keys, values, joined(qx, 256)))

    keys3 = joined_rows(128) + [key2[0:128], key2[256:384]]
    values3 = [joined(vx, 128), value2[:, 0:128], value2[:, 256:384]]
    for k in range(2):
        key, value = arrived(got3[k], 512 + 256 * k, 256)
        keys3 += [key[0:128], key[128:256]]
        values3.append(value)
    keys = jnp.concatenate(keys3, axis=0)
    values = jnp.concatenate(values3, axis=1)
    jobs.append((keys, values, joined(qx, 128)))

    lower = iota((KX, 128), 1) < 64

    def packed_pair(a, b):
        moved = pltpu.roll(b.astype(F32), 64, 1)
        return jnp.where(lower, a.astype(F32), moved).astype(BF16)

    keys4 = [key[0:64] for key in keys3]
    own = values3[0]
    values4 = [
        packed_pair(own[:, 0:128], own[:, 128:256]),
        packed_pair(values3[1], values3[2]),
    ]
    for far in values3[3:]:
        values4.append(packed_pair(far[:, 0:128], far[:, 128:256]))
    for k in range(4):
        key, value = arrived(got4[k], 1024 + 128 * k, 128)
        keys4.append(key)
        values4.append(value)
    keys = jnp.concatenate(keys4, axis=0)
    values = jnp.concatenate(values4, axis=1)
    query = packed_pair(qx[:, 0:128], qx[:, SEG : SEG + 128])
    jobs.append((keys, values, query))
    done = attend(jobs)
    for side in range(2):
        merge(slice(side * SEG, side * SEG + 512), *done[side])
    for (result, highest), width in ((done[2], 256), (done[3], 128)):
        for side in range(2):
            lanes = slice(side * width, (side + 1) * width)
            merge(
                slice(side * SEG, side * SEG + width), result[:, lanes], highest[:, lanes]
            )
    result, highest = done[4]
    highest = jnp.broadcast_to(highest, (8, 128))
    for side in range(2):
        if side == 1:
            result = pltpu.roll(result, 64, 1)
            highest = pltpu.roll(highest, 64, 1)
        lanes = slice(side * SEG, side * SEG + 128)
        merge(
            lanes,
            jnp.where(lower, result, 0.0),
            jnp.where(lower[0:1], highest[0:1], OUTSIDE),
        )

    for side in range(2):
        lanes = slice(side * SEG, (side + 1) * SEG)
        blended = (num[0:LS, lanes] * (1.0 / num[LS : LS + 1, lanes])).astype(BF16)
        natural = dot(blended, perm[...], NT).astype(BF16)
        for i in range(8):
            mix_out[side * 8 + i] = natural[:, i * ROWS : (i + 1) * ROWS]
    every(mix_copy, 15, "start")
    mix_in[pl.ds(mine, 1)] = mix_out[pl.ds(mine, 1)]
    match = (lane_target - first_row == iota((ROWS, 256), 0))
    match = jnp.where(match, 1.0, 0.0).astype(BF16)
    rows = cached[...].astype(F32) + dot(match, fresh_all[...])
    loads[4].wait()
    every(mix_copy, 15, "wait_recv")
    mixture = mix_in[...].reshape(LD, ROWS)
    out_ref[...] = (rows + dot(mixture, long_out[...], TN)).astype(BF16)

    for copy, count in (
        (named_copy, 15),
        (middle_copy, 7),
        (last_copy, 15),
        (head_copy, 15),
        (far_copy, 7),
        (reduce_copy, 7),
        (gather_copy, 7),
        (spread_copy, 15),
        (sibling_copy, 1),
        (mix_copy, 15),
    ):
        every(copy, count, "wait_send")


def whole_layer(*arguments):
    vmem = pl.BlockSpec(memory_space=pltpu.VMEM)
    smem = pl.BlockSpec(memory_space=pltpu.SMEM)
    hbm = pl.BlockSpec(memory_space=pl.ANY)
    return pl.pallas_call(
        whole_kernel,
        out_shape=jax.ShapeDtypeStruct((ROWS, LD), BF16),
        in_specs=[hbm, hbm, hbm, vmem, hbm, vmem, hbm, smem, smem, vmem, hbm, hbm],
        out_specs=vmem,
        scratch_shapes=[
            pltpu.VMEM((TILES_HERE, TOK, D), BF16),
            pltpu.VMEM((VW + 16, D), BF16),
            pltpu.VMEM((VW, 128), F32),
            pltpu.VMEM((VW, WIDE), BF16),
            pltpu.VMEM((VH_HERE * VS, TILES_HERE * TOK), BF16),
            pltpu.VMEM((8, D), F32),
            pltpu.VMEM((VH_HERE * VS, D), BF16),
            pltpu.VMEM((D, LD), BF16),
            pltpu.VMEM((ROWS, LD), BF16),
            pltpu.VMEM((LH * LW, LD), BF16),
            pltpu.VMEM((LD, LD), BF16),
            pltpu.VMEM((8, 2, D), F32),
            pltpu.VMEM((8, 2, D), F32),
            pltpu.VMEM((8, 2, LD), F32),
            pltpu.VMEM((256, LD), BF16),
            pltpu.VMEM((ROWS, LD), BF16),
            pltpu.VMEM((256, LD), BF16),
            pltpu.VMEM((256, LD), BF16),
            pltpu.VMEM((128, LD), BF16),
            pltpu.VMEM((256, LD), BF16),
            pltpu.VMEM((256, 256), BF16),
            pltpu.VMEM((256, CHUNK + FAR), BF16),
            pltpu.VMEM((8, CHUNK), F32),
            pltpu.VMEM((16, FAR), BF16),
            pltpu.VMEM((15, LW, ROWS), BF16),
            pltpu.VMEM((LW, CHUNK), BF16),
            pltpu.VMEM((SEG, SEG), BF16),
            pltpu.VMEM((KX, CHUNK), BF16),
            pltpu.VMEM((KX, CHUNK), BF16),
            pltpu.VMEM((KX, CHUNK), BF16),
            pltpu.VMEM((CHUNK, KX), BF16),
            pltpu.VMEM((2 * LS, 512), BF16),
            pltpu.VMEM((2 * LS, 256), BF16),
            pltpu.VMEM((2 * LS, 128), BF16),
            pltpu.VMEM((2 * LS, 512), BF16),
            pltpu.VMEM((2, 2 * LS, 256), BF16),
            pltpu.VMEM((4, 2 * LS, 128), BF16),
            pltpu.VMEM((KX, CHUNK), F32),
            pltpu.VMEM((8, CHUNK), F32),
            pltpu.VMEM((16, LS, ROWS), BF16),
            pltpu.VMEM((16, LS, ROWS), BF16),
            pltpu.SemaphoreType.DMA((TILES_HERE,)),
            pltpu.SemaphoreType.DMA((6,)),
            pltpu.SemaphoreType.DMA((2, 104)),
        ],
        compiler_params=pltpu.CompilerParams(
            collective_id=0,
            has_side_effects=True,
            vmem_limit_bytes=60 * 1024 * 1024,
        ),
    )(*arguments)


def body(
    tile_tokens,
    vit_qkv,
    vit_out,
    tile_norm_gain,
    fresh_proj,
    tile_target,
    cached_rows,
    slide_tiles,
    head_shift,
    long_gain,
    long_qkv,
    long_out,
):
    vit_rows = jnp.transpose(vit_qkv, (1, 2, 3, 0)).reshape(VW, D)
    long_rows = jnp.transpose(long_qkv, (1, 2, 3, 0)).reshape(LH * LW, LD)
    return whole_layer(
        tile_tokens,
        vit_rows,
        vit_out,
        tile_norm_gain.reshape(D // 128, 128),
        fresh_proj,
        tile_target.reshape(1, 256),
        cached_rows,
        slide_tiles,
        head_shift,
        long_gain.reshape(LD // 128, 128),
        long_rows,
        long_out,
    )


def solution(mesh):
    placed = (
        P("dp", None, None),
        P(None, "tensor", None, None),
        P("tensor", None),
        P(),
        P(),
        P(),
        P(("dp", "tensor"), None),
        P(),
        P(),
        P(),
        P(),
        P(),
    )
    return jax.shard_map(
        body, mesh=mesh, in_specs=placed, out_specs=P(("dp", "tensor"), None), check_vma=False
    )
```

```python
import functools
import math

import jax
import jax.numpy as jnp
from jax import lax
from jax.experimental import pallas as pl
from jax.experimental.pallas import tpu as pltpu
from jax.sharding import PartitionSpec as P

MESH = pl.DeviceIdType.MESH
EPSILON = 1e-06
OUTSIDE = -1e30
LOG2E = 1.4426950408889634
NN = (((1,), (0,)), ((), ()))
NT = (((1,), (1,)), ((), ()))
TN = (((0,), (0,)), ((), ()))
F32 = jnp.float32
BF16 = jnp.bfloat16

TILES_HERE = 16
TOK = 256
D = 1536
VH_HERE = 3
VS = 64
VW = VH_HERE * 3 * VS
LD = 768
LH = 16
LS = 48
LW = 3 * LS
ROWS = 128
SEG = 1024
CHUNK = 2048
KX = 64
FAR = 1536
GROUP = 4
WIDE = GROUP * TOK
AHEAD = 4
VIT_SCALE = LOG2E / math.sqrt(VS)
LONG_SCALE = LOG2E / math.sqrt(LS)


def dot(a, b, dims=NN):
    return lax.dot_general(a, b, dims, preferred_element_type=F32)


def iota(shape, dim):
    return lax.broadcasted_iota(jnp.int32, shape, dim)


def split3(value):
    high = value.astype(BF16)
    rest = value - high.astype(F32)
    middle = rest.astype(BF16)
    low = (rest - middle.astype(F32)).astype(BF16)
    return high, middle, low


def normalize_rows(values):
    center = values - jnp.mean(values, axis=-1, keepdims=True)
    return center * lax.rsqrt(jnp.mean(center * center, axis=-1, keepdims=True) + EPSILON)


def whole_row(ref):
    rows = ref[...].astype(F32)
    return jnp.concatenate([rows[k : k + 1] for k in range(rows.shape[0])], axis=1)


def whole_kernel(
    tokens_hbm,
    vit_qkv_hbm,
    vit_out_hbm,
    tile_gain_ref,
    fresh_proj_hbm,
    target_ref,
    cached_hbm,
    slide_tiles_ref,
    head_shift_ref,
    long_gain_ref,
    long_qkv_hbm,
    long_out_hbm,
    out_ref,
    tokens,
    vit_qkv,
    csum,
    projected,
    attended,
    token_mean,
    vit_out,
    fresh_proj,
    cached,
    long_qkv,
    long_out,
    part,
    part_in,
    fresh_in,
    fresh_all,
    hidden,
    named_out,
    named_in,
    named_mid,
    named_all,
    same,
    lands,
    keep,
    far_marks,
    packed,
    qkv,
    perm,
    qx,
    kx,
    vx,
    keys_by_row,
    send2,
    send3,
    send4,
    got2,
    got3,
    got4,
    num,
    top,
    mix_out,
    mix_in,
    token_sem,
    load_sem,
    sems,
):
    d = lax.axis_index("dp")
    t = lax.axis_index("tensor")
    chunk = d // 2
    half = d % 2
    mine = half * 8 + t

    def remote(i, src, dst, device):
        return pltpu.make_async_remote_copy(
            src_ref=src,
            dst_ref=dst,
            send_sem=sems.at[0, i],
            recv_sem=sems.at[1, i],
            device_id=device,
            device_id_type=MESH,
        )

    half_lanes = pl.ds(pl.multiple_of(t % 2 * (LD // 2), LD // 2), LD // 2)

    def tile_rows(index):
        return pl.ds(pl.multiple_of(index * 16, 16), 16)

    def chunk_device(index):
        return 2 * chunk + index // 8, index % 8

    def named_copy(k):
        peer = (d + k) % 16
        return remote(
            0, named_out.at[tile_rows(peer)], named_in.at[tile_rows(d)], (peer, t)
        )

    def middle_copy(k):
        slot = named_mid.at[tile_rows(t)]
        return remote(1, slot, slot, (d, (t + k) % 8))

    def last_copy(k):
        slot = named_all.at[tile_rows(d)]
        return remote(2, slot, slot, ((d + k) % 16, t))

    def head_copy(k):
        lanes = pl.ds(pl.multiple_of(mine * ROWS, ROWS), ROWS)
        head = (mine + k) % 16
        return remote(3, packed.at[head], qkv.at[:, lanes], chunk_device(head))

    def far_copy(k):
        quad, inner = chunk // 4, chunk % 4
        if k == 0:
            return remote(9, send2, got2, (2 * (chunk + 1 - 2 * (chunk % 2)) + half, t))
        if k < 3:
            other = quad * 4 + (1 - inner // 2) * 2 + (inner % 2 + k - 1) % 2
            return remote(9 + k, send3, got3.at[k - 1], (2 * other + half, t))
        other = (1 - quad) * 4 + (inner + k - 3) % 4
        return remote(9 + k, send4, got4.at[k - 3], (2 * other + half, t))

    def reduce_copy(k):
        peer = (t + k) % 8
        return remote(4, part.at[peer], part_in.at[t], (d, peer))

    def gather_copy(k):
        return remote(5, fresh_in.at[t], fresh_in.at[t], (d, (t + k) % 8))

    def spread_copy(k):
        slot = fresh_all.at[tile_rows(d), half_lanes]
        return remote(6, slot, slot, ((d + k) % 16, t))

    def sibling_copy(k):
        slot = fresh_all.at[:, half_lanes]
        return remote(7, slot, slot, (d, t + 1 - 2 * (t % 2)))

    def mix_copy(k):
        device = (mine + k) % 16
        return remote(8, mix_out.at[device], mix_in.at[mine], chunk_device(device))

    whole = {
        named_copy: (0, named_out.at[0:240]),
        middle_copy: (1, named_mid.at[0:112]),
        last_copy: (2, named_all.at[0:240]),
        head_copy: (3, packed.at[0:15]),
        reduce_copy: (4, part.at[0:7]),
        gather_copy: (5, fresh_in.at[0:7]),
        spread_copy: (6, fresh_all.at[0:240, half_lanes]),
        sibling_copy: (7, fresh_all.at[:, half_lanes]),
        mix_copy: (8, mix_out.at[0:15]),
    }

    def every(copy, count, what):
        if what != "start" and copy in whole:
            i, total = whole[copy]
            getattr(remote(i, total, total, (d, (t + 1) % 8)), what)()
            return
        first = 0 if copy is far_copy else 1
        for k in range(first, first + count):
            getattr(copy(k), what)()

    barrier = pltpu.get_barrier_semaphore()
    for k in range(1, 8):
        pl.semaphore_signal(barrier, 1, device_id=(d, (t + k) % 8), device_id_type=MESH)
        pl.semaphore_signal(
            barrier, 1, device_id=(2 * chunk + 1 - half, (t + k) % 8), device_id_type=MESH
        )
    for k in range(1, 16):
        pl.semaphore_signal(barrier, 1, device_id=((d + k) % 16, t), device_id_type=MESH)

    vit_load = pltpu.make_async_copy(vit_qkv_hbm, vit_qkv.at[0:VW], load_sem.at[5])
    vit_load.start()
    loads = [
        pltpu.make_async_copy(src, dst, load_sem.at[i])
        for i, (src, dst) in enumerate(
            [
                (vit_out_hbm, vit_out),
                (fresh_proj_hbm, fresh_proj),
                (cached_hbm, cached),
                (long_qkv_hbm, long_qkv),
                (long_out_hbm, long_out),
            ]
        )
    ]
    loads[2].start()
    def token_load(i):
        return pltpu.make_async_copy(tokens_hbm.at[i], tokens.at[i], token_sem.at[i])

    for i in range(AHEAD):
        token_load(i).start()

    row = iota((16, D), 0)
    col = iota((16, D), 1)
    extra = jnp.where(row == 0, 1.0, jnp.where((row == 1) & (col == 0), 1.0, 0.0))
    vit_qkv[VW : VW + 16, :] = extra.astype(BF16)
    shift = head_shift_ref[mine] & 15
    end0 = slide_tiles_ref[0]
    end1 = end0 + slide_tiles_ref[1]
    end2 = end1 + slide_tiles_ref[2]

    def picked_rows(count, bits, which):
        lane = iota((1, count), 1)
        spot = lane & ((1 << bits) - 1)
        rank = spot >> 6
        turned = ((rank & 1) << 3) | ((rank & 2) << 1) | ((rank & 4) >> 1) | ((rank & 8) >> 3)
        inside = ((spot & 63) << 4) + ((turned + shift) & 15)
        return SEG * (2 * which + (lane >> bits)) + inside

    quad = chunk // 4
    inner = chunk % 4
    beside = chunk + 1 - 2 * (chunk % 2)
    across = [quad * 4 + (1 - inner // 2) * 2 + (inner % 2 + k) % 2 for k in range(2)]
    beyond = [(1 - quad) * 4 + (inner + 4 - k) % 4 for k in range(4)]
    every_row = jnp.concatenate(
        [picked_rows(CHUNK, 10, chunk), picked_rows(512, 8, beside)]
        + [picked_rows(256, 7, which) for which in across]
        + [picked_rows(128, 6, which) for which in beyond],
        axis=1,
    )
    perm[...] = jnp.where(
        iota((SEG, SEG), 0) == picked_rows(SEG, 10, 0), 1.0, 0.0
    ).astype(BF16)
    ids = (
        (every_row >= end0).astype(jnp.int32)
        + (every_row >= end1).astype(jnp.int32)
        + (every_row >= end2).astype(jnp.int32)
    )
    feature = iota((16, CHUNK + FAR), 0)
    own = ids[:, 0:CHUNK]
    qx[LS:KX, :] = jnp.where(own == feature[:, 0:CHUNK], 1.0, 0.0).astype(BF16)
    marks = jnp.where((feature < 4) & (ids != feature), OUTSIDE, 0.0).astype(BF16)
    kx[LS:KX, :] = marks[:, 0:CHUNK]
    far_marks[...] = marks[:, CHUNK:]

    def value_marks(count):
        return jnp.where(iota((16, count), 0) == 0, 1.0, 0.0).astype(BF16)

    vx[LS:KX, :] = value_marks(CHUNK)

    lane_target = target_ref[...]
    diagonal = iota((256, 256), 0) == iota((256, 256), 1)
    target = jnp.sum(
        jnp.where(diagonal, lane_target.astype(F32), 0.0), axis=1, keepdims=True
    ).astype(jnp.int32)
    equal = target == lane_target
    same[...] = jnp.where(equal, 1.0, 0.0).astype(BF16)
    earlier = jnp.where(equal & (iota((256, 256), 1) < iota((256, 256), 0)), 1.0, 0.0)
    leads = jnp.sum(earlier, axis=1, keepdims=True) < 0.5
    lands[...] = jnp.where(jnp.where(leads, target, -1) == every_row, 1.0, 0.0).astype(BF16)
    keep[...] = 1.0 - dot(jnp.ones((16, 256), BF16), lands[:, 0:CHUNK])[0:8]

    loads[2].wait()
    first_row = (d * 8 + t) * ROWS
    stored = cached[...]
    hidden[...] = (normalize_rows(stored.astype(F32)) * whole_row(long_gain_ref)).astype(BF16)
    mine_only = jnp.where(target - first_row == iota((256, ROWS), 1), 1.0, 0.0).astype(BF16)
    named_out[...] = dot(mine_only, stored).astype(BF16)
    pl.semaphore_wait(barrier, 29)
    every(named_copy, 15, "start")
    named_in[tile_rows(d)] = named_out[tile_rows(d)]

    def sum_over_dp():
        every(named_copy, 15, "wait_recv")
        total = sum(named_in[16 * k : 16 * k + 16].astype(F32) for k in range(16))
        named_mid[tile_rows(t)] = total.astype(BF16)
        every(middle_copy, 7, "start")

    def sum_over_tensor():
        every(middle_copy, 7, "wait_recv")
        total = sum(named_mid[16 * k : 16 * k + 16].astype(F32) for k in range(8))
        named_all[tile_rows(d)] = total.astype(BF16)
        every(last_copy, 15, "start")

    def send_heads():
        loads[3].wait()
        packed[...] = dot(long_qkv[...], hidden[...], NT).astype(BF16).reshape(LH, LW, ROWS)
        every(head_copy, 15, "start")
        qkv[:, pl.ds(pl.multiple_of(mine * ROWS, ROWS), ROWS)] = packed[mine]

    def sort_rows():
        every(head_copy, 15, "wait_recv")
        low_half = iota((LW, 128), 1) < 64
        stacked = jnp.concatenate([qkv[:, 0:SEG], qkv[:, SEG:CHUNK]], axis=0)
        stacked = dot(stacked, perm[...])
        sides = []
        for side in range(2):
            lanes = slice(side * SEG, (side + 1) * SEG)
            ordered = stacked[side * LW : (side + 1) * LW] * keep[0:1, lanes]
            sides.append(ordered[:, 0:128])
            ordered = ordered.astype(BF16)
            qx[0:LS, lanes] = ordered[0:LS]
            kx[0:LS, lanes] = ordered[LS : 2 * LS]
            vx[0:LS, lanes] = ordered[2 * LS : LW]
            send2[:, side * 256 : (side + 1) * 256] = ordered[LS:LW, 0:256]
            send3[:, side * 128 : (side + 1) * 128] = ordered[LS:LW, 0:128]
        both = jnp.where(low_half, sides[0], pltpu.roll(sides[1], 64, 1)).astype(BF16)
        send4[...] = both[LS:LW]
        every(far_copy, 7, "start")

    vit_load.wait()
    csum[...] = dot(vit_qkv[0:VW], jnp.ones((D, 128), BF16))

    def project(group):
        for i in range(GROUP):
            token_load(group * GROUP + i).wait()
        for i in range(GROUP):
            after = group * GROUP + i + AHEAD

            @pl.when(after < TILES_HERE)
            def _():
                token_load(after).start()

        @pl.when(group == 0)
        def _():
            loads[3].start()

        x = tokens[pl.ds(group * GROUP, GROUP)].reshape(WIDE, D)
        raw = dot(vit_qkv[...], x, NT)
        mean = raw[VW : VW + 1] * (1.0 / D)
        shift_row = mean - raw[VW + 1 : VW + 2]
        first = x[:, 0:1].astype(F32)
        squares = jnp.zeros((WIDE, 128), F32)
        for k in range(D // 128):
            delta = x[:, 128 * k : 128 * (k + 1)].astype(F32) - first
            squares = squares + delta * delta
        ones = jnp.ones((16, 128), BF16)
        total = sum(dot(ones, piece, NT) for piece in split3(squares))
        variance = jnp.maximum(total[0:1] * (1.0 / D) - shift_row * shift_row, 0.0)
        scale = lax.rsqrt(variance + EPSILON)
        spread = jnp.concatenate([csum[...]] * (WIDE // 128), axis=1)
        projected[...] = ((raw[0:VW] - spread * mean) * scale).astype(BF16)

    def attention(group):
        def piece(job, which):
            i, head = job
            first = (head * 3 + which) * VS
            return projected[first : first + VS, i * TOK : (i + 1) * TOK]

        jobs = [(i, head) for i in range(GROUP) for head in range(VH_HERE)]
        scores = [dot(piece(job, 1), piece(job, 0), TN) for job in jobs]
        highest = [jnp.max(score, axis=0, keepdims=True) for score in scores]
        weights = [
            jnp.exp2((score - high) * VIT_SCALE) for score, high in zip(scores, highest)
        ]
        sums = [jnp.sum(weight, axis=0, keepdims=True) for weight in weights]
        mixed = [dot(piece(job, 2), weight.astype(BF16)) for job, weight in zip(jobs, weights)]
        for (i, head), mixture, total in zip(jobs, mixed, sums):
            place = pl.ds(pl.multiple_of((group * GROUP + i) * TOK, TOK), TOK)
            attended[head * VS : (head + 1) * VS, place] = (mixture / total).astype(BF16)

    groups = TILES_HERE // GROUP

    def one_group(group, carry):
        project(group)
        attention(group)

        @pl.when(group == 0)
        def _():
            send_heads()
            sum_over_dp()

        @pl.when(group == 1)
        def _():
            sort_rows()
            sum_over_tensor()

        @pl.when(group == 2)
        def _():
            for i in (0, 1, 4):
                loads[i].start()

        return carry

    lax.fori_loop(0, groups, one_group, 0)
    for i in range(2):
        sums = dot(jnp.ones((16, TOK), BF16), tokens[2 * t + i])
        token_mean[i : i + 1, :] = sums[0:1] * (1.0 / TOK)
    tile_of = iota((TILES_HERE, TILES_HERE * TOK), 1) // TOK
    picks = jnp.where(iota(tile_of.shape, 0) == tile_of, 1.0 / TOK, 0.0).astype(BF16)
    pooled_term = dot(picks, attended[...], NT)

    loads[0].wait()
    partial = dot(jnp.concatenate(split3(pooled_term), axis=0), vit_out[...])
    partial = partial[0:16] + partial[16:32] + partial[32:48]
    for k in range(8):
        part[k] = partial[2 * k : 2 * k + 2]
    every(reduce_copy, 7, "start")
    part_in[pl.ds(t, 1)] = part[pl.ds(t, 1)]

    every(reduce_copy, 7, "wait_recv")
    pooled = token_mean[0:2, :]
    for k in range(8):
        pooled = pooled + part_in[k]
    normed = (normalize_rows(pooled) * whole_row(tile_gain_ref)).astype(BF16)
    loads[1].wait()
    fresh = dot(normed, fresh_proj[...])
    fresh_in[pl.ds(t, 1)] = fresh[None]
    every(gather_copy, 7, "start")
    every(gather_copy, 7, "wait_recv")
    group = jnp.concatenate([fresh_in[k] for k in range(8)], axis=0).astype(BF16)
    fresh_all[tile_rows(d), half_lanes] = jnp.where(
        t % 2 == 0, group[:, 0 : LD // 2], group[:, LD // 2 : LD]
    )
    every(spread_copy, 15, "start")
    every(last_copy, 15, "wait_recv")
    every(far_copy, 7, "wait_recv")
    every(spread_copy, 15, "wait_recv")
    every(sibling_copy, 1, "start")
    every(sibling_copy, 1, "wait_recv")

    changed = named_all[...].astype(F32) + dot(same[...], fresh_all[...])
    changed = (normalize_rows(changed) * whole_row(long_gain_ref)).astype(BF16)
    weight = long_qkv[pl.ds(pl.multiple_of(mine * LW, LW), LW), :]
    renewed = dot(weight, changed, NT).astype(BF16)

    def add(ref, rows, lanes, change):
        ref[rows, lanes] = (ref[rows, lanes].astype(F32) + change).astype(BF16)

    change = dot(renewed, lands[:, 0:CHUNK])
    everything = slice(0, CHUNK)
    add(qx, slice(0, LS), everything, change[0:LS])
    add(kx, slice(0, LS), everything, change[LS : 2 * LS])
    add(vx, slice(0, LS), everything, change[2 * LS : LW])
    far_change = dot(renewed[LS:LW], lands[:, CHUNK : CHUNK + FAR])
    for side in range(2):
        lanes = slice(side * SEG, (side + 1) * SEG)
        keys_by_row[lanes, :] = jnp.transpose(kx[:, lanes])

    def attend(jobs):
        scores = [dot(keys, queries) for keys, _, queries in jobs]
        highest = [jnp.max(score, axis=0, keepdims=True) for score in scores]
        weights = [
            jnp.exp2((score - high) * LONG_SCALE).astype(BF16)
            for score, high in zip(scores, highest)
        ]
        results = [dot(values, weight) for (_, values, _), weight in zip(jobs, weights)]
        return list(zip(results, highest))

    def merge(lanes, other_num, other_top):
        old_top = top[0:1, lanes]
        new_top = jnp.maximum(old_top, other_top)
        num[:, lanes] = num[:, lanes] * jnp.exp2(
            (old_top - new_top) * LONG_SCALE
        ) + other_num * jnp.exp2((other_top - new_top) * LONG_SCALE)
        top[0:1, lanes] = new_top

    def first_pair(i, carry):
        jobs = []
        spots = []
        for side in range(2):
            lanes = slice(side * SEG, (side + 1) * SEG)
            spot = pl.ds(pl.multiple_of(side * SEG + i * 512, 512), 512)
            jobs.append((keys_by_row[lanes, :], vx[:, lanes], qx[:, spot]))
            spots.append(spot)
        for spot, (result, highest) in zip(spots, attend(jobs)):
            num[:, spot] = result
            top[0:1, spot] = highest
        return carry

    lax.fori_loop(0, 2, first_pair, 0)

    def joined(ref, width):
        return jnp.concatenate([ref[:, 0:width], ref[:, SEG : SEG + width]], axis=1)

    def joined_rows(width):
        return [keys_by_row[0:width, :], keys_by_row[SEG : SEG + width, :]]

    keys = jnp.concatenate(joined_rows(512), axis=0)
    values = joined(vx, 512)
    jobs = [(keys, values, qx[:, side * SEG : side * SEG + 512]) for side in range(2)]

    def arrived(block, begin, count):
        place = slice(begin, begin + count)
        block = (block.astype(F32) + far_change[:, place]).astype(BF16)
        key = jnp.concatenate([block[0:LS], far_marks[:, place]], axis=0)
        value = jnp.concatenate([block[LS : 2 * LS], value_marks(count)], axis=0)
        return jnp.transpose(key), value

    key2, value2 = arrived(got2[...], 0, 512)
    keys = jnp.concatenate(joined_rows(256) + [key2], axis=0)
    values = jnp.concatenate([joined(vx, 256), value2], axis=1)
    jobs.append((keys, values, joined(qx, 256)))

    keys3 = joined_rows(128) + [key2[0:128], key2[256:384]]
    values3 = [joined(vx, 128), value2[:, 0:128], value2[:, 256:384]]
    for k in range(2):
        key, value = arrived(got3[k], 512 + 256 * k, 256)
        keys3 += [key[0:128], key[128:256]]
        values3.append(value)
    keys = jnp.concatenate(keys3, axis=0)
    values = jnp.concatenate(values3, axis=1)
    jobs.append((keys, values, joined(qx, 128)))

    lower = iota((KX, 128), 1) < 64

    def packed_pair(a, b):
        moved = pltpu.roll(b.astype(F32), 64, 1)
        return jnp.where(lower, a.astype(F32), moved).astype(BF16)

    keys4 = [key[0:64] for key in keys3]
    own = values3[0]
    values4 = [
        packed_pair(own[:, 0:128], own[:, 128:256]),
        packed_pair(values3[1], values3[2]),
    ]
    for far in values3[3:]:
        values4.append(packed_pair(far[:, 0:128], far[:, 128:256]))
    for k in range(4):
        key, value = arrived(got4[k], 1024 + 128 * k, 128)
        keys4.append(key)
        values4.append(value)
    keys = jnp.concatenate(keys4, axis=0)
    values = jnp.concatenate(values4, axis=1)
    query = packed_pair(qx[:, 0:128], qx[:, SEG : SEG + 128])
    jobs.append((keys, values, query))
    done = attend(jobs)
    for side in range(2):
        merge(slice(side * SEG, side * SEG + 512), *done[side])
    for (result, highest), width in ((done[2], 256), (done[3], 128)):
        for side in range(2):
            lanes = slice(side * width, (side + 1) * width)
            merge(
                slice(side * SEG, side * SEG + width), result[:, lanes], highest[:, lanes]
            )
    result, highest = done[4]
    highest = jnp.broadcast_to(highest, (8, 128))
    for side in range(2):
        if side == 1:
            result = pltpu.roll(result, 64, 1)
            highest = pltpu.roll(highest, 64, 1)
        lanes = slice(side * SEG, side * SEG + 128)
        merge(
            lanes,
            jnp.where(lower, result, 0.0),
            jnp.where(lower[0:1], highest[0:1], OUTSIDE),
        )

    blended = []
    for side in range(2):
        lanes = slice(side * SEG, (side + 1) * SEG)
        blended.append((num[0:LS, lanes] * (1.0 / num[LS : LS + 1, lanes])).astype(BF16))
    natural = dot(jnp.concatenate(blended, axis=0), perm[...], NT).astype(BF16)
    for side in range(2):
        for i in range(8):
            mix_out[side * 8 + i] = natural[
                side * LS : (side + 1) * LS, i * ROWS : (i + 1) * ROWS
            ]
    every(mix_copy, 15, "start")
    mix_in[pl.ds(mine, 1)] = mix_out[pl.ds(mine, 1)]
    match = (lane_target - first_row == iota((ROWS, 256), 0))
    match = jnp.where(match, 1.0, 0.0).astype(BF16)
    rows = cached[...].astype(F32) + dot(match, fresh_all[...])
    loads[4].wait()
    every(mix_copy, 15, "wait_recv")
    mixture = mix_in[...].reshape(LD, ROWS)
    out_ref[...] = (rows + dot(mixture, long_out[...], TN)).astype(BF16)

    for copy, count in (
        (named_copy, 15),
        (middle_copy, 7),
        (last_copy, 15),
        (head_copy, 15),
        (far_copy, 7),
        (reduce_copy, 7),
        (gather_copy, 7),
        (spread_copy, 15),
        (sibling_copy, 1),
        (mix_copy, 15),
    ):
        every(copy, count, "wait_send")


def whole_layer(*arguments):
    vmem = pl.BlockSpec(memory_space=pltpu.VMEM)
    smem = pl.BlockSpec(memory_space=pltpu.SMEM)
    hbm = pl.BlockSpec(memory_space=pl.ANY)
    return pl.pallas_call(
        whole_kernel,
        out_shape=jax.ShapeDtypeStruct((ROWS, LD), BF16),
        in_specs=[hbm, hbm, hbm, vmem, hbm, vmem, hbm, smem, smem, vmem, hbm, hbm],
        out_specs=vmem,
        scratch_shapes=[
            pltpu.VMEM((TILES_HERE, TOK, D), BF16),
            pltpu.VMEM((VW + 16, D), BF16),
            pltpu.VMEM((VW, 128), F32),
            pltpu.VMEM((VW, WIDE), BF16),
            pltpu.VMEM((VH_HERE * VS, TILES_HERE * TOK), BF16),
            pltpu.VMEM((8, D), F32),
            pltpu.VMEM((VH_HERE * VS, D), BF16),
            pltpu.VMEM((D, LD), BF16),
            pltpu.VMEM((ROWS, LD), BF16),
            pltpu.VMEM((LH * LW, LD), BF16),
            pltpu.VMEM((LD, LD), BF16),
            pltpu.VMEM((8, 2, D), F32),
            pltpu.VMEM((8, 2, D), F32),
            pltpu.VMEM((8, 2, LD), F32),
            pltpu.VMEM((256, LD), BF16),
            pltpu.VMEM((ROWS, LD), BF16),
            pltpu.VMEM((256, LD), BF16),
            pltpu.VMEM((256, LD), BF16),
            pltpu.VMEM((128, LD), BF16),
            pltpu.VMEM((256, LD), BF16),
            pltpu.VMEM((256, 256), BF16),
            pltpu.VMEM((256, CHUNK + FAR), BF16),
            pltpu.VMEM((8, CHUNK), F32),
            pltpu.VMEM((16, FAR), BF16),
            pltpu.VMEM((16, LW, ROWS), BF16),
            pltpu.VMEM((LW, CHUNK), BF16),
            pltpu.VMEM((SEG, SEG), BF16),
            pltpu.VMEM((KX, CHUNK), BF16),
            pltpu.VMEM((KX, CHUNK), BF16),
            pltpu.VMEM((KX, CHUNK), BF16),
            pltpu.VMEM((CHUNK, KX), BF16),
            pltpu.VMEM((2 * LS, 512), BF16),
            pltpu.VMEM((2 * LS, 256), BF16),
            pltpu.VMEM((2 * LS, 128), BF16),
            pltpu.VMEM((2 * LS, 512), BF16),
            pltpu.VMEM((2, 2 * LS, 256), BF16),
            pltpu.VMEM((4, 2 * LS, 128), BF16),
            pltpu.VMEM((KX, CHUNK), F32),
            pltpu.VMEM((8, CHUNK), F32),
            pltpu.VMEM((16, LS, ROWS), BF16),
            pltpu.VMEM((16, LS, ROWS), BF16),
            pltpu.SemaphoreType.DMA((TILES_HERE,)),
            pltpu.SemaphoreType.DMA((6,)),
            pltpu.SemaphoreType.DMA((2, 16)),
        ],
        compiler_params=pltpu.CompilerParams(
            collective_id=0,
            has_side_effects=True,
            vmem_limit_bytes=60 * 1024 * 1024,
        ),
    )(*arguments)


def body(
    tile_tokens,
    vit_qkv,
    vit_out,
    tile_norm_gain,
    fresh_proj,
    tile_target,
    cached_rows,
    slide_tiles,
    head_shift,
    long_gain,
    long_qkv,
    long_out,
):
    vit_rows = jnp.transpose(vit_qkv, (1, 2, 3, 0)).reshape(VW, D)
    long_rows = jnp.transpose(long_qkv, (1, 2, 3, 0)).reshape(LH * LW, LD)
    return whole_layer(
        tile_tokens,
        vit_rows,
        vit_out,
        tile_norm_gain.reshape(D // 128, 128),
        fresh_proj,
        tile_target.reshape(1, 256),
        cached_rows,
        slide_tiles,
        head_shift,
        long_gain.reshape(LD // 128, 128),
        long_rows,
        long_out,
    )


def solution(mesh):
    placed = (
        P("dp", None, None),
        P(None, "tensor", None, None),
        P("tensor", None),
        P(),
        P(),
        P(),
        P(("dp", "tensor"), None),
        P(),
        P(),
        P(),
        P(),
        P(),
    )
    return jax.shard_map(
        body, mesh=mesh, in_specs=placed, out_specs=P(("dp", "tensor"), None), check_vma=False
    )
```

```python
import functools
import math

import jax
import jax.numpy as jnp
from jax import lax
from jax.experimental import pallas as pl
from jax.experimental.pallas import tpu as pltpu
from jax.sharding import PartitionSpec as P

MESH = pl.DeviceIdType.MESH
EPSILON = 1e-06
OUTSIDE = -1e30
LOG2E = 1.4426950408889634
NN = (((1,), (0,)), ((), ()))
NT = (((1,), (1,)), ((), ()))
TN = (((0,), (0,)), ((), ()))
F32 = jnp.float32
BF16 = jnp.bfloat16

TILES_HERE = 16
TOK = 256
D = 1536
VH_HERE = 3
VS = 64
VW = VH_HERE * 3 * VS
LD = 768
LH = 16
LS = 48
LW = 3 * LS
ROWS = 128
SEG = 1024
CHUNK = 2048
KX = 64
FAR = 1536
GROUP = 4
WIDE = GROUP * TOK
AHEAD = 4
VIT_SCALE = LOG2E / math.sqrt(VS)
LONG_SCALE = LOG2E / math.sqrt(LS)


def dot(a, b, dims=NN):
    return lax.dot_general(a, b, dims, preferred_element_type=F32)


def iota(shape, dim):
    return lax.broadcasted_iota(jnp.int32, shape, dim)


def split3(value):
    high = value.astype(BF16)
    rest = value - high.astype(F32)
    middle = rest.astype(BF16)
    low = (rest - middle.astype(F32)).astype(BF16)
    return high, middle, low


def normalize_rows(values):
    center = values - jnp.mean(values, axis=-1, keepdims=True)
    return center * lax.rsqrt(jnp.mean(center * center, axis=-1, keepdims=True) + EPSILON)


def whole_row(ref):
    rows = ref[...].astype(F32)
    return jnp.concatenate([rows[k : k + 1] for k in range(rows.shape[0])], axis=1)


def whole_kernel(
    tokens_hbm,
    vit_qkv_hbm,
    vit_out_hbm,
    tile_gain_ref,
    fresh_proj_hbm,
    target_ref,
    cached_hbm,
    slide_tiles_ref,
    head_shift_ref,
    long_gain_ref,
    long_qkv_hbm,
    long_out_hbm,
    out_ref,
    tokens,
    vit_qkv,
    csum,
    projected,
    attended,
    token_mean,
    vit_out,
    fresh_proj,
    cached,
    long_qkv,
    long_out,
    part,
    part_in,
    fresh_in,
    fresh_all,
    hidden,
    named_out,
    named_in,
    named_mid,
    named_all,
    same,
    lands,
    keep,
    far_marks,
    packed,
    qkv,
    perm,
    qx,
    kx,
    vx,
    keys_by_row,
    send2,
    send3,
    send4,
    got2,
    got3,
    got4,
    num,
    top,
    mix_out,
    mix_in,
    token_sem,
    load_sem,
    sems,
):
    d = lax.axis_index("dp")
    t = lax.axis_index("tensor")
    chunk = d // 2
    half = d % 2
    mine = half * 8 + t

    def remote(i, src, dst, device):
        return pltpu.make_async_remote_copy(
            src_ref=src,
            dst_ref=dst,
            send_sem=sems.at[0, i],
            recv_sem=sems.at[1, i],
            device_id=device,
            device_id_type=MESH,
        )

    half_lanes = pl.ds(pl.multiple_of(t % 2 * (LD // 2), LD // 2), LD // 2)

    def tile_rows(index):
        return pl.ds(pl.multiple_of(index * 16, 16), 16)

    def chunk_device(index):
        return 2 * chunk + index // 8, index % 8

    def named_copy(k):
        peer = (d + k) % 16
        return remote(
            0, named_out.at[tile_rows(peer)], named_in.at[tile_rows(d)], (peer, t)
        )

    def middle_copy(k):
        slot = named_mid.at[tile_rows(t)]
        return remote(1, slot, slot, (d, (t + k) % 8))

    def last_copy(k):
        slot = named_all.at[tile_rows(d)]
        return remote(2, slot, slot, ((d + k) % 16, t))

    def head_copy(k):
        lanes = pl.ds(pl.multiple_of(mine * ROWS, ROWS), ROWS)
        head = (mine + k) % 16
        return remote(3, packed.at[head], qkv.at[:, lanes], chunk_device(head))

    def far_copy(k):
        quad, inner = chunk // 4, chunk % 4
        if k == 0:
            return remote(9, send2, got2, (2 * (chunk + 1 - 2 * (chunk % 2)) + half, t))
        if k < 3:
            other = quad * 4 + (1 - inner // 2) * 2 + (inner % 2 + k - 1) % 2
            return remote(9 + k, send3, got3.at[k - 1], (2 * other + half, t))
        other = (1 - quad) * 4 + (inner + k - 3) % 4
        return remote(9 + k, send4, got4.at[k - 3], (2 * other + half, t))

    def reduce_copy(k):
        peer = (t + k) % 8
        return remote(4, part.at[peer], part_in.at[t], (d, peer))

    def gather_copy(k):
        return remote(5, fresh_in.at[t], fresh_in.at[t], (d, (t + k) % 8))

    def spread_copy(k):
        slot = fresh_all.at[tile_rows(d), half_lanes]
        return remote(6, slot, slot, ((d + k) % 16, t))

    def sibling_copy(k):
        slot = fresh_all.at[:, half_lanes]
        return remote(7, slot, slot, (d, t + 1 - 2 * (t % 2)))

    def mix_copy(k):
        device = (mine + k) % 16
        return remote(8, mix_out.at[device], mix_in.at[mine], chunk_device(device))

    whole = {
        named_copy: (0, named_out.at[0:240]),
        middle_copy: (1, named_mid.at[0:112]),
        last_copy: (2, named_all.at[0:240]),
        head_copy: (3, packed.at[0:15]),
        reduce_copy: (4, part.at[0:7]),
        gather_copy: (5, fresh_in.at[0:7]),
        spread_copy: (6, fresh_all.at[0:240, half_lanes]),
        sibling_copy: (7, fresh_all.at[:, half_lanes]),
        mix_copy: (8, mix_out.at[0:15]),
    }

    def every(copy, count, what):
        if what != "start" and copy in whole:
            i, total = whole[copy]
            getattr(remote(i, total, total, (d, (t + 1) % 8)), what)()
            return
        first = 0 if copy is far_copy else 1
        for k in range(first, first + count):
            getattr(copy(k), what)()

    barrier = pltpu.get_barrier_semaphore()
    for k in range(1, 8):
        pl.semaphore_signal(barrier, 1, device_id=(d, (t + k) % 8), device_id_type=MESH)
        pl.semaphore_signal(
            barrier, 1, device_id=(2 * chunk + 1 - half, (t + k) % 8), device_id_type=MESH
        )
    for k in range(1, 16):
        pl.semaphore_signal(barrier, 1, device_id=((d + k) % 16, t), device_id_type=MESH)

    vit_load = pltpu.make_async_copy(vit_qkv_hbm, vit_qkv.at[0:VW], load_sem.at[5])
    vit_load.start()
    loads = [
        pltpu.make_async_copy(src, dst, load_sem.at[i])
        for i, (src, dst) in enumerate(
            [
                (vit_out_hbm, vit_out),
                (fresh_proj_hbm, fresh_proj),
                (cached_hbm, cached),
                (long_qkv_hbm, long_qkv),
                (long_out_hbm, long_out),
            ]
        )
    ]
    loads[2].start()
    def token_load(i):
        return pltpu.make_async_copy(tokens_hbm.at[i], tokens.at[i], token_sem.at[i])

    for i in range(AHEAD):
        token_load(i).start()

    row = iota((16, D), 0)
    col = iota((16, D), 1)
    extra = jnp.where(row == 0, 1.0, jnp.where((row == 1) & (col == 0), 1.0, 0.0))
    vit_qkv[VW : VW + 16, :] = extra.astype(BF16)
    shift = head_shift_ref[mine] & 15
    end0 = slide_tiles_ref[0]
    end1 = end0 + slide_tiles_ref[1]
    end2 = end1 + slide_tiles_ref[2]

    def picked_rows(count, bits, which):
        lane = iota((1, count), 1)
        spot = lane & ((1 << bits) - 1)
        rank = spot >> 6
        turned = ((rank & 1) << 3) | ((rank & 2) << 1) | ((rank & 4) >> 1) | ((rank & 8) >> 3)
        inside = ((spot & 63) << 4) + ((turned + shift) & 15)
        return SEG * (2 * which + (lane >> bits)) + inside

    quad = chunk // 4
    inner = chunk % 4
    beside = chunk + 1 - 2 * (chunk % 2)
    across = [quad * 4 + (1 - inner // 2) * 2 + (inner % 2 + k) % 2 for k in range(2)]
    beyond = [(1 - quad) * 4 + (inner + 4 - k) % 4 for k in range(4)]
    every_row = jnp.concatenate(
        [picked_rows(CHUNK, 10, chunk), picked_rows(512, 8, beside)]
        + [picked_rows(256, 7, which) for which in across]
        + [picked_rows(128, 6, which) for which in beyond],
        axis=1,
    )
    perm[...] = jnp.where(
        iota((SEG, SEG), 0) == picked_rows(SEG, 10, 0), 1.0, 0.0
    ).astype(BF16)
    ids = (
        (every_row >= end0).astype(jnp.int32)
        + (every_row >= end1).astype(jnp.int32)
        + (every_row >= end2).astype(jnp.int32)
    )
    feature = iota((16, CHUNK + FAR), 0)
    own = ids[:, 0:CHUNK]
    qx[LS:KX, :] = jnp.where(own == feature[:, 0:CHUNK], 1.0, 0.0).astype(BF16)
    marks = jnp.where((feature < 4) & (ids != feature), OUTSIDE, 0.0).astype(BF16)
    kx[LS:KX, :] = marks[:, 0:CHUNK]
    far_marks[...] = marks[:, CHUNK:]

    def value_marks(count):
        return jnp.where(iota((16, count), 0) == 0, 1.0, 0.0).astype(BF16)

    vx[LS:KX, :] = value_marks(CHUNK)

    lane_target = target_ref[...]
    diagonal = iota((256, 256), 0) == iota((256, 256), 1)
    target = jnp.sum(
        jnp.where(diagonal, lane_target.astype(F32), 0.0), axis=1, keepdims=True
    ).astype(jnp.int32)
    equal = target == lane_target
    same[...] = jnp.where(equal, 1.0, 0.0).astype(BF16)
    earlier = jnp.where(equal & (iota((256, 256), 1) < iota((256, 256), 0)), 1.0, 0.0)
    leads = jnp.sum(earlier, axis=1, keepdims=True) < 0.5
    lands[...] = jnp.where(jnp.where(leads, target, -1) == every_row, 1.0, 0.0).astype(BF16)
    keep[...] = 1.0 - dot(jnp.ones((16, 256), BF16), lands[:, 0:CHUNK])[0:8]

    loads[2].wait()
    first_row = (d * 8 + t) * ROWS
    stored = cached[...]
    hidden[...] = (normalize_rows(stored.astype(F32)) * whole_row(long_gain_ref)).astype(BF16)
    mine_only = jnp.where(target - first_row == iota((256, ROWS), 1), 1.0, 0.0).astype(BF16)
    named_out[...] = dot(mine_only, stored).astype(BF16)
    pl.semaphore_wait(barrier, 29)
    every(named_copy, 15, "start")
    named_in[tile_rows(d)] = named_out[tile_rows(d)]

    def sum_over_dp():
        every(named_copy, 15, "wait_recv")
        total = sum(named_in[16 * k : 16 * k + 16].astype(F32) for k in range(16))
        named_mid[tile_rows(t)] = total.astype(BF16)
        every(middle_copy, 7, "start")

    def sum_over_tensor():
        every(middle_copy, 7, "wait_recv")
        total = sum(named_mid[16 * k : 16 * k + 16].astype(F32) for k in range(8))
        named_all[tile_rows(d)] = total.astype(BF16)
        every(last_copy, 15, "start")

    def send_heads():
        loads[3].wait()
        packed[...] = dot(long_qkv[...], hidden[...], NT).astype(BF16).reshape(LH, LW, ROWS)
        every(head_copy, 15, "start")
        qkv[:, pl.ds(pl.multiple_of(mine * ROWS, ROWS), ROWS)] = packed[mine]

    def sort_rows():
        every(head_copy, 15, "wait_recv")
        low_half = iota((LW, 128), 1) < 64
        stacked = jnp.concatenate([qkv[:, 0:SEG], qkv[:, SEG:CHUNK]], axis=0)
        stacked = dot(stacked, perm[...])
        sides = []
        for side in range(2):
            lanes = slice(side * SEG, (side + 1) * SEG)
            ordered = stacked[side * LW : (side + 1) * LW] * keep[0:1, lanes]
            sides.append(ordered[:, 0:128])
            ordered = ordered.astype(BF16)
            qx[0:LS, lanes] = ordered[0:LS]
            kx[0:LS, lanes] = ordered[LS : 2 * LS]
            vx[0:LS, lanes] = ordered[2 * LS : LW]
            send2[:, side * 256 : (side + 1) * 256] = ordered[LS:LW, 0:256]
            send3[:, side * 128 : (side + 1) * 128] = ordered[LS:LW, 0:128]
        both = jnp.where(low_half, sides[0], pltpu.roll(sides[1], 64, 1)).astype(BF16)
        send4[...] = both[LS:LW]
        every(far_copy, 7, "start")

    vit_load.wait()
    csum[...] = dot(vit_qkv[0:VW], jnp.ones((D, 128), BF16))

    def project(group):
        for i in range(GROUP):
            token_load(group * GROUP + i).wait()
        for i in range(GROUP):
            after = group * GROUP + i + AHEAD

            @pl.when(after < TILES_HERE)
            def _():
                token_load(after).start()

        @pl.when(group == 0)
        def _():
            loads[3].start()

        x = tokens[pl.ds(group * GROUP, GROUP)].reshape(WIDE, D)
        raw = dot(vit_qkv[...], x, NT)
        mean = raw[VW : VW + 1] * (1.0 / D)
        shift_row = mean - raw[VW + 1 : VW + 2]
        first = x[:, 0:1].astype(F32)
        squares = jnp.zeros((WIDE, 128), F32)
        for k in range(D // 128):
            delta = x[:, 128 * k : 128 * (k + 1)].astype(F32) - first
            squares = squares + delta * delta
        ones = jnp.ones((16, 128), BF16)
        total = sum(dot(ones, piece, NT) for piece in split3(squares))
        variance = jnp.maximum(total[0:1] * (1.0 / D) - shift_row * shift_row, 0.0)
        scale = lax.rsqrt(variance + EPSILON)
        spread = jnp.concatenate([csum[...]] * (WIDE // 128), axis=1)
        projected[...] = ((raw[0:VW] - spread * mean) * scale).astype(BF16)

    def attention(group):
        def piece(job, which):
            i, head = job
            first = (head * 3 + which) * VS
            return projected[first : first + VS, i * TOK : (i + 1) * TOK]

        jobs = [(i, head) for i in range(GROUP) for head in range(VH_HERE)]
        scores = [dot(piece(job, 1), piece(job, 0), TN) for job in jobs]
        highest = [jnp.max(score, axis=0, keepdims=True) for score in scores]
        weights = [
            jnp.exp2((score - high) * VIT_SCALE) for score, high in zip(scores, highest)
        ]
        sums = [jnp.sum(weight, axis=0, keepdims=True) for weight in weights]
        mixed = [dot(piece(job, 2), weight.astype(BF16)) for job, weight in zip(jobs, weights)]
        for (i, head), mixture, total in zip(jobs, mixed, sums):
            place = pl.ds(pl.multiple_of((group * GROUP + i) * TOK, TOK), TOK)
            attended[head * VS : (head + 1) * VS, place] = (mixture / total).astype(BF16)

    groups = TILES_HERE // GROUP

    def one_group(group, carry):
        project(group)
        attention(group)

        @pl.when(group == 0)
        def _():
            send_heads()
            sum_over_dp()

        @pl.when(group == 1)
        def _():
            sum_over_tensor()
            for i in (0, 1, 4):
                loads[i].start()

        @pl.when(group == 2)
        def _():
            sort_rows()

        return carry

    lax.fori_loop(0, groups, one_group, 0)
    for i in range(2):
        sums = dot(jnp.ones((16, TOK), BF16), tokens[2 * t + i])
        token_mean[i : i + 1, :] = sums[0:1] * (1.0 / TOK)
    tile_of = iota((TILES_HERE, TILES_HERE * TOK), 1) // TOK
    picks = jnp.where(iota(tile_of.shape, 0) == tile_of, 1.0 / TOK, 0.0).astype(BF16)
    pooled_term = dot(picks, attended[...], NT)

    loads[0].wait()
    partial = dot(jnp.concatenate(split3(pooled_term), axis=0), vit_out[...])
    partial = partial[0:16] + partial[16:32] + partial[32:48]
    for k in range(8):
        part[k] = partial[2 * k : 2 * k + 2]
    every(reduce_copy, 7, "start")
    part_in[pl.ds(t, 1)] = part[pl.ds(t, 1)]

    every(reduce_copy, 7, "wait_recv")
    pooled = token_mean[0:2, :]
    for k in range(8):
        pooled = pooled + part_in[k]
    normed = (normalize_rows(pooled) * whole_row(tile_gain_ref)).astype(BF16)
    loads[1].wait()
    fresh = dot(normed, fresh_proj[...])
    fresh_in[pl.ds(t, 1)] = fresh[None]
    every(gather_copy, 7, "start")
    every(gather_copy, 7, "wait_recv")
    group = jnp.concatenate([fresh_in[k] for k in range(8)], axis=0).astype(BF16)
    fresh_all[tile_rows(d), half_lanes] = jnp.where(
        t % 2 == 0, group[:, 0 : LD // 2], group[:, LD // 2 : LD]
    )
    every(spread_copy, 15, "start")
    every(last_copy, 15, "wait_recv")
    every(far_copy, 7, "wait_recv")
    every(spread_copy, 15, "wait_recv")
    every(sibling_copy, 1, "start")
    every(sibling_copy, 1, "wait_recv")

    changed = named_all[...].astype(F32) + dot(same[...], fresh_all[...])
    changed = (normalize_rows(changed) * whole_row(long_gain_ref)).astype(BF16)
    weight = long_qkv[pl.ds(pl.multiple_of(mine * LW, LW), LW), :]
    renewed = dot(weight, changed, NT).astype(BF16)

    def add(ref, rows, lanes, change):
        ref[rows, lanes] = (ref[rows, lanes].astype(F32) + change).astype(BF16)

    change = dot(renewed, lands[:, 0:CHUNK])
    everything = slice(0, CHUNK)
    add(qx, slice(0, LS), everything, change[0:LS])
    add(kx, slice(0, LS), everything, change[LS : 2 * LS])
    add(vx, slice(0, LS), everything, change[2 * LS : LW])
    far_change = dot(renewed[LS:LW], lands[:, CHUNK : CHUNK + FAR])
    for side in range(2):
        lanes = slice(side * SEG, (side + 1) * SEG)
        keys_by_row[lanes, :] = jnp.transpose(kx[:, lanes])

    def attend(jobs):
        scores = [dot(keys, queries) for keys, _, queries in jobs]
        highest = [jnp.max(score, axis=0, keepdims=True) for score in scores]
        weights = [
            jnp.exp2((score - high) * LONG_SCALE).astype(BF16)
            for score, high in zip(scores, highest)
        ]
        results = [dot(values, weight) for (_, values, _), weight in zip(jobs, weights)]
        return list(zip(results, highest))

    def merge(lanes, other_num, other_top):
        old_top = top[0:1, lanes]
        new_top = jnp.maximum(old_top, other_top)
        num[:, lanes] = num[:, lanes] * jnp.exp2(
            (old_top - new_top) * LONG_SCALE
        ) + other_num * jnp.exp2((other_top - new_top) * LONG_SCALE)
        top[0:1, lanes] = new_top

    def first_pair(i, carry):
        jobs = []
        spots = []
        for side in range(2):
            lanes = slice(side * SEG, (side + 1) * SEG)
            spot = pl.ds(pl.multiple_of(side * SEG + i * 512, 512), 512)
            jobs.append((keys_by_row[lanes, :], vx[:, lanes], qx[:, spot]))
            spots.append(spot)
        for spot, (result, highest) in zip(spots, attend(jobs)):
            num[:, spot] = result
            top[0:1, spot] = highest
        return carry

    lax.fori_loop(0, 2, first_pair, 0)

    def joined(ref, width):
        return jnp.concatenate([ref[:, 0:width], ref[:, SEG : SEG + width]], axis=1)

    def joined_rows(width):
        return [keys_by_row[0:width, :], keys_by_row[SEG : SEG + width, :]]

    keys = jnp.concatenate(joined_rows(512), axis=0)
    values = joined(vx, 512)
    jobs = [(keys, values, qx[:, side * SEG : side * SEG + 512]) for side in range(2)]

    def arrived(block, begin, count):
        place = slice(begin, begin + count)
        block = (block.astype(F32) + far_change[:, place]).astype(BF16)
        key = jnp.concatenate([block[0:LS], far_marks[:, place]], axis=0)
        value = jnp.concatenate([block[LS : 2 * LS], value_marks(count)], axis=0)
        return jnp.transpose(key), value

    key2, value2 = arrived(got2[...], 0, 512)
    keys = jnp.concatenate(joined_rows(256) + [key2], axis=0)
    values = jnp.concatenate([joined(vx, 256), value2], axis=1)
    jobs.append((keys, values, joined(qx, 256)))

    keys3 = joined_rows(128) + [key2[0:128], key2[256:384]]
    values3 = [joined(vx, 128), value2[:, 0:128], value2[:, 256:384]]
    for k in range(2):
        key, value = arrived(got3[k], 512 + 256 * k, 256)
        keys3 += [key[0:128], key[128:256]]
        values3.append(value)
    keys = jnp.concatenate(keys3, axis=0)
    values = jnp.concatenate(values3, axis=1)
    jobs.append((keys, values, joined(qx, 128)))

    lower = iota((KX, 128), 1) < 64

    def packed_pair(a, b):
        moved = pltpu.roll(b.astype(F32), 64, 1)
        return jnp.where(lower, a.astype(F32), moved).astype(BF16)

    keys4 = [key[0:64] for key in keys3]
    own = values3[0]
    values4 = [
        packed_pair(own[:, 0:128], own[:, 128:256]),
        packed_pair(values3[1], values3[2]),
    ]
    for far in values3[3:]:
        values4.append(packed_pair(far[:, 0:128], far[:, 128:256]))
    for k in range(4):
        key, value = arrived(got4[k], 1024 + 128 * k, 128)
        keys4.append(key)
        values4.append(value)
    keys = jnp.concatenate(keys4, axis=0)
    values = jnp.concatenate(values4, axis=1)
    query = packed_pair(qx[:, 0:128], qx[:, SEG : SEG + 128])
    jobs.append((keys, values, query))
    done = attend(jobs)
    for side in range(2):
        merge(slice(side * SEG, side * SEG + 512), *done[side])
    for (result, highest), width in ((done[2], 256), (done[3], 128)):
        for side in range(2):
            lanes = slice(side * width, (side + 1) * width)
            merge(
                slice(side * SEG, side * SEG + width), result[:, lanes], highest[:, lanes]
            )
    result, highest = done[4]
    highest = jnp.broadcast_to(highest, (8, 128))
    for side in range(2):
        if side == 1:
            result = pltpu.roll(result, 64, 1)
            highest = pltpu.roll(highest, 64, 1)
        lanes = slice(side * SEG, side * SEG + 128)
        merge(
            lanes,
            jnp.where(lower, result, 0.0),
            jnp.where(lower[0:1], highest[0:1], OUTSIDE),
        )

    blended = []
    for side in range(2):
        lanes = slice(side * SEG, (side + 1) * SEG)
        blended.append((num[0:LS, lanes] * (1.0 / num[LS : LS + 1, lanes])).astype(BF16))
    natural = dot(jnp.concatenate(blended, axis=0), perm[...], NT).astype(BF16)
    for side in range(2):
        for i in range(8):
            mix_out[side * 8 + i] = natural[
                side * LS : (side + 1) * LS, i * ROWS : (i + 1) * ROWS
            ]
    every(mix_copy, 15, "start")
    mix_in[pl.ds(mine, 1)] = mix_out[pl.ds(mine, 1)]
    match = (lane_target - first_row == iota((ROWS, 256), 0))
    match = jnp.where(match, 1.0, 0.0).astype(BF16)
    rows = cached[...].astype(F32) + dot(match, fresh_all[...])
    loads[4].wait()
    every(mix_copy, 15, "wait_recv")
    mixture = mix_in[...].reshape(LD, ROWS)
    out_ref[...] = (rows + dot(mixture, long_out[...], TN)).astype(BF16)

    for copy, count in (
        (named_copy, 15),
        (middle_copy, 7),
        (last_copy, 15),
        (head_copy, 15),
        (far_copy, 7),
        (reduce_copy, 7),
        (gather_copy, 7),
        (spread_copy, 15),
        (sibling_copy, 1),
        (mix_copy, 15),
    ):
        every(copy, count, "wait_send")


def whole_layer(*arguments):
    vmem = pl.BlockSpec(memory_space=pltpu.VMEM)
    smem = pl.BlockSpec(memory_space=pltpu.SMEM)
    hbm = pl.BlockSpec(memory_space=pl.ANY)
    return pl.pallas_call(
        whole_kernel,
        out_shape=jax.ShapeDtypeStruct((ROWS, LD), BF16),
        in_specs=[hbm, hbm, hbm, vmem, hbm, vmem, hbm, smem, smem, vmem, hbm, hbm],
        out_specs=vmem,
        scratch_shapes=[
            pltpu.VMEM((TILES_HERE, TOK, D), BF16),
            pltpu.VMEM((VW + 16, D), BF16),
            pltpu.VMEM((VW, 128), F32),
            pltpu.VMEM((VW, WIDE), BF16),
            pltpu.VMEM((VH_HERE * VS, TILES_HERE * TOK), BF16),
            pltpu.VMEM((8, D), F32),
            pltpu.VMEM((VH_HERE * VS, D), BF16),
            pltpu.VMEM((D, LD), BF16),
            pltpu.VMEM((ROWS, LD), BF16),
            pltpu.VMEM((LH * LW, LD), BF16),
            pltpu.VMEM((LD, LD), BF16),
            pltpu.VMEM((8, 2, D), F32),
            pltpu.VMEM((8, 2, D), F32),
            pltpu.VMEM((8, 2, LD), F32),
            pltpu.VMEM((256, LD), BF16),
            pltpu.VMEM((ROWS, LD), BF16),
            pltpu.VMEM((256, LD), BF16),
            pltpu.VMEM((256, LD), BF16),
            pltpu.VMEM((128, LD), BF16),
            pltpu.VMEM((256, LD), BF16),
            pltpu.VMEM((256, 256), BF16),
            pltpu.VMEM((256, CHUNK + FAR), BF16),
            pltpu.VMEM((8, CHUNK), F32),
            pltpu.VMEM((16, FAR), BF16),
            pltpu.VMEM((16, LW, ROWS), BF16),
            pltpu.VMEM((LW, CHUNK), BF16),
            pltpu.VMEM((SEG, SEG), BF16),
            pltpu.VMEM((KX, CHUNK), BF16),
            pltpu.VMEM((KX, CHUNK), BF16),
            pltpu.VMEM((KX, CHUNK), BF16),
            pltpu.VMEM((CHUNK, KX), BF16),
            pltpu.VMEM((2 * LS, 512), BF16),
            pltpu.VMEM((2 * LS, 256), BF16),
            pltpu.VMEM((2 * LS, 128), BF16),
            pltpu.VMEM((2 * LS, 512), BF16),
            pltpu.VMEM((2, 2 * LS, 256), BF16),
            pltpu.VMEM((4, 2 * LS, 128), BF16),
            pltpu.VMEM((KX, CHUNK), F32),
            pltpu.VMEM((8, CHUNK), F32),
            pltpu.VMEM((16, LS, ROWS), BF16),
            pltpu.VMEM((16, LS, ROWS), BF16),
            pltpu.SemaphoreType.DMA((TILES_HERE,)),
            pltpu.SemaphoreType.DMA((6,)),
            pltpu.SemaphoreType.DMA((2, 16)),
        ],
        compiler_params=pltpu.CompilerParams(
            collective_id=0,
            has_side_effects=True,
            vmem_limit_bytes=60 * 1024 * 1024,
        ),
    )(*arguments)


def body(
    tile_tokens,
    vit_qkv,
    vit_out,
    tile_norm_gain,
    fresh_proj,
    tile_target,
    cached_rows,
    slide_tiles,
    head_shift,
    long_gain,
    long_qkv,
    long_out,
):
    vit_rows = jnp.transpose(vit_qkv, (1, 2, 3, 0)).reshape(VW, D)
    long_rows = jnp.transpose(long_qkv, (1, 2, 3, 0)).reshape(LH * LW, LD)
    return whole_layer(
        tile_tokens,
        vit_rows,
        vit_out,
        tile_norm_gain.reshape(D // 128, 128),
        fresh_proj,
        tile_target.reshape(1, 256),
        cached_rows,
        slide_tiles,
        head_shift,
        long_gain.reshape(LD // 128, 128),
        long_rows,
        long_out,
    )


def solution(mesh):
    placed = (
        P("dp", None, None),
        P(None, "tensor", None, None),
        P("tensor", None),
        P(),
        P(),
        P(),
        P(("dp", "tensor"), None),
        P(),
        P(),
        P(),
        P(),
        P(),
    )
    return jax.shard_map(
        body, mesh=mesh, in_specs=placed, out_specs=P(("dp", "tensor"), None), check_vma=False
    )
```

```python
import functools
import math

import jax
import jax.numpy as jnp
from jax import lax
from jax.experimental import pallas as pl
from jax.experimental.pallas import tpu as pltpu
from jax.sharding import PartitionSpec as P

MESH = pl.DeviceIdType.MESH
EPSILON = 1e-06
OUTSIDE = -1e30
LOG2E = 1.4426950408889634
NN = (((1,), (0,)), ((), ()))
NT = (((1,), (1,)), ((), ()))
TN = (((0,), (0,)), ((), ()))
F32 = jnp.float32
BF16 = jnp.bfloat16

TILES_HERE = 16
TOK = 256
D = 1536
VH_HERE = 3
VS = 64
VW = VH_HERE * 3 * VS
LD = 768
LH = 16
LS = 48
LW = 3 * LS
ROWS = 128
SEG = 1024
CHUNK = 2048
KX = 64
FAR = 1536
GROUP = 4
WIDE = GROUP * TOK
AHEAD = 4
VIT_SCALE = LOG2E / math.sqrt(VS)
LONG_SCALE = LOG2E / math.sqrt(LS)


def dot(a, b, dims=NN):
    return lax.dot_general(a, b, dims, preferred_element_type=F32)


def iota(shape, dim):
    return lax.broadcasted_iota(jnp.int32, shape, dim)


def split3(value):
    high = value.astype(BF16)
    rest = value - high.astype(F32)
    middle = rest.astype(BF16)
    low = (rest - middle.astype(F32)).astype(BF16)
    return high, middle, low


def normalize_rows(values):
    center = values - jnp.mean(values, axis=-1, keepdims=True)
    return center * lax.rsqrt(jnp.mean(center * center, axis=-1, keepdims=True) + EPSILON)


def whole_row(ref):
    rows = ref[...].astype(F32)
    return jnp.concatenate([rows[k : k + 1] for k in range(rows.shape[0])], axis=1)


def whole_kernel(
    tokens_hbm,
    vit_qkv_hbm,
    vit_out_hbm,
    tile_gain_ref,
    fresh_proj_hbm,
    target_ref,
    cached_hbm,
    slide_tiles_ref,
    head_shift_ref,
    long_gain_ref,
    long_qkv_hbm,
    long_out_hbm,
    out_ref,
    tokens,
    vit_qkv,
    csum,
    projected,
    attended,
    token_mean,
    vit_out,
    fresh_proj,
    cached,
    long_qkv,
    long_out,
    part,
    part_in,
    fresh_in,
    fresh_all,
    hidden,
    named_out,
    named_in,
    named_mid,
    named_all,
    same,
    lands,
    keep,
    far_marks,
    packed,
    qkv,
    perm,
    qx,
    kx,
    vx,
    keys_by_row,
    send2,
    send3,
    send4,
    got2,
    got3,
    got4,
    num,
    top,
    mix_out,
    mix_in,
    token_sem,
    load_sem,
    sems,
):
    d = lax.axis_index("dp")
    t = lax.axis_index("tensor")
    chunk = d // 2
    half = d % 2
    mine = half * 8 + t

    def remote(i, src, dst, device):
        return pltpu.make_async_remote_copy(
            src_ref=src,
            dst_ref=dst,
            send_sem=sems.at[0, i],
            recv_sem=sems.at[1, i],
            device_id=device,
            device_id_type=MESH,
        )

    half_lanes = pl.ds(pl.multiple_of(t % 2 * (LD // 2), LD // 2), LD // 2)

    def tile_rows(index):
        return pl.ds(pl.multiple_of(index * 16, 16), 16)

    def chunk_device(index):
        return 2 * chunk + index // 8, index % 8

    def named_copy(k):
        peer = (d + k) % 16
        return remote(
            0, named_out.at[tile_rows(peer)], named_in.at[tile_rows(d)], (peer, t)
        )

    def middle_copy(k):
        slot = named_mid.at[tile_rows(t)]
        return remote(1, slot, slot, (d, (t + k) % 8))

    def last_copy(k):
        slot = named_all.at[tile_rows(d)]
        return remote(2, slot, slot, ((d + k) % 16, t))

    def head_copy(k):
        lanes = pl.ds(pl.multiple_of(mine * ROWS, ROWS), ROWS)
        head = (mine + k) % 16
        return remote(3, packed.at[head], qkv.at[:, lanes], chunk_device(head))

    def far_copy(k):
        quad, inner = chunk // 4, chunk % 4
        if k == 0:
            return remote(9, send2, got2, (2 * (chunk + 1 - 2 * (chunk % 2)) + half, t))
        if k < 3:
            other = quad * 4 + (1 - inner // 2) * 2 + (inner % 2 + k - 1) % 2
            return remote(9 + k, send3, got3.at[k - 1], (2 * other + half, t))
        other = (1 - quad) * 4 + (inner + k - 3) % 4
        return remote(9 + k, send4, got4.at[k - 3], (2 * other + half, t))

    def reduce_copy(k):
        peer = (t + k) % 8
        return remote(4, part.at[peer], part_in.at[t], (d, peer))

    def gather_copy(k):
        return remote(5, fresh_in.at[t], fresh_in.at[t], (d, (t + k) % 8))

    def spread_copy(k):
        slot = fresh_all.at[tile_rows(d), half_lanes]
        return remote(6, slot, slot, ((d + k) % 16, t))

    def sibling_copy(k):
        slot = fresh_all.at[:, half_lanes]
        return remote(7, slot, slot, (d, t + 1 - 2 * (t % 2)))

    def mix_copy(k):
        device = (mine + k) % 16
        return remote(8, mix_out.at[device], mix_in.at[mine], chunk_device(device))

    whole = {
        named_copy: (0, named_out.at[0:240]),
        middle_copy: (1, named_mid.at[0:112]),
        last_copy: (2, named_all.at[0:240]),
        head_copy: (3, packed.at[0:15]),
        reduce_copy: (4, part.at[0:7]),
        gather_copy: (5, fresh_in.at[0:7]),
        spread_copy: (6, fresh_all.at[0:240, half_lanes]),
        sibling_copy: (7, fresh_all.at[:, half_lanes]),
        mix_copy: (8, mix_out.at[0:15]),
    }

    def every(copy, count, what):
        if what != "start" and copy in whole:
            i, total = whole[copy]
            getattr(remote(i, total, total, (d, (t + 1) % 8)), what)()
            return
        first = 0 if copy is far_copy else 1
        for k in range(first, first + count):
            getattr(copy(k), what)()

    barrier = pltpu.get_barrier_semaphore()
    for k in range(1, 8):
        pl.semaphore_signal(barrier, 1, device_id=(d, (t + k) % 8), device_id_type=MESH)
        pl.semaphore_signal(
            barrier, 1, device_id=(2 * chunk + 1 - half, (t + k) % 8), device_id_type=MESH
        )
    for k in range(1, 16):
        pl.semaphore_signal(barrier, 1, device_id=((d + k) % 16, t), device_id_type=MESH)

    vit_load = pltpu.make_async_copy(vit_qkv_hbm, vit_qkv.at[0:VW], load_sem.at[5])
    vit_load.start()
    loads = [
        pltpu.make_async_copy(src, dst, load_sem.at[i])
        for i, (src, dst) in enumerate(
            [
                (vit_out_hbm, vit_out),
                (fresh_proj_hbm, fresh_proj),
                (cached_hbm, cached),
                (long_qkv_hbm, long_qkv),
                (long_out_hbm, long_out),
            ]
        )
    ]
    loads[2].start()
    def token_load(i):
        return pltpu.make_async_copy(tokens_hbm.at[i], tokens.at[i], token_sem.at[i])

    for i in range(AHEAD):
        token_load(i).start()

    row = iota((16, D), 0)
    col = iota((16, D), 1)
    extra = jnp.where(row == 0, 1.0, jnp.where((row == 1) & (col == 0), 1.0, 0.0))
    vit_qkv[VW : VW + 16, :] = extra.astype(BF16)
    shift = head_shift_ref[mine] & 15
    end0 = slide_tiles_ref[0]
    end1 = end0 + slide_tiles_ref[1]
    end2 = end1 + slide_tiles_ref[2]

    def picked_rows(count, bits, which):
        lane = iota((1, count), 1)
        spot = lane & ((1 << bits) - 1)
        rank = spot >> 6
        turned = ((rank & 1) << 3) | ((rank & 2) << 1) | ((rank & 4) >> 1) | ((rank & 8) >> 3)
        inside = ((spot & 63) << 4) + ((turned + shift) & 15)
        return SEG * (2 * which + (lane >> bits)) + inside

    quad = chunk // 4
    inner = chunk % 4
    beside = chunk + 1 - 2 * (chunk % 2)
    across = [quad * 4 + (1 - inner // 2) * 2 + (inner % 2 + k) % 2 for k in range(2)]
    beyond = [(1 - quad) * 4 + (inner + 4 - k) % 4 for k in range(4)]
    every_row = jnp.concatenate(
        [picked_rows(CHUNK, 10, chunk), picked_rows(512, 8, beside)]
        + [picked_rows(256, 7, which) for which in across]
        + [picked_rows(128, 6, which) for which in beyond],
        axis=1,
    )
    perm[...] = jnp.where(
        iota((SEG, SEG), 0) == picked_rows(SEG, 10, 0), 1.0, 0.0
    ).astype(BF16)
    ids = (
        (every_row >= end0).astype(jnp.int32)
        + (every_row >= end1).astype(jnp.int32)
        + (every_row >= end2).astype(jnp.int32)
    )
    feature = iota((16, CHUNK + FAR), 0)
    own = ids[:, 0:CHUNK]
    qx[LS:KX, :] = jnp.where(own == feature[:, 0:CHUNK], 1.0, 0.0).astype(BF16)
    marks = jnp.where((feature < 4) & (ids != feature), OUTSIDE, 0.0).astype(BF16)
    kx[LS:KX, :] = marks[:, 0:CHUNK]
    far_marks[...] = marks[:, CHUNK:]

    def value_marks(count):
        return jnp.where(iota((16, count), 0) == 0, 1.0, 0.0).astype(BF16)

    vx[LS:KX, :] = value_marks(CHUNK)

    lane_target = target_ref[...]
    diagonal = iota((256, 256), 0) == iota((256, 256), 1)
    target = jnp.sum(
        jnp.where(diagonal, lane_target.astype(F32), 0.0), axis=1, keepdims=True
    ).astype(jnp.int32)
    equal = target == lane_target
    same[...] = jnp.where(equal, 1.0, 0.0).astype(BF16)
    earlier = jnp.where(equal & (iota((256, 256), 1) < iota((256, 256), 0)), 1.0, 0.0)
    leads = jnp.sum(earlier, axis=1, keepdims=True) < 0.5
    lands[...] = jnp.where(jnp.where(leads, target, -1) == every_row, 1.0, 0.0).astype(BF16)
    keep[...] = 1.0 - dot(jnp.ones((16, 256), BF16), lands[:, 0:CHUNK])[0:8]

    loads[2].wait()
    first_row = (d * 8 + t) * ROWS
    stored = cached[...]
    hidden[...] = (normalize_rows(stored.astype(F32)) * whole_row(long_gain_ref)).astype(BF16)
    mine_only = jnp.where(target - first_row == iota((256, ROWS), 1), 1.0, 0.0).astype(BF16)
    named_out[...] = dot(mine_only, stored).astype(BF16)
    pl.semaphore_wait(barrier, 29)
    every(named_copy, 15, "start")
    named_in[tile_rows(d)] = named_out[tile_rows(d)]

    def sum_over_dp():
        every(named_copy, 15, "wait_recv")
        total = sum(named_in[16 * k : 16 * k + 16].astype(F32) for k in range(16))
        named_mid[tile_rows(t)] = total.astype(BF16)
        every(middle_copy, 7, "start")

    def sum_over_tensor():
        every(middle_copy, 7, "wait_recv")
        total = sum(named_mid[16 * k : 16 * k + 16].astype(F32) for k in range(8))
        named_all[tile_rows(d)] = total.astype(BF16)
        every(last_copy, 15, "start")

    def send_heads():
        loads[3].wait()
        packed[...] = dot(long_qkv[...], hidden[...], NT).astype(BF16).reshape(LH, LW, ROWS)
        every(head_copy, 15, "start")
        qkv[:, pl.ds(pl.multiple_of(mine * ROWS, ROWS), ROWS)] = packed[mine]

    def sort_rows():
        every(head_copy, 15, "wait_recv")
        low_half = iota((LW, 128), 1) < 64
        stacked = jnp.concatenate([qkv[:, 0:SEG], qkv[:, SEG:CHUNK]], axis=0)
        stacked = dot(stacked, perm[...])
        sides = []
        for side in range(2):
            lanes = slice(side * SEG, (side + 1) * SEG)
            ordered = stacked[side * LW : (side + 1) * LW] * keep[0:1, lanes]
            sides.append(ordered[:, 0:128])
            ordered = ordered.astype(BF16)
            qx[0:LS, lanes] = ordered[0:LS]
            kx[0:LS, lanes] = ordered[LS : 2 * LS]
            vx[0:LS, lanes] = ordered[2 * LS : LW]
            send2[:, side * 256 : (side + 1) * 256] = ordered[LS:LW, 0:256]
            send3[:, side * 128 : (side + 1) * 128] = ordered[LS:LW, 0:128]
        both = jnp.where(low_half, sides[0], pltpu.roll(sides[1], 64, 1)).astype(BF16)
        send4[...] = both[LS:LW]
        every(far_copy, 7, "start")

    vit_load.wait()
    csum[...] = dot(vit_qkv[0:VW], jnp.ones((D, 128), BF16))

    def project(group):
        for i in range(GROUP):
            token_load(group * GROUP + i).wait()
        for i in range(GROUP):
            after = group * GROUP + i + AHEAD

            @pl.when(after < TILES_HERE)
            def _():
                token_load(after).start()

        @pl.when(group == 0)
        def _():
            loads[3].start()

        x = tokens[pl.ds(group * GROUP, GROUP)].reshape(WIDE, D)
        raw = dot(vit_qkv[...], x, NT)
        mean = raw[VW : VW + 1] * (1.0 / D)
        shift_row = mean - raw[VW + 1 : VW + 2]
        first = x[:, 0:1].astype(F32)
        squares = jnp.zeros((WIDE, 128), F32)
        for k in range(D // 128):
            delta = x[:, 128 * k : 128 * (k + 1)].astype(F32) - first
            squares = squares + delta * delta
        ones = jnp.ones((16, 128), BF16)
        total = sum(dot(ones, piece, NT) for piece in split3(squares))
        variance = jnp.maximum(total[0:1] * (1.0 / D) - shift_row * shift_row, 0.0)
        scale = lax.rsqrt(variance + EPSILON)
        spread = jnp.concatenate([csum[...]] * (WIDE // 128), axis=1)
        projected[...] = ((raw[0:VW] - spread * mean) * scale).astype(BF16)

    def attention(group):
        def piece(job, which):
            i, head = job
            first = (head * 3 + which) * VS
            return projected[first : first + VS, i * TOK : (i + 1) * TOK]

        jobs = [(i, head) for i in range(GROUP) for head in range(VH_HERE)]
        scores = [dot(piece(job, 1), piece(job, 0), TN) for job in jobs]
        highest = [jnp.max(score, axis=0, keepdims=True) for score in scores]
        weights = [
            jnp.exp2((score - high) * VIT_SCALE) for score, high in zip(scores, highest)
        ]
        sums = [jnp.sum(weight, axis=0, keepdims=True) for weight in weights]
        mixed = [dot(piece(job, 2), weight.astype(BF16)) for job, weight in zip(jobs, weights)]
        for (i, head), mixture, total in zip(jobs, mixed, sums):
            place = pl.ds(pl.multiple_of((group * GROUP + i) * TOK, TOK), TOK)
            attended[head * VS : (head + 1) * VS, place] = (mixture / total).astype(BF16)

    groups = TILES_HERE // GROUP

    def one_group(group, carry):
        project(group)
        attention(group)

        @pl.when(group == 0)
        def _():
            send_heads()
            sum_over_dp()

        @pl.when(group == 1)
        def _():
            sort_rows()
            sum_over_tensor()

        @pl.when(group == 2)
        def _():
            for i in (0, 1, 4):
                loads[i].start()

        return carry

    lax.fori_loop(0, groups, one_group, 0)
    tile_of = iota((TILES_HERE, TILES_HERE * TOK), 1) // TOK
    picks = jnp.where(iota(tile_of.shape, 0) == tile_of, 1.0 / TOK, 0.0).astype(BF16)
    pooled_term = dot(picks, attended[...], NT)

    loads[0].wait()
    partial = dot(jnp.concatenate(split3(pooled_term), axis=0), vit_out[...])
    partial = partial[0:16] + partial[16:32] + partial[32:48]
    for k in range(8):
        part[k] = partial[2 * k : 2 * k + 2]
    every(reduce_copy, 7, "start")
    part_in[pl.ds(t, 1)] = part[pl.ds(t, 1)]
    for i in range(2):
        sums = dot(jnp.ones((16, TOK), BF16), tokens[2 * t + i])
        token_mean[i : i + 1, :] = sums[0:1] * (1.0 / TOK)

    every(reduce_copy, 7, "wait_recv")
    pooled = token_mean[0:2, :]
    for k in range(8):
        pooled = pooled + part_in[k]
    normed = (normalize_rows(pooled) * whole_row(tile_gain_ref)).astype(BF16)
    loads[1].wait()
    fresh = dot(normed, fresh_proj[...])
    fresh_in[pl.ds(t, 1)] = fresh[None]
    every(gather_copy, 7, "start")
    every(gather_copy, 7, "wait_recv")
    group = jnp.concatenate([fresh_in[k] for k in range(8)], axis=0).astype(BF16)
    fresh_all[tile_rows(d), half_lanes] = jnp.where(
        t % 2 == 0, group[:, 0 : LD // 2], group[:, LD // 2 : LD]
    )
    every(spread_copy, 15, "start")
    every(last_copy, 15, "wait_recv")
    every(far_copy, 7, "wait_recv")
    every(spread_copy, 15, "wait_recv")
    every(sibling_copy, 1, "start")
    every(sibling_copy, 1, "wait_recv")

    changed = named_all[...].astype(F32) + dot(same[...], fresh_all[...])
    changed = (normalize_rows(changed) * whole_row(long_gain_ref)).astype(BF16)
    weight = long_qkv[pl.ds(pl.multiple_of(mine * LW, LW), LW), :]
    renewed = dot(weight, changed, NT).astype(BF16)

    def add(ref, rows, lanes, change):
        ref[rows, lanes] = (ref[rows, lanes].astype(F32) + change).astype(BF16)

    change = dot(renewed, lands[:, 0:CHUNK])
    everything = slice(0, CHUNK)
    add(qx, slice(0, LS), everything, change[0:LS])
    add(kx, slice(0, LS), everything, change[LS : 2 * LS])
    add(vx, slice(0, LS), everything, change[2 * LS : LW])
    far_change = dot(renewed[LS:LW], lands[:, CHUNK : CHUNK + FAR])
    for side in range(2):
        lanes = slice(side * SEG, (side + 1) * SEG)
        keys_by_row[lanes, :] = jnp.transpose(kx[:, lanes])

    def attend(jobs):
        scores = [dot(keys, queries) for keys, _, queries in jobs]
        highest = [jnp.max(score, axis=0, keepdims=True) for score in scores]
        weights = [
            jnp.exp2((score - high) * LONG_SCALE).astype(BF16)
            for score, high in zip(scores, highest)
        ]
        results = [dot(values, weight) for (_, values, _), weight in zip(jobs, weights)]
        return list(zip(results, highest))

    def merge(lanes, other_num, other_top):
        old_top = top[0:1, lanes]
        new_top = jnp.maximum(old_top, other_top)
        num[:, lanes] = num[:, lanes] * jnp.exp2(
            (old_top - new_top) * LONG_SCALE
        ) + other_num * jnp.exp2((other_top - new_top) * LONG_SCALE)
        top[0:1, lanes] = new_top

    def first_pair(i, carry):
        jobs = []
        spots = []
        for side in range(2):
            lanes = slice(side * SEG, (side + 1) * SEG)
            spot = pl.ds(pl.multiple_of(side * SEG + i * 512, 512), 512)
            jobs.append((keys_by_row[lanes, :], vx[:, lanes], qx[:, spot]))
            spots.append(spot)
        for spot, (result, highest) in zip(spots, attend(jobs)):
            num[:, spot] = result
            top[0:1, spot] = highest
        return carry

    lax.fori_loop(0, 2, first_pair, 0)

    def joined(ref, width):
        return jnp.concatenate([ref[:, 0:width], ref[:, SEG : SEG + width]], axis=1)

    def joined_rows(width):
        return [keys_by_row[0:width, :], keys_by_row[SEG : SEG + width, :]]

    keys = jnp.concatenate(joined_rows(512), axis=0)
    values = joined(vx, 512)
    jobs = [(keys, values, qx[:, side * SEG : side * SEG + 512]) for side in range(2)]

    def arrived(block, begin, count):
        place = slice(begin, begin + count)
        block = (block.astype(F32) + far_change[:, place]).astype(BF16)
        key = jnp.concatenate([block[0:LS], far_marks[:, place]], axis=0)
        value = jnp.concatenate([block[LS : 2 * LS], value_marks(count)], axis=0)
        return jnp.transpose(key), value

    key2, value2 = arrived(got2[...], 0, 512)
    keys = jnp.concatenate(joined_rows(256) + [key2], axis=0)
    values = jnp.concatenate([joined(vx, 256), value2], axis=1)
    jobs.append((keys, values, joined(qx, 256)))

    keys3 = joined_rows(128) + [key2[0:128], key2[256:384]]
    values3 = [joined(vx, 128), value2[:, 0:128], value2[:, 256:384]]
    for k in range(2):
        key, value = arrived(got3[k], 512 + 256 * k, 256)
        keys3 += [key[0:128], key[128:256]]
        values3.append(value)
    keys = jnp.concatenate(keys3, axis=0)
    values = jnp.concatenate(values3, axis=1)
    jobs.append((keys, values, joined(qx, 128)))

    lower = iota((KX, 128), 1) < 64

    def packed_pair(a, b):
        moved = pltpu.roll(b.astype(F32), 64, 1)
        return jnp.where(lower, a.astype(F32), moved).astype(BF16)

    keys4 = [key[0:64] for key in keys3]
    own = values3[0]
    values4 = [
        packed_pair(own[:, 0:128], own[:, 128:256]),
        packed_pair(values3[1], values3[2]),
    ]
    for far in values3[3:]:
        values4.append(packed_pair(far[:, 0:128], far[:, 128:256]))
    for k in range(4):
        key, value = arrived(got4[k], 1024 + 128 * k, 128)
        keys4.append(key)
        values4.append(value)
    keys = jnp.concatenate(keys4, axis=0)
    values = jnp.concatenate(values4, axis=1)
    query = packed_pair(qx[:, 0:128], qx[:, SEG : SEG + 128])
    jobs.append((keys, values, query))
    done = attend(jobs)
    for side in range(2):
        merge(slice(side * SEG, side * SEG + 512), *done[side])
    for (result, highest), width in ((done[2], 256), (done[3], 128)):
        for side in range(2):
            lanes = slice(side * width, (side + 1) * width)
            merge(
                slice(side * SEG, side * SEG + width), result[:, lanes], highest[:, lanes]
            )
    result, highest = done[4]
    highest = jnp.broadcast_to(highest, (8, 128))
    for side in range(2):
        if side == 1:
            result = pltpu.roll(result, 64, 1)
            highest = pltpu.roll(highest, 64, 1)
        lanes = slice(side * SEG, side * SEG + 128)
        merge(
            lanes,
            jnp.where(lower, result, 0.0),
            jnp.where(lower[0:1], highest[0:1], OUTSIDE),
        )

    blended = []
    for side in range(2):
        lanes = slice(side * SEG, (side + 1) * SEG)
        blended.append((num[0:LS, lanes] * (1.0 / num[LS : LS + 1, lanes])).astype(BF16))
    natural = dot(jnp.concatenate(blended, axis=0), perm[...], NT).astype(BF16)
    for side in range(2):
        for i in range(8):
            mix_out[side * 8 + i] = natural[
                side * LS : (side + 1) * LS, i * ROWS : (i + 1) * ROWS
            ]
    every(mix_copy, 15, "start")
    mix_in[pl.ds(mine, 1)] = mix_out[pl.ds(mine, 1)]
    match = (lane_target - first_row == iota((ROWS, 256), 0))
    match = jnp.where(match, 1.0, 0.0).astype(BF16)
    rows = cached[...].astype(F32) + dot(match, fresh_all[...])
    loads[4].wait()
    every(mix_copy, 15, "wait_recv")
    mixture = mix_in[...].reshape(LD, ROWS)
    out_ref[...] = (rows + dot(mixture, long_out[...], TN)).astype(BF16)

    for copy, count in (
        (named_copy, 15),
        (middle_copy, 7),
        (last_copy, 15),
        (head_copy, 15),
        (far_copy, 7),
        (reduce_copy, 7),
        (gather_copy, 7),
        (spread_copy, 15),
        (sibling_copy, 1),
        (mix_copy, 15),
    ):
        every(copy, count, "wait_send")


def whole_layer(*arguments):
    vmem = pl.BlockSpec(memory_space=pltpu.VMEM)
    smem = pl.BlockSpec(memory_space=pltpu.SMEM)
    hbm = pl.BlockSpec(memory_space=pl.ANY)
    return pl.pallas_call(
        whole_kernel,
        out_shape=jax.ShapeDtypeStruct((ROWS, LD), BF16),
        in_specs=[hbm, hbm, hbm, vmem, hbm, vmem, hbm, smem, smem, vmem, hbm, hbm],
        out_specs=vmem,
        scratch_shapes=[
            pltpu.VMEM((TILES_HERE, TOK, D), BF16),
            pltpu.VMEM((VW + 16, D), BF16),
            pltpu.VMEM((VW, 128), F32),
            pltpu.VMEM((VW, WIDE), BF16),
            pltpu.VMEM((VH_HERE * VS, TILES_HERE * TOK), BF16),
            pltpu.VMEM((8, D), F32),
            pltpu.VMEM((VH_HERE * VS, D), BF16),
            pltpu.VMEM((D, LD), BF16),
            pltpu.VMEM((ROWS, LD), BF16),
            pltpu.VMEM((LH * LW, LD), BF16),
            pltpu.VMEM((LD, LD), BF16),
            pltpu.VMEM((8, 2, D), F32),
            pltpu.VMEM((8, 2, D), F32),
            pltpu.VMEM((8, 2, LD), F32),
            pltpu.VMEM((256, LD), BF16),
            pltpu.VMEM((ROWS, LD), BF16),
            pltpu.VMEM((256, LD), BF16),
            pltpu.VMEM((256, LD), BF16),
            pltpu.VMEM((128, LD), BF16),
            pltpu.VMEM((256, LD), BF16),
            pltpu.VMEM((256, 256), BF16),
            pltpu.VMEM((256, CHUNK + FAR), BF16),
            pltpu.VMEM((8, CHUNK), F32),
            pltpu.VMEM((16, FAR), BF16),
            pltpu.VMEM((16, LW, ROWS), BF16),
            pltpu.VMEM((LW, CHUNK), BF16),
            pltpu.VMEM((SEG, SEG), BF16),
            pltpu.VMEM((KX, CHUNK), BF16),
            pltpu.VMEM((KX, CHUNK), BF16),
            pltpu.VMEM((KX, CHUNK), BF16),
            pltpu.VMEM((CHUNK, KX), BF16),
            pltpu.VMEM((2 * LS, 512), BF16),
            pltpu.VMEM((2 * LS, 256), BF16),
            pltpu.VMEM((2 * LS, 128), BF16),
            pltpu.VMEM((2 * LS, 512), BF16),
            pltpu.VMEM((2, 2 * LS, 256), BF16),
            pltpu.VMEM((4, 2 * LS, 128), BF16),
            pltpu.VMEM((KX, CHUNK), F32),
            pltpu.VMEM((8, CHUNK), F32),
            pltpu.VMEM((16, LS, ROWS), BF16),
            pltpu.VMEM((16, LS, ROWS), BF16),
            pltpu.SemaphoreType.DMA((TILES_HERE,)),
            pltpu.SemaphoreType.DMA((6,)),
            pltpu.SemaphoreType.DMA((2, 16)),
        ],
        compiler_params=pltpu.CompilerParams(
            collective_id=0,
            has_side_effects=True,
            vmem_limit_bytes=60 * 1024 * 1024,
        ),
    )(*arguments)


def body(
    tile_tokens,
    vit_qkv,
    vit_out,
    tile_norm_gain,
    fresh_proj,
    tile_target,
    cached_rows,
    slide_tiles,
    head_shift,
    long_gain,
    long_qkv,
    long_out,
):
    vit_rows = jnp.transpose(vit_qkv, (1, 2, 3, 0)).reshape(VW, D)
    long_rows = jnp.transpose(long_qkv, (1, 2, 3, 0)).reshape(LH * LW, LD)
    return whole_layer(
        tile_tokens,
        vit_rows,
        vit_out,
        tile_norm_gain.reshape(D // 128, 128),
        fresh_proj,
        tile_target.reshape(1, 256),
        cached_rows,
        slide_tiles,
        head_shift,
        long_gain.reshape(LD // 128, 128),
        long_rows,
        long_out,
    )


def solution(mesh):
    placed = (
        P("dp", None, None),
        P(None, "tensor", None, None),
        P("tensor", None),
        P(),
        P(),
        P(),
        P(("dp", "tensor"), None),
        P(),
        P(),
        P(),
        P(),
        P(),
    )
    return jax.shard_map(
        body, mesh=mesh, in_specs=placed, out_specs=P(("dp", "tensor"), None), check_vma=False
    )
```

```python
import functools
import math

import jax
import jax.numpy as jnp
from jax import lax
from jax.experimental import pallas as pl
from jax.experimental.pallas import tpu as pltpu
from jax.sharding import PartitionSpec as P

MESH = pl.DeviceIdType.MESH
EPSILON = 1e-06
OUTSIDE = -1e30
LOG2E = 1.4426950408889634
NN = (((1,), (0,)), ((), ()))
NT = (((1,), (1,)), ((), ()))
TN = (((0,), (0,)), ((), ()))
F32 = jnp.float32
BF16 = jnp.bfloat16

TILES_HERE = 16
TOK = 256
D = 1536
VH_HERE = 3
VS = 64
VW = VH_HERE * 3 * VS
LD = 768
LH = 16
LS = 48
LW = 3 * LS
ROWS = 128
SEG = 1024
CHUNK = 2048
KX = 64
FAR = 1536
GROUP = 4
WIDE = GROUP * TOK
AHEAD = 4
VIT_SCALE = LOG2E / math.sqrt(VS)
LONG_SCALE = LOG2E / math.sqrt(LS)


def dot(a, b, dims=NN):
    return lax.dot_general(a, b, dims, preferred_element_type=F32)


def iota(shape, dim):
    return lax.broadcasted_iota(jnp.int32, shape, dim)


def split3(value):
    high = value.astype(BF16)
    rest = value - high.astype(F32)
    middle = rest.astype(BF16)
    low = (rest - middle.astype(F32)).astype(BF16)
    return high, middle, low


def normalize_rows(values):
    center = values - jnp.mean(values, axis=-1, keepdims=True)
    return center * lax.rsqrt(jnp.mean(center * center, axis=-1, keepdims=True) + EPSILON)


def whole_row(ref):
    rows = ref[...].astype(F32)
    return jnp.concatenate([rows[k : k + 1] for k in range(rows.shape[0])], axis=1)


def whole_kernel(
    tokens_hbm,
    vit_qkv_hbm,
    vit_out_hbm,
    tile_gain_ref,
    fresh_proj_hbm,
    target_ref,
    cached_hbm,
    slide_tiles_ref,
    head_shift_ref,
    long_gain_ref,
    long_qkv_hbm,
    long_out_hbm,
    out_ref,
    tokens,
    vit_qkv,
    csum,
    projected,
    attended,
    token_mean,
    vit_out,
    fresh_proj,
    cached,
    long_qkv,
    long_out,
    part,
    part_in,
    fresh_in,
    fresh_all,
    hidden,
    named_out,
    named_in,
    named_mid,
    named_all,
    same,
    lands,
    keep,
    far_marks,
    packed,
    qkv,
    perm,
    qx,
    kx,
    vx,
    keys_by_row,
    send2,
    send3,
    send4,
    got2,
    got3,
    got4,
    num,
    top,
    mix_out,
    mix_in,
    token_sem,
    load_sem,
    sems,
):
    d = lax.axis_index("dp")
    t = lax.axis_index("tensor")
    chunk = d // 2
    half = d % 2
    mine = half * 8 + t

    def remote(i, src, dst, device):
        return pltpu.make_async_remote_copy(
            src_ref=src,
            dst_ref=dst,
            send_sem=sems.at[0, i],
            recv_sem=sems.at[1, i],
            device_id=device,
            device_id_type=MESH,
        )

    half_lanes = pl.ds(pl.multiple_of(t % 2 * (LD // 2), LD // 2), LD // 2)

    def tile_rows(index):
        return pl.ds(pl.multiple_of(index * 16, 16), 16)

    def chunk_device(index):
        return 2 * chunk + index // 8, index % 8

    def named_copy(k):
        peer = (d + k) % 16
        return remote(
            0, named_out.at[tile_rows(peer)], named_in.at[tile_rows(d)], (peer, t)
        )

    def middle_copy(k):
        slot = named_mid.at[tile_rows(t)]
        return remote(1, slot, slot, (d, (t + k) % 8))

    def last_copy(k):
        slot = named_all.at[tile_rows(d)]
        return remote(2, slot, slot, ((d + k) % 16, t))

    def head_copy(k):
        lanes = pl.ds(pl.multiple_of(mine * ROWS, ROWS), ROWS)
        head = (mine + k) % 16
        return remote(3, packed.at[head], qkv.at[:, lanes], chunk_device(head))

    def far_copy(k):
        quad, inner = chunk // 4, chunk % 4
        if k == 0:
            return remote(9, send2, got2, (2 * (chunk + 1 - 2 * (chunk % 2)) + half, t))
        if k < 3:
            other = quad * 4 + (1 - inner // 2) * 2 + (inner % 2 + k - 1) % 2
            return remote(9 + k, send3, got3.at[k - 1], (2 * other + half, t))
        other = (1 - quad) * 4 + (inner + k - 3) % 4
        return remote(9 + k, send4, got4.at[k - 3], (2 * other + half, t))

    def reduce_copy(k):
        peer = (t + k) % 8
        return remote(4, part.at[peer], part_in.at[t], (d, peer))

    def gather_copy(k):
        return remote(5, fresh_in.at[t], fresh_in.at[t], (d, (t + k) % 8))

    def spread_copy(k):
        slot = fresh_all.at[tile_rows(d), half_lanes]
        return remote(6, slot, slot, ((d + k) % 16, t))

    def sibling_copy(k):
        slot = fresh_all.at[:, half_lanes]
        return remote(7, slot, slot, (d, t + 1 - 2 * (t % 2)))

    def mix_copy(k):
        device = (mine + k) % 16
        return remote(8, mix_out.at[device], mix_in.at[mine], chunk_device(device))

    whole = {
        named_copy: (0, named_out.at[0:240]),
        middle_copy: (1, named_mid.at[0:112]),
        last_copy: (2, named_all.at[0:240]),
        head_copy: (3, packed.at[0:15]),
        reduce_copy: (4, part.at[0:7]),
        gather_copy: (5, fresh_in.at[0:7]),
        spread_copy: (6, fresh_all.at[0:240, half_lanes]),
        sibling_copy: (7, fresh_all.at[:, half_lanes]),
        mix_copy: (8, mix_out.at[0:15]),
    }

    def every(copy, count, what):
        if what != "start" and copy in whole:
            i, total = whole[copy]
            getattr(remote(i, total, total, (d, (t + 1) % 8)), what)()
            return
        first = 0 if copy is far_copy else 1
        for k in range(first, first + count):
            getattr(copy(k), what)()

    barrier = pltpu.get_barrier_semaphore()
    for k in range(1, 8):
        pl.semaphore_signal(barrier, 1, device_id=(d, (t + k) % 8), device_id_type=MESH)
        pl.semaphore_signal(
            barrier, 1, device_id=(2 * chunk + 1 - half, (t + k) % 8), device_id_type=MESH
        )
    for k in range(1, 16):
        pl.semaphore_signal(barrier, 1, device_id=((d + k) % 16, t), device_id_type=MESH)

    vit_load = pltpu.make_async_copy(vit_qkv_hbm, vit_qkv.at[0:VW], load_sem.at[5])
    vit_load.start()
    loads = [
        pltpu.make_async_copy(src, dst, load_sem.at[i])
        for i, (src, dst) in enumerate(
            [
                (vit_out_hbm, vit_out),
                (fresh_proj_hbm, fresh_proj),
                (cached_hbm, cached),
                (long_qkv_hbm, long_qkv),
                (long_out_hbm, long_out),
            ]
        )
    ]
    loads[2].start()
    def token_load(i):
        return pltpu.make_async_copy(tokens_hbm.at[i], tokens.at[i], token_sem.at[i])

    for i in range(AHEAD):
        token_load(i).start()

    row = iota((16, D), 0)
    col = iota((16, D), 1)
    extra = jnp.where(row == 0, 1.0, jnp.where((row == 1) & (col == 0), 1.0, 0.0))
    vit_qkv[VW : VW + 16, :] = extra.astype(BF16)
    shift = head_shift_ref[mine] & 15
    end0 = slide_tiles_ref[0]
    end1 = end0 + slide_tiles_ref[1]
    end2 = end1 + slide_tiles_ref[2]

    def picked_rows(count, bits, which):
        lane = iota((1, count), 1)
        spot = lane & ((1 << bits) - 1)
        rank = spot >> 6
        turned = ((rank & 1) << 3) | ((rank & 2) << 1) | ((rank & 4) >> 1) | ((rank & 8) >> 3)
        inside = ((spot & 63) << 4) + ((turned + shift) & 15)
        return SEG * (2 * which + (lane >> bits)) + inside

    quad = chunk // 4
    inner = chunk % 4
    beside = chunk + 1 - 2 * (chunk % 2)
    across = [quad * 4 + (1 - inner // 2) * 2 + (inner % 2 + k) % 2 for k in range(2)]
    beyond = [(1 - quad) * 4 + (inner + 4 - k) % 4 for k in range(4)]
    every_row = jnp.concatenate(
        [picked_rows(CHUNK, 10, chunk), picked_rows(512, 8, beside)]
        + [picked_rows(256, 7, which) for which in across]
        + [picked_rows(128, 6, which) for which in beyond],
        axis=1,
    )
    perm[...] = jnp.where(
        iota((SEG, SEG), 0) == picked_rows(SEG, 10, 0), 1.0, 0.0
    ).astype(BF16)
    ids = (
        (every_row >= end0).astype(jnp.int32)
        + (every_row >= end1).astype(jnp.int32)
        + (every_row >= end2).astype(jnp.int32)
    )
    feature = iota((16, CHUNK + FAR), 0)
    own = ids[:, 0:CHUNK]
    qx[LS:KX, :] = jnp.where(own == feature[:, 0:CHUNK], 1.0, 0.0).astype(BF16)
    marks = jnp.where((feature < 4) & (ids != feature), OUTSIDE, 0.0).astype(BF16)
    kx[LS:KX, :] = marks[:, 0:CHUNK]
    far_marks[...] = marks[:, CHUNK:]

    def value_marks(count):
        return jnp.where(iota((16, count), 0) == 0, 1.0, 0.0).astype(BF16)

    vx[LS:KX, :] = value_marks(CHUNK)

    lane_target = target_ref[...]
    diagonal = iota((256, 256), 0) == iota((256, 256), 1)
    target = jnp.sum(
        jnp.where(diagonal, lane_target.astype(F32), 0.0), axis=1, keepdims=True
    ).astype(jnp.int32)
    equal = target == lane_target
    same[...] = jnp.where(equal, 1.0, 0.0).astype(BF16)
    earlier = jnp.where(equal & (iota((256, 256), 1) < iota((256, 256), 0)), 1.0, 0.0)
    leads = jnp.sum(earlier, axis=1, keepdims=True) < 0.5
    lands[...] = jnp.where(jnp.where(leads, target, -1) == every_row, 1.0, 0.0).astype(BF16)
    keep[...] = 1.0 - dot(jnp.ones((16, 256), BF16), lands[:, 0:CHUNK])[0:8]

    loads[2].wait()
    first_row = (d * 8 + t) * ROWS
    stored = cached[...]
    hidden[...] = (normalize_rows(stored.astype(F32)) * whole_row(long_gain_ref)).astype(BF16)
    mine_only = jnp.where(target - first_row == iota((256, ROWS), 1), 1.0, 0.0).astype(BF16)
    named_out[...] = dot(mine_only, stored).astype(BF16)
    def greet():
        pl.semaphore_wait(barrier, 29)
        every(named_copy, 15, "start")
        named_in[tile_rows(d)] = named_out[tile_rows(d)]

    def sum_over_dp():
        every(named_copy, 15, "wait_recv")
        total = sum(named_in[16 * k : 16 * k + 16].astype(F32) for k in range(16))
        named_mid[tile_rows(t)] = total.astype(BF16)
        every(middle_copy, 7, "start")

    def sum_over_tensor():
        every(middle_copy, 7, "wait_recv")
        total = sum(named_mid[16 * k : 16 * k + 16].astype(F32) for k in range(8))
        named_all[tile_rows(d)] = total.astype(BF16)
        every(last_copy, 15, "start")

    def send_heads():
        loads[3].wait()
        packed[...] = dot(long_qkv[...], hidden[...], NT).astype(BF16).reshape(LH, LW, ROWS)
        every(head_copy, 15, "start")
        qkv[:, pl.ds(pl.multiple_of(mine * ROWS, ROWS), ROWS)] = packed[mine]

    def sort_rows():
        every(head_copy, 15, "wait_recv")
        low_half = iota((LW, 128), 1) < 64
        stacked = jnp.concatenate([qkv[:, 0:SEG], qkv[:, SEG:CHUNK]], axis=0)
        stacked = dot(stacked, perm[...])
        sides = []
        for side in range(2):
            lanes = slice(side * SEG, (side + 1) * SEG)
            ordered = stacked[side * LW : (side + 1) * LW] * keep[0:1, lanes]
            sides.append(ordered[:, 0:128])
            ordered = ordered.astype(BF16)
            qx[0:LS, lanes] = ordered[0:LS]
            kx[0:LS, lanes] = ordered[LS : 2 * LS]
            vx[0:LS, lanes] = ordered[2 * LS : LW]
            send2[:, side * 256 : (side + 1) * 256] = ordered[LS:LW, 0:256]
            send3[:, side * 128 : (side + 1) * 128] = ordered[LS:LW, 0:128]
        both = jnp.where(low_half, sides[0], pltpu.roll(sides[1], 64, 1)).astype(BF16)
        send4[...] = both[LS:LW]
        every(far_copy, 7, "start")

    vit_load.wait()
    csum[...] = dot(vit_qkv[0:VW], jnp.ones((D, 128), BF16))

    def project(group):
        for i in range(GROUP):
            token_load(group * GROUP + i).wait()
        for i in range(GROUP):
            after = group * GROUP + i + AHEAD

            @pl.when(after < TILES_HERE)
            def _():
                token_load(after).start()

        @pl.when(group == 0)
        def _():
            loads[3].start()

        x = tokens[pl.ds(group * GROUP, GROUP)].reshape(WIDE, D)
        raw = dot(vit_qkv[...], x, NT)
        mean = raw[VW : VW + 1] * (1.0 / D)
        shift_row = mean - raw[VW + 1 : VW + 2]
        first = x[:, 0:1].astype(F32)
        squares = jnp.zeros((WIDE, 128), F32)
        for k in range(D // 128):
            delta = x[:, 128 * k : 128 * (k + 1)].astype(F32) - first
            squares = squares + delta * delta
        ones = jnp.ones((16, 128), BF16)
        total = sum(dot(ones, piece, NT) for piece in split3(squares))
        variance = jnp.maximum(total[0:1] * (1.0 / D) - shift_row * shift_row, 0.0)
        scale = lax.rsqrt(variance + EPSILON)
        spread = jnp.concatenate([csum[...]] * (WIDE // 128), axis=1)
        projected[...] = ((raw[0:VW] - spread * mean) * scale).astype(BF16)

    def attention(group):
        def piece(job, which):
            i, head = job
            first = (head * 3 + which) * VS
            return projected[first : first + VS, i * TOK : (i + 1) * TOK]

        jobs = [(i, head) for i in range(GROUP) for head in range(VH_HERE)]
        scores = [dot(piece(job, 1), piece(job, 0), TN) for job in jobs]
        highest = [jnp.max(score, axis=0, keepdims=True) for score in scores]
        weights = [
            jnp.exp2((score - high) * VIT_SCALE) for score, high in zip(scores, highest)
        ]
        sums = [jnp.sum(weight, axis=0, keepdims=True) for weight in weights]
        mixed = [dot(piece(job, 2), weight.astype(BF16)) for job, weight in zip(jobs, weights)]
        for (i, head), mixture, total in zip(jobs, mixed, sums):
            place = pl.ds(pl.multiple_of((group * GROUP + i) * TOK, TOK), TOK)
            attended[head * VS : (head + 1) * VS, place] = (mixture / total).astype(BF16)

    groups = TILES_HERE // GROUP

    def one_group(group, carry):
        project(group)
        attention(group)

        @pl.when(group == 0)
        def _():
            greet()
            send_heads()

        @pl.when(group == 1)
        def _():
            sum_over_dp()
            for i in (0, 1, 4):
                loads[i].start()

        @pl.when(group == 2)
        def _():
            sum_over_tensor()
            sort_rows()

        return carry

    lax.fori_loop(0, groups, one_group, 0)
    tile_of = iota((TILES_HERE, TILES_HERE * TOK), 1) // TOK
    picks = jnp.where(iota(tile_of.shape, 0) == tile_of, 1.0 / TOK, 0.0).astype(BF16)
    pooled_term = dot(picks, attended[...], NT)

    loads[0].wait()
    partial = dot(jnp.concatenate(split3(pooled_term), axis=0), vit_out[...])
    partial = partial[0:16] + partial[16:32] + partial[32:48]
    for k in range(8):
        part[k] = partial[2 * k : 2 * k + 2]
    every(reduce_copy, 7, "start")
    part_in[pl.ds(t, 1)] = part[pl.ds(t, 1)]
    for i in range(2):
        sums = dot(jnp.ones((16, TOK), BF16), tokens[2 * t + i])
        token_mean[i : i + 1, :] = sums[0:1] * (1.0 / TOK)

    every(reduce_copy, 7, "wait_recv")
    pooled = token_mean[0:2, :]
    for k in range(8):
        pooled = pooled + part_in[k]
    normed = (normalize_rows(pooled) * whole_row(tile_gain_ref)).astype(BF16)
    loads[1].wait()
    fresh = dot(normed, fresh_proj[...])
    fresh_in[pl.ds(t, 1)] = fresh[None]
    every(gather_copy, 7, "start")
    every(gather_copy, 7, "wait_recv")
    group = jnp.concatenate([fresh_in[k] for k in range(8)], axis=0).astype(BF16)
    fresh_all[tile_rows(d), half_lanes] = jnp.where(
        t % 2 == 0, group[:, 0 : LD // 2], group[:, LD // 2 : LD]
    )
    every(spread_copy, 15, "start")
    every(last_copy, 15, "wait_recv")
    every(far_copy, 7, "wait_recv")
    every(spread_copy, 15, "wait_recv")
    every(sibling_copy, 1, "start")
    every(sibling_copy, 1, "wait_recv")

    changed = named_all[...].astype(F32) + dot(same[...], fresh_all[...])
    changed = (normalize_rows(changed) * whole_row(long_gain_ref)).astype(BF16)
    weight = long_qkv[pl.ds(pl.multiple_of(mine * LW, LW), LW), :]
    renewed = dot(weight, changed, NT).astype(BF16)

    def add(ref, rows, lanes, change):
        ref[rows, lanes] = (ref[rows, lanes].astype(F32) + change).astype(BF16)

    change = dot(renewed, lands[:, 0:CHUNK])
    everything = slice(0, CHUNK)
    add(qx, slice(0, LS), everything, change[0:LS])
    add(kx, slice(0, LS), everything, change[LS : 2 * LS])
    add(vx, slice(0, LS), everything, change[2 * LS : LW])
    far_change = dot(renewed[LS:LW], lands[:, CHUNK : CHUNK + FAR])
    for side in range(2):
        lanes = slice(side * SEG, (side + 1) * SEG)
        keys_by_row[lanes, :] = jnp.transpose(kx[:, lanes])

    def attend(jobs):
        scores = [dot(keys, queries) for keys, _, queries in jobs]
        highest = [jnp.max(score, axis=0, keepdims=True) for score in scores]
        weights = [
            jnp.exp2((score - high) * LONG_SCALE).astype(BF16)
            for score, high in zip(scores, highest)
        ]
        results = [dot(values, weight) for (_, values, _), weight in zip(jobs, weights)]
        return list(zip(results, highest))

    def merge(lanes, other_num, other_top):
        old_top = top[0:1, lanes]
        new_top = jnp.maximum(old_top, other_top)
        num[:, lanes] = num[:, lanes] * jnp.exp2(
            (old_top - new_top) * LONG_SCALE
        ) + other_num * jnp.exp2((other_top - new_top) * LONG_SCALE)
        top[0:1, lanes] = new_top

    def first_pair(i, carry):
        jobs = []
        spots = []
        for side in range(2):
            lanes = slice(side * SEG, (side + 1) * SEG)
            spot = pl.ds(pl.multiple_of(side * SEG + i * 512, 512), 512)
            jobs.append((keys_by_row[lanes, :], vx[:, lanes], qx[:, spot]))
            spots.append(spot)
        for spot, (result, highest) in zip(spots, attend(jobs)):
            num[:, spot] = result
            top[0:1, spot] = highest
        return carry

    lax.fori_loop(0, 2, first_pair, 0)

    def joined(ref, width):
        return jnp.concatenate([ref[:, 0:width], ref[:, SEG : SEG + width]], axis=1)

    def joined_rows(width):
        return [keys_by_row[0:width, :], keys_by_row[SEG : SEG + width, :]]

    keys = jnp.concatenate(joined_rows(512), axis=0)
    values = joined(vx, 512)
    jobs = [(keys, values, qx[:, side * SEG : side * SEG + 512]) for side in range(2)]

    def arrived(block, begin, count):
        place = slice(begin, begin + count)
        block = (block.astype(F32) + far_change[:, place]).astype(BF16)
        key = jnp.concatenate([block[0:LS], far_marks[:, place]], axis=0)
        value = jnp.concatenate([block[LS : 2 * LS], value_marks(count)], axis=0)
        return jnp.transpose(key), value

    key2, value2 = arrived(got2[...], 0, 512)
    keys = jnp.concatenate(joined_rows(256) + [key2], axis=0)
    values = jnp.concatenate([joined(vx, 256), value2], axis=1)
    jobs.append((keys, values, joined(qx, 256)))

    keys3 = joined_rows(128) + [key2[0:128], key2[256:384]]
    values3 = [joined(vx, 128), value2[:, 0:128], value2[:, 256:384]]
    for k in range(2):
        key, value = arrived(got3[k], 512 + 256 * k, 256)
        keys3 += [key[0:128], key[128:256]]
        values3.append(value)
    keys = jnp.concatenate(keys3, axis=0)
    values = jnp.concatenate(values3, axis=1)
    jobs.append((keys, values, joined(qx, 128)))

    lower = iota((KX, 128), 1) < 64

    def packed_pair(a, b):
        moved = pltpu.roll(b.astype(F32), 64, 1)
        return jnp.where(lower, a.astype(F32), moved).astype(BF16)

    keys4 = [key[0:64] for key in keys3]
    own = values3[0]
    values4 = [
        packed_pair(own[:, 0:128], own[:, 128:256]),
        packed_pair(values3[1], values3[2]),
    ]
    for far in values3[3:]:
        values4.append(packed_pair(far[:, 0:128], far[:, 128:256]))
    for k in range(4):
        key, value = arrived(got4[k], 1024 + 128 * k, 128)
        keys4.append(key)
        values4.append(value)
    keys = jnp.concatenate(keys4, axis=0)
    values = jnp.concatenate(values4, axis=1)
    query = packed_pair(qx[:, 0:128], qx[:, SEG : SEG + 128])
    jobs.append((keys, values, query))
    done = attend(jobs)
    for side in range(2):
        merge(slice(side * SEG, side * SEG + 512), *done[side])
    for (result, highest), width in ((done[2], 256), (done[3], 128)):
        for side in range(2):
            lanes = slice(side * width, (side + 1) * width)
            merge(
                slice(side * SEG, side * SEG + width), result[:, lanes], highest[:, lanes]
            )
    result, highest = done[4]
    highest = jnp.broadcast_to(highest, (8, 128))
    for side in range(2):
        if side == 1:
            result = pltpu.roll(result, 64, 1)
            highest = pltpu.roll(highest, 64, 1)
        lanes = slice(side * SEG, side * SEG + 128)
        merge(
            lanes,
            jnp.where(lower, result, 0.0),
            jnp.where(lower[0:1], highest[0:1], OUTSIDE),
        )

    blended = []
    for side in range(2):
        lanes = slice(side * SEG, (side + 1) * SEG)
        blended.append((num[0:LS, lanes] * (1.0 / num[LS : LS + 1, lanes])).astype(BF16))
    natural = dot(jnp.concatenate(blended, axis=0), perm[...], NT).astype(BF16)
    for side in range(2):
        for i in range(8):
            mix_out[side * 8 + i] = natural[
                side * LS : (side + 1) * LS, i * ROWS : (i + 1) * ROWS
            ]
    every(mix_copy, 15, "start")
    mix_in[pl.ds(mine, 1)] = mix_out[pl.ds(mine, 1)]
    match = (lane_target - first_row == iota((ROWS, 256), 0))
    match = jnp.where(match, 1.0, 0.0).astype(BF16)
    rows = cached[...].astype(F32) + dot(match, fresh_all[...])
    loads[4].wait()
    every(mix_copy, 15, "wait_recv")
    mixture = mix_in[...].reshape(LD, ROWS)
    out_ref[...] = (rows + dot(mixture, long_out[...], TN)).astype(BF16)

    for copy, count in (
        (named_copy, 15),
        (middle_copy, 7),
        (last_copy, 15),
        (head_copy, 15),
        (far_copy, 7),
        (reduce_copy, 7),
        (gather_copy, 7),
        (spread_copy, 15),
        (sibling_copy, 1),
        (mix_copy, 15),
    ):
        every(copy, count, "wait_send")


def whole_layer(*arguments):
    vmem = pl.BlockSpec(memory_space=pltpu.VMEM)
    smem = pl.BlockSpec(memory_space=pltpu.SMEM)
    hbm = pl.BlockSpec(memory_space=pl.ANY)
    return pl.pallas_call(
        whole_kernel,
        out_shape=jax.ShapeDtypeStruct((ROWS, LD), BF16),
        in_specs=[hbm, hbm, hbm, vmem, hbm, vmem, hbm, smem, smem, vmem, hbm, hbm],
        out_specs=vmem,
        scratch_shapes=[
            pltpu.VMEM((TILES_HERE, TOK, D), BF16),
            pltpu.VMEM((VW + 16, D), BF16),
            pltpu.VMEM((VW, 128), F32),
            pltpu.VMEM((VW, WIDE), BF16),
            pltpu.VMEM((VH_HERE * VS, TILES_HERE * TOK), BF16),
            pltpu.VMEM((8, D), F32),
            pltpu.VMEM((VH_HERE * VS, D), BF16),
            pltpu.VMEM((D, LD), BF16),
            pltpu.VMEM((ROWS, LD), BF16),
            pltpu.VMEM((LH * LW, LD), BF16),
            pltpu.VMEM((LD, LD), BF16),
            pltpu.VMEM((8, 2, D), F32),
            pltpu.VMEM((8, 2, D), F32),
            pltpu.VMEM((8, 2, LD), F32),
            pltpu.VMEM((256, LD), BF16),
            pltpu.VMEM((ROWS, LD), BF16),
            pltpu.VMEM((256, LD), BF16),
            pltpu.VMEM((256, LD), BF16),
            pltpu.VMEM((128, LD), BF16),
            pltpu.VMEM((256, LD), BF16),
            pltpu.VMEM((256, 256), BF16),
            pltpu.VMEM((256, CHUNK + FAR), BF16),
            pltpu.VMEM((8, CHUNK), F32),
            pltpu.VMEM((16, FAR), BF16),
            pltpu.VMEM((16, LW, ROWS), BF16),
            pltpu.VMEM((LW, CHUNK), BF16),
            pltpu.VMEM((SEG, SEG), BF16),
            pltpu.VMEM((KX, CHUNK), BF16),
            pltpu.VMEM((KX, CHUNK), BF16),
            pltpu.VMEM((KX, CHUNK), BF16),
            pltpu.VMEM((CHUNK, KX), BF16),
            pltpu.VMEM((2 * LS, 512), BF16),
            pltpu.VMEM((2 * LS, 256), BF16),
            pltpu.VMEM((2 * LS, 128), BF16),
            pltpu.VMEM((2 * LS, 512), BF16),
            pltpu.VMEM((2, 2 * LS, 256), BF16),
            pltpu.VMEM((4, 2 * LS, 128), BF16),
            pltpu.VMEM((KX, CHUNK), F32),
            pltpu.VMEM((8, CHUNK), F32),
            pltpu.VMEM((16, LS, ROWS), BF16),
            pltpu.VMEM((16, LS, ROWS), BF16),
            pltpu.SemaphoreType.DMA((TILES_HERE,)),
            pltpu.SemaphoreType.DMA((6,)),
            pltpu.SemaphoreType.DMA((2, 16)),
        ],
        compiler_params=pltpu.CompilerParams(
            collective_id=0,
            has_side_effects=True,
            vmem_limit_bytes=60 * 1024 * 1024,
        ),
    )(*arguments)


def body(
    tile_tokens,
    vit_qkv,
    vit_out,
    tile_norm_gain,
    fresh_proj,
    tile_target,
    cached_rows,
    slide_tiles,
    head_shift,
    long_gain,
    long_qkv,
    long_out,
):
    vit_rows = jnp.transpose(vit_qkv, (1, 2, 3, 0)).reshape(VW, D)
    long_rows = jnp.transpose(long_qkv, (1, 2, 3, 0)).reshape(LH * LW, LD)
    return whole_layer(
        tile_tokens,
        vit_rows,
        vit_out,
        tile_norm_gain.reshape(D // 128, 128),
        fresh_proj,
        tile_target.reshape(1, 256),
        cached_rows,
        slide_tiles,
        head_shift,
        long_gain.reshape(LD // 128, 128),
        long_rows,
        long_out,
    )


def solution(mesh):
    placed = (
        P("dp", None, None),
        P(None, "tensor", None, None),
        P("tensor", None),
        P(),
        P(),
        P(),
        P(("dp", "tensor"), None),
        P(),
        P(),
        P(),
        P(),
        P(),
    )
    return jax.shard_map(
        body, mesh=mesh, in_specs=placed, out_specs=P(("dp", "tensor"), None), check_vma=False
    )
```
